256 devices in a mesh: grp: 8 (over z), gz: 32 (over x, y, core).
Axes of the slice: x: 4, y: 4, z: 8, core: 2. Of those that a mesh axis runs over, the one named last changes fastest.
Arguments:
- spectrum: float32 [2, 3, 256, 256, 256], P(None, None, ('grp', 'gz')), may hold values from -16 to 16
- marker_fraction: float32 [8192, 3, 256], P(('grp', 'gz')), may hold values from 0 to 1
- marker_offsets: int32 [8192, 3, 256], P(('grp', 'gz')), may hold values from 0 to 8, as said below
- block_source: int32 [8192, 1], P(('grp', 'gz')), may hold values from 0 to 31; in each aligned block of 32 rows (0 to 31, 32 to 63, ...) at most 2 rows name the same one
- block_tile: int32 [8192, 2], P(('grp', 'gz')), may hold values from 0 to 31
Outputs:
- marker_velocity: float32 [8192, 3, 256], P(('grp', 'gz'))
The draws below stay inside these ranges and needn't reach their ends.
Inputs may be any that keep to these rules, and one draw needn't show every extreme that they name: marker_offsets[b, 0, m] is 0 or 1; the other two entries run from 0 to 8. `block_source`: the rows of one device name one index at most 2 times.
All inputs are finite; a program needn't handle non-finite values.
Results may differ from the reference program's by a relative error of at most 0.0003.
Values sent between devices are 32-bit elements; how exact they have to be, the bound alone decides.
A program may use at most 320 MiB of HBM per device.

```python
import math
import jax
import jax.numpy as jnp
import numpy as np
from jax import lax

NXY = 256
MARK = 256
BLK_DEV = 32
NZ = 256
BLOCKS = 8192
CAP = 2
N_GZ = 32


def draw_marker_offsets(key, part):
    key_z = jax.random.fold_in(key, 11)
    key_xy = jax.random.fold_in(key, 12)
    z_start = jax.random.randint(key_z, (BLOCKS, 1, MARK), 0, 2, dtype=jnp.int32)
    xy_start = jax.random.randint(key_xy, (BLOCKS, 2, MARK), 0, 9, dtype=jnp.int32)
    return jnp.concatenate([z_start, xy_start], axis=1)


def plant(entries, key, least, largest):
    longest = entries.shape.index(max(entries.shape))
    spots = []
    for shift in (0, 1):
        where = [jax.random.randint(jax.random.fold_in(key, axis), (), 0, length) for axis, length in enumerate(entries.shape)]
        where[longest] = (where[longest] + shift) % entries.shape[longest]
        spots.append(tuple(where))
    return entries.at[spots[0]].set(least).at[spots[1]].set(largest)


def shard_levels(key, extent, shards, least, high):
    loudness = 1.0
    for dim, parts in shards:
        steps = jax.random.uniform(jax.random.fold_in(jax.random.fold_in(key, 6), dim), (parts,), jnp.float32, least / len(shards), high / len(shards))
        loudness = loudness * jnp.repeat(jnp.exp(steps), extent[dim] // parts).reshape((-1,) + (1,) * (len(extent) - 1 - dim))
    return loudness


def routed_block(key, own, number, rows, count, top, most, slope):
    order = jax.random.permutation(key, count)
    packed, usual = shares(count, rows * top, most, slope, True), shares(count, rows * top, most, slope, False)
    places = jnp.arange(count)

    def named(sizes, turn):
        used = int((sizes > 0).sum())
        fixed = max(1, used // 4)
        shifted = fixed + (places - fixed + turn * (used - fixed)) % max(1, count - fixed)
        return jnp.zeros((count,), jnp.int32).at[order[jnp.where(places < fixed, places, shifted)]].set(jnp.asarray(sizes, jnp.int32))

    sizes = jnp.where(number % 4 == 0, named(packed, number // 4), named(usual, number - number // 4 - 1))
    mixed = jax.random.permutation(jax.random.fold_in(own, 3), count)
    giver, sink = mixed[0:count // 2 * 2:2], mixed[1:count // 2 * 2:2]
    slack = jnp.minimum(sizes[giver] - 1, most - sizes[sink]) // 2
    slack = jnp.where((giver == order[0]) | (sink == order[0]) | (sizes[sink] == 0), 0, jnp.maximum(slack, 0))
    shifted = jax.random.randint(jax.random.fold_in(own, 4), (count // 2,), 0, 1 << 20) % (slack + 1)
    sizes = sizes.at[giver].add(-shifted).at[sink].add(shifted)
    labels = jnp.searchsorted(jnp.cumsum(sizes), jnp.arange(rows * top), side="right").astype(jnp.int32)
    grid = labels.reshape(top, rows).T
    grid = grid[jax.random.permutation(jax.random.fold_in(own, 1), rows)]
    turn = jax.random.randint(jax.random.fold_in(own, 2), (rows, 1), 0, top)
    return jnp.take_along_axis(grid, (jnp.arange(top)[None, :] + turn) % top, axis=1)


def shares(number_of, total, bound, skew, full):
    portions = [(1 << 20) // math.isqrt(standing ** skew) + 1 for standing in range(1, number_of + 1)]
    largest = bound if full else min(bound, max(-(-total // number_of), total * portions[0] // sum(portions)))
    least = 1 if total - largest >= number_of - 1 else 0
    holding, spare = [largest] + [least] * (number_of - 1), total - largest - least * (number_of - 1)
    while spare > 0:
        candidates = [i for i in range(1, number_of) if holding[i] < largest] or [i for i in range(1, number_of) if holding[i] < bound]
        whole, left = sum([portions[i] for i in candidates]), spare
        for i in candidates:
            extra = min(bound - holding[i], max(1, left * portions[i] // whole), spare)
            holding[i] = holding[i] + extra
            spare = spare - extra
    return np.array(holding)


def scatter_about(rng, extent, width, limit, pieces=(), held_as=jnp.bfloat16):
    values = width * jax.random.normal(rng, extent, jnp.float32)
    if pieces:
        values = values * shard_levels(rng, extent, pieces, -0.22, 0.18)
    return jnp.clip(values, -limit, limit).astype(held_as)


def setup_inputs(seed: int = 0) -> dict:
    keys = jax.random.split(jax.random.key(seed), 6)
    spectrum = scatter_about(keys[0], (2, 3, NZ, NXY, NXY), 3.0, 16.0, ((2, 256),), jnp.float32)
    marker_fraction = jnp.clip(1.0 * jax.random.uniform(keys[1], (BLOCKS, 3, MARK), jnp.float32) ** shard_levels(keys[1], (BLOCKS, 3, MARK), ((0, 256),), -0.2, 0.2), 0.0, 1.0)
    marker_offsets = draw_marker_offsets(jax.random.fold_in(keys[5], 71), 0)
    block_source_keys = jax.random.split(jax.random.fold_in(keys[3], 1), BLOCKS // BLK_DEV)
    block_source_turns = jax.random.permutation(jax.random.fold_in(keys[3], 3), BLOCKS // BLK_DEV)
    block_source = jax.vmap(lambda own, number: routed_block(jax.random.fold_in(keys[3], 2), own, number, BLK_DEV, N_GZ, 1, CAP, 2))(block_source_keys, block_source_turns).reshape((BLOCKS, 1))
    block_tile = plant(jax.random.randint(keys[4], (BLOCKS, 2), 0, NXY // 8), jax.random.fold_in(keys[4], 1), 0, (NXY // 8) - 1).astype(jnp.int32)
    return {"spectrum": spectrum, "marker_fraction": marker_fraction, "marker_offsets": marker_offsets, "block_source": block_source, "block_tile": block_tile}


def bit_reverse(total_count):
    width_bits = total_count.bit_length() - 1
    result = []
    for position in range(total_count):
        reversed_value = 0
        for bit_number in range(width_bits):
            reversed_value = reversed_value + ((position >> bit_number & 1) << width_bits - 1 - bit_number)
        result.append(reversed_value)
    return np.array(result, dtype=np.int32)

def peskin_taps(fraction):
    root_term = jnp.sqrt(1.0 + 4.0 * fraction - 4.0 * fraction * fraction)
    return jnp.stack([(3.0 - 2.0 * fraction - root_term) / 8.0, (3.0 - 2.0 * fraction + root_term) / 8.0, (1.0 + 2.0 * fraction + root_term) / 8.0, (1.0 + 2.0 * fraction - root_term) / 8.0], axis=-2)

def spread_rows(tap_weights, first_cell, row_count):
    row_ids = jnp.arange(row_count, dtype=jnp.int32)[:, None]
    result = jnp.zeros((row_count, tap_weights.shape[-1]), tap_weights.dtype)
    for offset in range(4):
        result = result + jnp.where(row_ids == first_cell[None, :] + offset, tap_weights[offset][None, :], 0.0)
    return result

def sample_tile(tile_cells, weight_z, weight_x, weight_y):
    reduced = jnp.einsum('czxy,ym->czxm', tile_cells, weight_y, precision=lax.Precision.HIGHEST)
    reduced = jnp.einsum('czxm,xm->czm', reduced, weight_x, precision=lax.Precision.HIGHEST)
    return jnp.einsum('czm,zm->cm', reduced, weight_z, precision=lax.Precision.HIGHEST)

def reference(spectrum, marker_fraction, marker_offsets, block_source, block_tile):
    lookup = jnp.asarray(bit_reverse(NZ), dtype=jnp.int32)
    natural = jnp.take(spectrum, lookup, axis=2)
    coeffs = lax.complex(natural[0], natural[1])
    synthesized = jnp.fft.ifftn(coeffs, axes=(1, 2, 3))
    velocity = jnp.real(synthesized) * math.sqrt(NXY * NXY * NZ)
    block_ids = jnp.arange(BLOCKS, dtype=jnp.int32)
    group_ids = block_ids // BLK_DEV // N_GZ
    plane_ids = (group_ids * N_GZ + block_source[:, 0]).astype(jnp.int32)

    def one_block(operands):
        fraction, offsets, plane_id, tile_pair = operands
        z_cells = (plane_id - 2 + jnp.arange(5, dtype=jnp.int32)) % NZ
        x_cells = (8 * tile_pair[0] - 2 + jnp.arange(12, dtype=jnp.int32)) % NXY
        y_cells = (8 * tile_pair[1] - 2 + jnp.arange(12, dtype=jnp.int32)) % NXY
        tile_cells = velocity[:, z_cells[:, None, None], x_cells[None, :, None], y_cells[None, None, :]]
        tap_weights = peskin_taps(fraction)
        weight_z = spread_rows(tap_weights[0], offsets[0], 5)
        weight_x = spread_rows(tap_weights[1], offsets[1], 12)
        weight_y = spread_rows(tap_weights[2], offsets[2], 12)
        return sample_tile(tile_cells, weight_z, weight_x, weight_y)
    return lax.map(one_block, (marker_fraction, marker_offsets, plane_ids, block_tile))
```

```python
import functools
import math

import jax
import jax.numpy as jnp
import ml_dtypes
import numpy as np
from jax import lax
from jax.experimental import pallas as pl
from jax.experimental.pallas import tpu as pltpu
from jax.sharding import PartitionSpec as P

MESH = pl.DeviceIdType.MESH
REACH = 2
PLANES = 2 * REACH + 1
CELLS = 12
LANES = 128
ROWS_OUT = 40


def bit_reversed(count):
    bits = count.bit_length() - 1
    return np.array([int(format(i, f"0{bits}b")[::-1], 2) if bits else 0 for i in range(count)])


def split_table(values):
    high = values.astype(ml_dtypes.bfloat16)
    low = (values - high.astype(np.float64)).astype(ml_dtypes.bfloat16)
    return jnp.asarray(high), jnp.asarray(low)


def split(x):
    high = x.astype(jnp.bfloat16)
    return high, (x - high.astype(jnp.float32)).astype(jnp.bfloat16)


def dot(a, b):
    return jnp.dot(a, b, preferred_element_type=jnp.float32)


def dot3(a, b):
    return dot(a[0], b[0]) + (dot(a[1], b[0]) + dot(a[0], b[1]))


def turn(re, im, angle_num, angle_den):
    eighth = 8 * angle_num % (8 * angle_den) / angle_den
    if eighth == 0:
        return re, im
    if eighth == 2:
        return -im, re
    cosine, sine = math.cos(math.pi * eighth / 4), math.sin(math.pi * eighth / 4)
    if eighth == 1:
        return (re - im) * cosine, (re + im) * cosine
    if eighth == 3:
        return (re + im) * cosine, (re - im) * sine
    return cosine * re - sine * im, sine * re + cosine * im


def butterflies(items, first_half, position_of, real_at_end=False):
    count = len(items)
    half = 1
    while half < count:
        last = real_at_end and 2 * half == count
        for low in range(count):
            if low // half % 2:
                continue
            high = low + half
            span = half * first_half
            re, im = turn(*items[high], position_of(low) % span, 2 * span)
            first = items[low]
            if last:
                items[low], items[high] = (first[0] + re, None), (first[0] - re, None)
            else:
                items[low] = (first[0] + re, first[1] + im)
                items[high] = (first[0] - re, first[1] - im)
        half *= 2
    return items


def wait_for(ref, semaphore):
    pltpu.make_async_copy(ref, ref, semaphore).wait()


def transform_kernel(
    groups,
    slabs,
    spec_ref,
    cos_hi,
    cos_lo,
    sin_hi,
    sin_lo,
    twiddle_ref,
    out_ref,
    plane_t,
    rows_in,
    rows_z,
    ring_in,
    real_z,
    velocity,
    send_a,
    recv_a,
    send_b,
    recv_b,
    send_c,
    recv_c,
):
    g = lax.axis_index("grp")
    s = lax.axis_index("gz")
    side = spec_ref.shape[2]
    rows = side // slabs
    share = slabs // groups
    components = spec_ref.shape[1]

    barrier = pltpu.get_barrier_semaphore()

    def greet_slab(i, carry):
        pl.semaphore_signal(barrier, inc=1, device_id=(g, lax.rem(s + i, slabs)), device_id_type=MESH)
        return carry

    def greet_ring(i, carry):
        pl.semaphore_signal(barrier, inc=1, device_id=(lax.rem(g + i, groups), s), device_id_type=MESH)
        return carry

    lax.fori_loop(1, slabs, greet_slab, 0)
    lax.fori_loop(1, groups, greet_ring, 0)

    def transform_plane(c):
        cosine, sine = (cos_hi[...], cos_lo[...]), (sin_hi[...], sin_lo[...])
        re, im = split(spec_ref[0, c]), split(spec_ref[1, c])
        row_re = split(dot3(re, cosine) - dot3(im, sine))
        row_im = split(dot3(re, sine) + dot3(im, cosine))
        plane_t[c, 0] = dot3(cosine, row_re) - dot3(sine, row_im)
        plane_t[c, 1] = dot3(sine, row_re) + dot3(cosine, row_im)

    def send_rows(c):
        def one(i, carry):
            r = lax.rem(s + i, slabs)
            pltpu.make_async_remote_copy(
                src_ref=plane_t.at[c, :, pl.ds(pl.multiple_of(r * rows, rows), rows), :],
                dst_ref=rows_in.at[c, s],
                send_sem=send_a.at[c],
                recv_sem=recv_a.at[c],
                device_id=(g, r),
                device_id_type=MESH,
            ).start()
            return carry

        pltpu.make_async_copy(
            plane_t.at[c, :, pl.ds(pl.multiple_of(s * rows, rows), rows), :],
            rows_in.at[c, s],
            recv_a.at[c],
        ).start()
        lax.fori_loop(1, slabs, one, 0)

    transform_plane(0)
    pl.semaphore_wait(barrier, slabs - 1 + groups - 1)
    send_rows(0)

    def later_plane(c, carry):
        transform_plane(c)
        send_rows(c)
        return carry

    lax.fori_loop(1, components, later_plane, 0)

    inner = min(8, slabs)
    outer = slabs // inner

    def along_slab(c, carry):
        wait_for(rows_in.at[c], recv_a.at[c])
        for block in range(outer):
            items = {k: (rows_in[c, inner * block + k, 0], rows_in[c, inner * block + k, 1]) for k in range(inner)}
            items = butterflies(items, 1, lambda k: k)
            for k in range(inner):
                rows_in[c, inner * block + k, 0], rows_in[c, inner * block + k, 1] = items[k]
        for k in range(inner):
            items = {m: (rows_in[c, inner * m + k, 0], rows_in[c, inner * m + k, 1]) for m in range(outer)}
            items = butterflies(items, inner, lambda m, k=k: inner * m + k)
            for m in range(outer):
                w = inner * m + k
                cosine, sine = twiddle_ref[g * 2 * slabs + 2 * w], twiddle_ref[g * 2 * slabs + 2 * w + 1]
                re, im = items[m]
                rows_z[c, w, 0] = cosine * re - sine * im
                rows_z[c, w, 1] = sine * re + cosine * im

        def one(i, inner_carry):
            to = lax.rem(g + i, groups)
            pltpu.make_async_remote_copy(
                src_ref=rows_z.at[c, pl.ds(to * share, share)],
                dst_ref=ring_in.at[c, g],
                send_sem=send_b.at[c],
                recv_sem=recv_b.at[c],
                device_id=(to, s),
                device_id_type=MESH,
            ).start()
            return inner_carry

        pltpu.make_async_copy(rows_z.at[c, pl.ds(g * share, share)], ring_in.at[c, g], recv_b.at[c]).start()
        lax.fori_loop(1, groups, one, 0)
        return carry

    lax.fori_loop(0, components, along_slab, 0)

    def along_ring(c, carry):
        wait_for(ring_in.at[c], recv_b.at[c])
        for k in range(share):
            items = {q: (ring_in[c, q, k, 0], ring_in[c, q, k, 1]) for q in range(groups)}
            items = butterflies(items, 1, lambda q: q, real_at_end=True)
            for u in range(groups):
                real_z[c, u, k] = items[u][0]

        def one(i, inner_carry):
            to = lax.rem(g + lax.div(i, share), groups)
            k = lax.rem(i, share)
            w = g * share + k
            mine = jnp.logical_and(to == g, w == s)
            place = velocity.at[c, pl.ds(pl.multiple_of(s * rows, rows), rows), :]

            @pl.when(mine)
            def _():
                pltpu.make_async_copy(real_z.at[c, to, k], place, recv_c.at[c]).start()

            @pl.when(jnp.logical_not(mine))
            def _():
                pltpu.make_async_remote_copy(
                    src_ref=real_z.at[c, to, k],
                    dst_ref=place,
                    send_sem=send_c.at[c],
                    recv_sem=recv_c.at[c],
                    device_id=(to, w),
                    device_id_type=MESH,
                ).start()

            return inner_carry

        lax.fori_loop(0, slabs, one, 0)
        return carry

    lax.fori_loop(0, components, along_ring, 0)

    def finish(c, carry):
        wait_for(velocity.at[c], recv_c.at[c])
        for half in range(side // LANES):
            columns = slice(half * LANES, (half + 1) * LANES)
            out_ref[c, half, REACH : REACH + side, :] = velocity[c, :, columns]
            out_ref[c, half, 0:REACH, :] = velocity[c, side - REACH : side, columns]
            out_ref[c, half, side + REACH : side + 8, :] = velocity[c, 0 : 8 - REACH, columns]
        return carry

    lax.fori_loop(0, components, finish, 0)

    holds_own = lax.div(s, share) == g

    def drain(c, carry):
        wait_for(rows_in.at[c, pl.ds(0, slabs - 1)], send_a.at[c])
        wait_for(ring_in.at[c, pl.ds(0, groups - 1)], send_b.at[c])

        @pl.when(holds_own)
        def _():
            wait_for(velocity.at[c, pl.ds(0, side - rows)], send_c.at[c])

        @pl.when(jnp.logical_not(holds_own))
        def _():
            wait_for(velocity.at[c], send_c.at[c])

        return carry

    lax.fori_loop(0, components, drain, 0)


def synthesize(spectrum, groups, slabs):
    components, side = spectrum.shape[1], spectrum.shape[3]
    rows, share = side // slabs, slabs // groups
    ids = np.arange(side)
    angle = 2.0 * np.pi / side * (ids[:, None] * ids[None, :] % side)
    tables = split_table(np.cos(angle)) + split_table(np.sin(angle))
    count = groups * slabs
    twist = 2.0 * np.pi / count * (bit_reversed(groups)[:, None] * np.arange(slabs)[None, :])
    scale = 1.0 / math.sqrt(side * side * count)
    twiddle = np.stack([np.cos(twist), np.sin(twist)], axis=-1) * scale
    twiddle = jnp.asarray(twiddle.reshape(-1).astype(np.float32))
    vmem = pl.BlockSpec(memory_space=pltpu.VMEM)
    f32 = jnp.float32
    return pl.pallas_call(
        functools.partial(transform_kernel, groups, slabs),
        out_shape=jax.ShapeDtypeStruct((components, side // LANES, side + 8, LANES), f32),
        in_specs=[vmem] * 5 + [pl.BlockSpec(memory_space=pltpu.SMEM)],
        out_specs=vmem,
        scratch_shapes=[
            pltpu.VMEM((components, 2, side, side), f32),
            pltpu.VMEM((components, slabs, 2, rows, side), f32),
            pltpu.VMEM((components, slabs, 2, rows, side), f32),
            pltpu.VMEM((components, groups, share, 2, rows, side), f32),
            pltpu.VMEM((components, groups, share, rows, side), f32),
            pltpu.VMEM((components, side, side), f32),
        ]
        + [pltpu.SemaphoreType.DMA((components,))] * 6,
        compiler_params=pltpu.CompilerParams(
            collective_id=0, has_side_effects=True, vmem_limit_bytes=40 * 2**20
        ),
        cost_estimate=pl.CostEstimate(flops=2_500_000_000, bytes_accessed=100_000_000, transcendentals=0),
    )(spectrum[:, :, 0], *tables, twiddle)


def cut_kernel(plane_ref, request_ref, message_ref):
    slabs = message_ref.shape[0]
    lane = lax.broadcasted_iota(jnp.int32, (16, LANES), 1)
    low_half = lax.broadcasted_iota(jnp.int32, (8, LANES), 0) < 4

    def serve(home, carry):
        cut = [jnp.zeros((16, LANES), jnp.float32) for _ in range(3)]
        for slot in range(2 * PLANES):
            start = pl.multiple_of(request_ref[(slot * slabs + home) * 2], 8)
            first = request_ref[(slot * slabs + home) * 2 + 1]
            half = first >> 7
            first = first & (LANES - 1)
            taken = jnp.logical_and(lane >= CELLS * slot, lane < CELLS * (slot + 1))
            near = lane >= first
            for c in range(3):
                cells = jnp.where(
                    near,
                    plane_ref[c, half, pl.ds(start, 16), :],
                    plane_ref[c, 1 - half, pl.ds(start, 16), :],
                )
                moved = pltpu.roll(cells, (CELLS * slot + LANES - first) & (LANES - 1), 1)
                cut[c] = jnp.where(taken, moved, cut[c])
        for c in range(3):
            message_ref[home, 8 * c : 8 * c + 8, :] = cut[c][0:8]
        message_ref[home, 24:32, :] = jnp.where(low_half, cut[0][8:16], pltpu.roll(cut[1][8:16], 4, 0))
        message_ref[home, 32:40, :] = cut[2][8:16]
        return carry

    lax.fori_loop(0, slabs, serve, 0)


def exchange_kernel(groups, slabs, message, inbox, send_sem, edge_sem, recv_sem):
    g = lax.axis_index("grp")
    s = lax.axis_index("gz")
    below, above = lax.rem(g + groups - 1, groups), lax.rem(g + 1, groups)
    at_start, at_end = s < REACH, s >= slabs - REACH
    at_edge = jnp.logical_or(at_start, at_end)

    barrier = pltpu.get_barrier_semaphore()

    def greet_slab(i, carry):
        pl.semaphore_signal(barrier, inc=1, device_id=(g, lax.rem(s + i, slabs)), device_id_type=MESH)
        return carry

    lax.fori_loop(1, slabs, greet_slab, 0)
    for k in range(REACH):
        pl.semaphore_signal(barrier, inc=1, device_id=(below, slabs - 1 - k), device_id_type=MESH)
        pl.semaphore_signal(barrier, inc=1, device_id=(above, k), device_id_type=MESH)

    @pl.when(at_edge)
    def _():
        pl.semaphore_wait(barrier, 2 * slabs - 1)

    @pl.when(jnp.logical_not(at_edge))
    def _():
        pl.semaphore_wait(barrier, slabs - 1)

    edge_group = jnp.where(at_start, below, above)
    edge_place = jnp.where(at_start, slabs + REACH + s, s - (slabs - REACH))

    def send(i, carry):
        home = lax.rem(s + i, slabs)

        @pl.when(at_edge)
        def _():
            pltpu.make_async_remote_copy(
                src_ref=message.at[home],
                dst_ref=inbox.at[edge_place],
                send_sem=edge_sem,
                recv_sem=recv_sem,
                device_id=(edge_group, home),
                device_id_type=MESH,
            ).start()

        @pl.when(i == 0)
        def _():
            pltpu.make_async_copy(message.at[home], inbox.at[REACH + s], recv_sem).start()

        @pl.when(i > 0)
        def _():
            pltpu.make_async_remote_copy(
                src_ref=message.at[home],
                dst_ref=inbox.at[REACH + s],
                send_sem=send_sem,
                recv_sem=recv_sem,
                device_id=(g, home),
                device_id_type=MESH,
            ).start()

        return carry

    lax.fori_loop(0, slabs, send, 0)
    wait_for(inbox, recv_sem)
    wait_for(inbox.at[pl.ds(0, slabs - 1)], send_sem)

    @pl.when(at_edge)
    def _():
        wait_for(inbox.at[pl.ds(0, slabs)], edge_sem)


def interpolate_kernel(inbox, home_ref, fraction_ref, offset_ref, out_ref, weights):
    blocks, markers = fraction_ref.shape[0], fraction_ref.shape[2]
    weights[...] = jnp.zeros_like(weights)
    row_y = lax.broadcasted_iota(jnp.int32, (16, markers), 0)
    row_x = jnp.where(row_y < 12, row_y, row_y - 4)
    in_low = lax.broadcasted_iota(jnp.int32, (8, markers), 0) < 4

    def interpolate(i, carry):
        f = fraction_ref[i]
        o = offset_ref[i]
        root = jnp.sqrt(1.0 + 4.0 * f - 4.0 * f * f)
        low, high = 3.0 - 2.0 * f, 1.0 + 2.0 * f
        taps = ((low - root) * 0.125, (low + root) * 0.125, (high + root) * 0.125, (high - root) * 0.125)
        weight_x = jnp.zeros((16, markers), jnp.float32)
        weight_y = jnp.zeros((16, markers), jnp.float32)
        for e in range(4):
            weight_x = jnp.where(row_x == o[1:2] + e, taps[e][1:2], weight_x)
            weight_y = jnp.where(row_y == o[2:3] + e, taps[e][2:3], weight_y)
        y_high, y_low = split(weight_y)
        weights[0, 0:16, :] = y_high
        weights[1, 0:16, :] = y_low
        near = o[0:1] == 0
        none = jnp.zeros((1, markers), jnp.float32)
        tap_z = [none] + [tap[0:1] for tap in taps] + [none]
        weight_z = [jnp.where(near, tap_z[j + 1], tap_z[j]) for j in range(PLANES)]
        source = home_ref[i]
        slot = home_ref[blocks + i]
        cells = []
        for j in range(PLANES):
            place = CELLS * (2 * (PLANES - 1 - j) + slot)
            cells.append(pltpu.roll(inbox[source + j], (2 * LANES - place) & (LANES - 1), 1))
        cells_high, cells_low = split(jnp.concatenate(cells, axis=0))
        values = dot(cells_high, weights[0]) + (dot(cells_low, weights[0]) + dot(cells_high, weights[1]))
        sums = []
        for t in range(ROWS_OUT // 8):
            total = weight_z[0] * values[8 * t : 8 * t + 8]
            for j in range(1, PLANES):
                total = total + weight_z[j] * values[ROWS_OUT * j + 8 * t : ROWS_OUT * j + 8 * t + 8]
            sums.append(total)
        x_first, x_last = weight_x[0:8], weight_x[8:16]
        mixed, last = sums[3] * x_last, sums[4] * x_last
        tails = (jnp.where(in_low, mixed, 0.0), jnp.where(in_low, 0.0, mixed), jnp.where(in_low, last, 0.0))
        for c in range(3):
            out_ref[i, c : c + 1, :] = jnp.sum(sums[c] * x_first + tails[c], axis=0, keepdims=True)
        return carry

    lax.fori_loop(0, blocks, interpolate, 0)


def sample(plane, requests, home, fraction, offsets, groups, slabs):
    vmem, smem = pl.BlockSpec(memory_space=pltpu.VMEM), pl.BlockSpec(memory_space=pltpu.SMEM)
    anywhere = pl.BlockSpec(memory_space=pl.ANY)
    markers = fraction.shape[2]
    message = pl.pallas_call(
        cut_kernel,
        out_shape=jax.ShapeDtypeStruct((slabs, ROWS_OUT, LANES), jnp.float32),
        in_specs=[vmem, smem],
        out_specs=vmem,
        cost_estimate=pl.CostEstimate(flops=5_000_000, bytes_accessed=1_500_000, transcendentals=0),
    )(plane, requests)
    inbox = pl.pallas_call(
        functools.partial(exchange_kernel, groups, slabs),
        out_shape=jax.ShapeDtypeStruct((slabs + 2 * REACH, ROWS_OUT, LANES), jnp.float32),
        in_specs=[anywhere],
        out_specs=anywhere,
        scratch_shapes=[pltpu.SemaphoreType.DMA] * 3,
        compiler_params=pltpu.CompilerParams(collective_id=1, has_side_effects=True),
        cost_estimate=pl.CostEstimate(flops=0, bytes_accessed=20_000_000, transcendentals=0),
    )(message)
    return pl.pallas_call(
        interpolate_kernel,
        out_shape=jax.ShapeDtypeStruct(fraction.shape, jnp.float32),
        in_specs=[vmem, smem, vmem, vmem],
        out_specs=vmem,
        scratch_shapes=[pltpu.VMEM((2, LANES, markers), jnp.bfloat16)],
        cost_estimate=pl.CostEstimate(flops=200_000_000, bytes_accessed=1_500_000, transcendentals=25_000),
    )(inbox, home, fraction, offsets)


def patch_requests(block_source, block_tile, groups, slabs, side):
    asked = jnp.concatenate([block_source, block_tile], axis=1)
    everyone = lax.all_gather(asked, ("grp", "gz"), axis=0, tiled=False)
    blocks = block_source.shape[0]
    everyone = everyone.reshape(groups, slabs, blocks, 3)
    position = lax.axis_index("grp") * slabs + lax.axis_index("gz")
    count = groups * slabs
    order = jnp.arange(blocks, dtype=jnp.int32)
    requests = []
    for step in range(-REACH, REACH + 1):
        centre = (position + step + count) % count
        near = lax.dynamic_index_in_dim(everyone, centre // slabs, 0, keepdims=False)
        named = near[:, :, 0] == centre % slabs
        code = (order[None, :] * side + near[:, :, 1]) * side + near[:, :, 2]
        first = jnp.min(jnp.where(named, code, side * side * blocks), axis=1)
        second = jnp.max(jnp.where(named, code, 0), axis=1)
        for chosen in (first, second):
            tile_x, tile_y = chosen // side % side, chosen % side
            requests.append(jnp.stack([8 * tile_x, (8 * tile_y - 2 + side) % side], axis=-1))
    return jnp.stack(requests).reshape(-1)


def local(groups, slabs, spectrum, marker_fraction, marker_offsets, block_source, block_tile):
    side = spectrum.shape[3]
    requests = patch_requests(block_source, block_tile, groups, slabs, side)
    source = block_source[:, 0]
    order = jnp.arange(source.shape[0])
    again = jnp.any((source[:, None] == source[None, :]) & (order[:, None] > order[None, :]), axis=1)
    home = jnp.concatenate([source, again.astype(jnp.int32)])
    plane = synthesize(spectrum, groups, slabs)
    return sample(plane, requests, home, marker_fraction, marker_offsets, groups, slabs)


def solution(mesh):
    groups, slabs = mesh.shape["grp"], mesh.shape["gz"]
    both = ("grp", "gz")
    return jax.shard_map(
        functools.partial(local, groups, slabs),
        mesh=mesh,
        in_specs=(
            P(None, None, both, None, None),
            P(both, None, None),
            P(both, None, None),
            P(both, None),
            P(both, None),
        ),
        out_specs=P(both, None, None),
        check_vma=False,
    )
```

```python
import functools
import math

import jax
import jax.numpy as jnp
import ml_dtypes
import numpy as np
from jax import lax
from jax.experimental import pallas as pl
from jax.experimental.pallas import tpu as pltpu
from jax.sharding import PartitionSpec as P

MESH = pl.DeviceIdType.MESH
REACH = 2
PLANES = 2 * REACH + 1
CELLS = 12
LANES = 128
ROWS_OUT = 40


def bit_reversed(count):
    bits = count.bit_length() - 1
    return np.array([int(format(i, f"0{bits}b")[::-1], 2) if bits else 0 for i in range(count)])


def split_table(values):
    high = values.astype(ml_dtypes.bfloat16)
    low = (values - high.astype(np.float64)).astype(ml_dtypes.bfloat16)
    return jnp.asarray(high), jnp.asarray(low)


def split(x):
    high = x.astype(jnp.bfloat16)
    return high, (x - high.astype(jnp.float32)).astype(jnp.bfloat16)


def dot(a, b):
    return jnp.dot(a, b, preferred_element_type=jnp.float32)


def dot3(a, b):
    return dot(a[0], b[0]) + (dot(a[1], b[0]) + dot(a[0], b[1]))


def turn(re, im, angle_num, angle_den):
    eighth = 8 * angle_num % (8 * angle_den) / angle_den
    if eighth == 0:
        return re, im
    if eighth == 2:
        return -im, re
    cosine, sine = math.cos(math.pi * eighth / 4), math.sin(math.pi * eighth / 4)
    if eighth == 1:
        return (re - im) * cosine, (re + im) * cosine
    if eighth == 3:
        return (re + im) * cosine, (re - im) * sine
    return cosine * re - sine * im, sine * re + cosine * im


def butterflies(items, first_half, position_of, real_at_end=False):
    count = len(items)
    half = 1
    while half < count:
        last = real_at_end and 2 * half == count
        for low in range(count):
            if low // half % 2:
                continue
            high = low + half
            span = half * first_half
            re, im = turn(*items[high], position_of(low) % span, 2 * span)
            first = items[low]
            if last:
                items[low], items[high] = (first[0] + re, None), (first[0] - re, None)
            else:
                items[low] = (first[0] + re, first[1] + im)
                items[high] = (first[0] - re, first[1] - im)
        half *= 2
    return items


def wait_for(ref, semaphore):
    pltpu.make_async_copy(ref, ref, semaphore).wait()


def nearby(me, i, count):
    return lax.rem(me + (2 * lax.rem(i, 2) - 1) * lax.div(i + 1, 2) + count, count)


def transform_kernel(
    groups,
    slabs,
    asking_ref,
    spec_ref,
    cos_hi,
    cos_lo,
    sin_hi,
    sin_lo,
    twiddle_ref,
    out_ref,
    asked_ref,
    plane_t,
    rows_in,
    rows_z,
    ring_in,
    real_z,
    velocity,
    send_a,
    recv_a,
    send_b,
    recv_b,
    send_c,
    recv_c,
    send_q,
    recv_q,
):
    g = lax.axis_index("grp")
    s = lax.axis_index("gz")
    side = spec_ref.shape[2]
    rows = side // slabs
    share = slabs // groups
    components = spec_ref.shape[1]

    below, above = lax.rem(g + groups - 1, groups), lax.rem(g + 1, groups)
    at_start, at_end = s < REACH, s >= slabs - REACH
    at_edge = jnp.logical_or(at_start, at_end)
    edge_group = jnp.where(at_start, below, above)

    barrier = pltpu.get_barrier_semaphore()

    def greet_slab(i, carry):
        pl.semaphore_signal(barrier, inc=1, device_id=(g, lax.rem(s + i, slabs)), device_id_type=MESH)
        return carry

    def greet_edge(i, carry):
        pl.semaphore_signal(barrier, inc=1, device_id=(edge_group, lax.rem(s + i, slabs)), device_id_type=MESH)
        return carry

    def greet_ring(i, carry):
        pl.semaphore_signal(barrier, inc=1, device_id=(lax.rem(g + i, groups), s), device_id_type=MESH)
        return carry

    lax.fori_loop(1, slabs, greet_slab, 0)
    lax.fori_loop(1, groups, greet_ring, 0)

    @pl.when(at_edge)
    def _():
        lax.fori_loop(0, slabs, greet_edge, 0)


    def transform_plane(c):
        cosine, sine = (cos_hi[...], cos_lo[...]), (sin_hi[...], sin_lo[...])
        re, im = split(spec_ref[0, c]), split(spec_ref[1, c])
        row_re = split(dot3(re, cosine) - dot3(im, sine))
        row_im = split(dot3(re, sine) + dot3(im, cosine))
        plane_t[c, 0] = dot3(cosine, row_re) - dot3(sine, row_im)
        plane_t[c, 1] = dot3(sine, row_re) + dot3(cosine, row_im)

    def send_rows(c):
        def one(i, carry):
            r = nearby(s, i, slabs)
            pltpu.make_async_remote_copy(
                src_ref=plane_t.at[c, :, pl.ds(pl.multiple_of(r * rows, rows), rows), :],
                dst_ref=rows_in.at[c, s],
                send_sem=send_a.at[c],
                recv_sem=recv_a.at[c],
                device_id=(g, r),
                device_id_type=MESH,
            ).start()
            return carry

        pltpu.make_async_copy(
            plane_t.at[c, :, pl.ds(pl.multiple_of(s * rows, rows), rows), :],
            rows_in.at[c, s],
            recv_a.at[c],
        ).start()
        lax.fori_loop(1, slabs, one, 0)

    def ask(place, device):
        pltpu.make_async_remote_copy(
            src_ref=asking_ref,
            dst_ref=asked_ref.at[place],
            send_sem=send_q,
            recv_sem=recv_q,
            device_id=device,
            device_id_type=MESH,
        ).start()

    def ask_slab(i, carry):
        ask(s, (g, nearby(s, i, slabs)))
        return carry

    transform_plane(0)
    pl.semaphore_wait(barrier, slabs - 1 + groups - 1 + 2 * REACH)
    send_rows(0)
    pltpu.make_async_copy(asking_ref, asked_ref.at[s], recv_q).start()
    lax.fori_loop(1, slabs, ask_slab, 0)
    for k in range(REACH):
        ask(slabs + s, (below, slabs - 1 - k))
        ask(slabs + s, (above, k))

    def later_plane(c, carry):
        transform_plane(c)
        send_rows(c)
        return carry

    lax.fori_loop(1, components, later_plane, 0)

    inner = min(8, slabs)
    outer = slabs // inner

    def along_slab(c, carry):
        wait_for(rows_in.at[c], recv_a.at[c])
        for block in range(outer):
            items = {k: (rows_in[c, inner * block + k, 0], rows_in[c, inner * block + k, 1]) for k in range(inner)}
            items = butterflies(items, 1, lambda k: k)
            for k in range(inner):
                rows_in[c, inner * block + k, 0], rows_in[c, inner * block + k, 1] = items[k]
        for k in range(inner):
            items = {m: (rows_in[c, inner * m + k, 0], rows_in[c, inner * m + k, 1]) for m in range(outer)}
            items = butterflies(items, inner, lambda m, k=k: inner * m + k)
            for m in range(outer):
                w = inner * m + k
                cosine, sine = twiddle_ref[g * 2 * slabs + 2 * w], twiddle_ref[g * 2 * slabs + 2 * w + 1]
                re, im = items[m]
                rows_z[c, w, 0] = cosine * re - sine * im
                rows_z[c, w, 1] = sine * re + cosine * im

        def one(i, inner_carry):
            to = nearby(g, i, groups)
            pltpu.make_async_remote_copy(
                src_ref=rows_z.at[c, pl.ds(to * share, share)],
                dst_ref=ring_in.at[c, g],
                send_sem=send_b.at[c],
                recv_sem=recv_b.at[c],
                device_id=(to, s),
                device_id_type=MESH,
            ).start()
            return inner_carry

        pltpu.make_async_copy(rows_z.at[c, pl.ds(g * share, share)], ring_in.at[c, g], recv_b.at[c]).start()
        lax.fori_loop(1, groups, one, 0)
        return carry

    lax.fori_loop(0, components, along_slab, 0)

    def along_ring(c, carry):
        wait_for(ring_in.at[c], recv_b.at[c])
        for k in range(share):
            items = {q: (ring_in[c, q, k, 0], ring_in[c, q, k, 1]) for q in range(groups)}
            items = butterflies(items, 1, lambda q: q, real_at_end=True)
            for u in range(groups):
                real_z[c, u, k] = items[u][0]

        def one(i, inner_carry):
            to = nearby(g, lax.div(i, share), groups)
            k = lax.rem(i, share)
            w = g * share + k
            mine = jnp.logical_and(to == g, w == s)
            place = velocity.at[c, pl.ds(pl.multiple_of(s * rows, rows), rows), :]

            @pl.when(mine)
            def _():
                pltpu.make_async_copy(real_z.at[c, to, k], place, recv_c.at[c]).start()

            @pl.when(jnp.logical_not(mine))
            def _():
                pltpu.make_async_remote_copy(
                    src_ref=real_z.at[c, to, k],
                    dst_ref=place,
                    send_sem=send_c.at[c],
                    recv_sem=recv_c.at[c],
                    device_id=(to, w),
                    device_id_type=MESH,
                ).start()

            return inner_carry

        lax.fori_loop(0, slabs, one, 0)
        return carry

    lax.fori_loop(0, components, along_ring, 0)

    def finish(c, carry):
        wait_for(velocity.at[c], recv_c.at[c])
        for half in range(side // LANES):
            columns = slice(half * LANES, (half + 1) * LANES)
            out_ref[c, half, REACH : REACH + side, :] = velocity[c, :, columns]
            out_ref[c, half, 0:REACH, :] = velocity[c, side - REACH : side, columns]
            out_ref[c, half, side + REACH : side + 8, :] = velocity[c, 0 : 8 - REACH, columns]
        return carry

    lax.fori_loop(0, components, finish, 0)

    @pl.when(at_edge)
    def _():
        wait_for(asked_ref, recv_q)

    @pl.when(jnp.logical_not(at_edge))
    def _():
        wait_for(asked_ref.at[pl.ds(0, slabs)], recv_q)

    wait_for(asked_ref.at[pl.ds(0, slabs - 1 + 2 * REACH)], send_q)

    holds_own = lax.div(s, share) == g

    def drain(c, carry):
        wait_for(rows_in.at[c, pl.ds(0, slabs - 1)], send_a.at[c])
        wait_for(ring_in.at[c, pl.ds(0, groups - 1)], send_b.at[c])

        @pl.when(holds_own)
        def _():
            wait_for(velocity.at[c, pl.ds(0, side - rows)], send_c.at[c])

        @pl.when(jnp.logical_not(holds_own))
        def _():
            wait_for(velocity.at[c], send_c.at[c])

        return carry

    lax.fori_loop(0, components, drain, 0)


def synthesize(asking, spectrum, groups, slabs):
    components, side = spectrum.shape[1], spectrum.shape[3]
    rows, share = side // slabs, slabs // groups
    ids = np.arange(side)
    angle = 2.0 * np.pi / side * (ids[:, None] * ids[None, :] % side)
    tables = split_table(np.cos(angle)) + split_table(np.sin(angle))
    count = groups * slabs
    twist = 2.0 * np.pi / count * (bit_reversed(groups)[:, None] * np.arange(slabs)[None, :])
    scale = 1.0 / math.sqrt(side * side * count)
    twiddle = np.stack([np.cos(twist), np.sin(twist)], axis=-1) * scale
    twiddle = jnp.asarray(twiddle.reshape(-1).astype(np.float32))
    vmem = pl.BlockSpec(memory_space=pltpu.VMEM)
    f32 = jnp.float32
    return pl.pallas_call(
        functools.partial(transform_kernel, groups, slabs),
        out_shape=(
            jax.ShapeDtypeStruct((components, side // LANES, side + 8, LANES), f32),
            jax.ShapeDtypeStruct((2 * slabs, 1, LANES), jnp.int32),
        ),
        in_specs=[vmem] * 6 + [pl.BlockSpec(memory_space=pltpu.SMEM)],
        out_specs=(vmem, vmem),
        scratch_shapes=[
            pltpu.VMEM((components, 2, side, side), f32),
            pltpu.VMEM((components, slabs, 2, rows, side), f32),
            pltpu.VMEM((components, slabs, 2, rows, side), f32),
            pltpu.VMEM((components, groups, share, 2, rows, side), f32),
            pltpu.VMEM((components, groups, share, rows, side), f32),
            pltpu.VMEM((components, side, side), f32),
        ]
        + [pltpu.SemaphoreType.DMA((components,))] * 6
        + [pltpu.SemaphoreType.DMA] * 2,
        compiler_params=pltpu.CompilerParams(
            collective_id=0, has_side_effects=True, vmem_limit_bytes=40 * 2**20
        ),
        cost_estimate=pl.CostEstimate(flops=2_500_000_000, bytes_accessed=100_000_000, transcendentals=0),
    )(asking, spectrum[:, :, 0], *tables, twiddle)


def cut_kernel(plane_ref, request_ref, message_ref):
    slabs = message_ref.shape[0]
    s = lax.axis_index("gz")
    lane = lax.broadcasted_iota(jnp.int32, (16, LANES), 1)
    low_half = lax.broadcasted_iota(jnp.int32, (8, LANES), 0) < 4

    def serve(home, carry):
        cut = [jnp.zeros((16, LANES), jnp.float32) for _ in range(3)]
        for slot in range(2 * PLANES):
            centre = s + slot // 2 - REACH
            inside = jnp.logical_and(centre >= 0, centre < slabs)
            row = jnp.where(inside, home, home + slabs)
            column = 4 * lax.rem(centre + slabs, slabs) + 2 * (slot % 2)
            start = pl.multiple_of(request_ref[row, 0, column], 8)
            first = request_ref[row, 0, column + 1]
            half = first >> 7
            first = first & (LANES - 1)
            taken = jnp.logical_and(lane >= CELLS * slot, lane < CELLS * (slot + 1))
            near = lane >= first
            for c in range(3):
                cells = jnp.where(
                    near,
                    plane_ref[c, half, pl.ds(start, 16), :],
                    plane_ref[c, 1 - half, pl.ds(start, 16), :],
                )
                moved = pltpu.roll(cells, (CELLS * slot + LANES - first) & (LANES - 1), 1)
                cut[c] = jnp.where(taken, moved, cut[c])
        for c in range(3):
            message_ref[home, 8 * c : 8 * c + 8, :] = cut[c][0:8]
        message_ref[home, 24:32, :] = jnp.where(low_half, cut[0][8:16], pltpu.roll(cut[1][8:16], 4, 0))
        message_ref[home, 32:40, :] = cut[2][8:16]
        return carry

    lax.fori_loop(0, slabs, serve, 0)


def exchange_kernel(groups, slabs, message, inbox, send_sem, edge_sem, recv_sem):
    g = lax.axis_index("grp")
    s = lax.axis_index("gz")
    below, above = lax.rem(g + groups - 1, groups), lax.rem(g + 1, groups)
    at_start, at_end = s < REACH, s >= slabs - REACH
    at_edge = jnp.logical_or(at_start, at_end)

    barrier = pltpu.get_barrier_semaphore()

    def greet_slab(i, carry):
        pl.semaphore_signal(barrier, inc=1, device_id=(g, lax.rem(s + i, slabs)), device_id_type=MESH)
        return carry

    lax.fori_loop(1, slabs, greet_slab, 0)
    for k in range(REACH):
        pl.semaphore_signal(barrier, inc=1, device_id=(below, slabs - 1 - k), device_id_type=MESH)
        pl.semaphore_signal(barrier, inc=1, device_id=(above, k), device_id_type=MESH)

    @pl.when(at_edge)
    def _():
        pl.semaphore_wait(barrier, 2 * slabs - 1)

    @pl.when(jnp.logical_not(at_edge))
    def _():
        pl.semaphore_wait(barrier, slabs - 1)

    edge_group = jnp.where(at_start, below, above)
    edge_place = jnp.where(at_start, slabs + REACH + s, s - (slabs - REACH))

    def send(i, carry):
        home = nearby(s, i, slabs)

        @pl.when(at_edge)
        def _():
            pltpu.make_async_remote_copy(
                src_ref=message.at[home],
                dst_ref=inbox.at[edge_place],
                send_sem=edge_sem,
                recv_sem=recv_sem,
                device_id=(edge_group, home),
                device_id_type=MESH,
            ).start()

        @pl.when(i == 0)
        def _():
            pltpu.make_async_copy(message.at[home], inbox.at[REACH + s], recv_sem).start()

        @pl.when(i > 0)
        def _():
            pltpu.make_async_remote_copy(
                src_ref=message.at[home],
                dst_ref=inbox.at[REACH + s],
                send_sem=send_sem,
                recv_sem=recv_sem,
                device_id=(g, home),
                device_id_type=MESH,
            ).start()

        return carry

    lax.fori_loop(0, slabs, send, 0)
    wait_for(inbox, recv_sem)
    wait_for(inbox.at[pl.ds(0, slabs - 1)], send_sem)

    @pl.when(at_edge)
    def _():
        wait_for(inbox.at[pl.ds(0, slabs)], edge_sem)


def interpolate_kernel(inbox, home_ref, fraction_ref, offset_ref, out_ref, weights):
    blocks, markers = fraction_ref.shape[1], fraction_ref.shape[2]
    weights[...] = jnp.zeros_like(weights)
    row_y = lax.broadcasted_iota(jnp.int32, (16, markers), 0)
    row_x = jnp.where(row_y < 12, row_y, row_y - 4)
    in_low = lax.broadcasted_iota(jnp.int32, (8, markers), 0) < 4

    def interpolate(i, carry):
        f = jnp.concatenate([fraction_ref[d, pl.ds(i, 1), :] for d in range(3)], axis=0)
        o = [offset_ref[d, pl.ds(i, 1), :] for d in range(3)]
        root = jnp.sqrt(1.0 + 4.0 * f - 4.0 * f * f)
        low, high = 3.0 - 2.0 * f, 1.0 + 2.0 * f
        taps = ((low - root) * 0.125, (low + root) * 0.125, (high + root) * 0.125, (high - root) * 0.125)
        weight_x = jnp.zeros((16, markers), jnp.float32)
        weight_y = jnp.zeros((16, markers), jnp.float32)
        for e in range(4):
            weight_x = jnp.where(row_x == o[1] + e, taps[e][1:2], weight_x)
            weight_y = jnp.where(row_y == o[2] + e, taps[e][2:3], weight_y)
        y_high, y_low = split(weight_y)
        weights[0, 0:16, :] = y_high
        weights[1, 0:16, :] = y_low
        near = o[0] == 0
        none = jnp.zeros((1, markers), jnp.float32)
        tap_z = [none] + [tap[0:1] for tap in taps] + [none]
        weight_z = [jnp.where(near, tap_z[j + 1], tap_z[j]) for j in range(PLANES)]
        source = home_ref[i]
        slot = home_ref[blocks + i]
        cells = []
        for j in range(PLANES):
            place = CELLS * (2 * (PLANES - 1 - j) + slot)
            cells.append(pltpu.roll(inbox[source + j], (2 * LANES - place) & (LANES - 1), 1))
        cells_high, cells_low = split(jnp.concatenate(cells, axis=0))
        values = dot(cells_high, weights[0]) + (dot(cells_low, weights[0]) + dot(cells_high, weights[1]))
        sums = []
        for t in range(ROWS_OUT // 8):
            total = weight_z[0] * values[8 * t : 8 * t + 8]
            for j in range(1, PLANES):
                total = total + weight_z[j] * values[ROWS_OUT * j + 8 * t : ROWS_OUT * j + 8 * t + 8]
            sums.append(total)
        x_first, x_last = weight_x[0:8], weight_x[8:16]
        mixed, last = sums[3] * x_last, sums[4] * x_last
        tails = (jnp.where(in_low, mixed, 0.0), jnp.where(in_low, 0.0, mixed), jnp.where(in_low, last, 0.0))
        for c in range(3):
            out_ref[c, pl.ds(i, 1), :] = jnp.sum(sums[c] * x_first + tails[c], axis=0, keepdims=True)
        return carry

    lax.fori_loop(0, blocks, interpolate, 0)


def sample(plane, requests, home, fraction, offsets, groups, slabs):
    vmem, smem = pl.BlockSpec(memory_space=pltpu.VMEM), pl.BlockSpec(memory_space=pltpu.SMEM)
    markers = fraction.shape[2]
    message = pl.pallas_call(
        cut_kernel,
        out_shape=jax.ShapeDtypeStruct((slabs, ROWS_OUT, LANES), jnp.float32),
        in_specs=[vmem, smem],
        out_specs=vmem,
        cost_estimate=pl.CostEstimate(flops=5_000_000, bytes_accessed=1_500_000, transcendentals=0),
    )(plane, requests)
    inbox = pl.pallas_call(
        functools.partial(exchange_kernel, groups, slabs),
        out_shape=jax.ShapeDtypeStruct((slabs + 2 * REACH, ROWS_OUT, LANES), jnp.float32),
        in_specs=[vmem],
        out_specs=vmem,
        scratch_shapes=[pltpu.SemaphoreType.DMA] * 3,
        compiler_params=pltpu.CompilerParams(collective_id=1, has_side_effects=True),
        cost_estimate=pl.CostEstimate(flops=0, bytes_accessed=20_000_000, transcendentals=0),
    )(message)
    return pl.pallas_call(
        interpolate_kernel,
        out_shape=jax.ShapeDtypeStruct(fraction.shape, jnp.float32),
        in_specs=[vmem, smem, vmem, vmem],
        out_specs=vmem,
        scratch_shapes=[pltpu.VMEM((2, LANES, markers), jnp.bfloat16)],
        cost_estimate=pl.CostEstimate(flops=200_000_000, bytes_accessed=1_500_000, transcendentals=25_000),
    )(inbox, home, fraction, offsets)


def patch_requests(source, block_tile, slabs, side):
    blocks = source.shape[0]
    order = jnp.arange(blocks, dtype=jnp.int32)
    code = (order * side + block_tile[:, 0]) * side + block_tile[:, 1]
    named = source[None, :] == jnp.arange(slabs, dtype=jnp.int32)[:, None]
    first = jnp.min(jnp.where(named, code[None, :], side * side * blocks), axis=1)
    second = jnp.max(jnp.where(named, code[None, :], 0), axis=1)
    chosen = jnp.stack([first, second], axis=1)
    starts = jnp.stack([8 * (chosen // side % side), (8 * (chosen % side) - 2 + side) % side], axis=2)
    return jnp.pad(starts.reshape(1, -1), ((0, 0), (0, LANES - 4 * slabs)))


def local(groups, slabs, spectrum, marker_fraction, marker_offsets, block_source, block_tile):
    source = block_source[:, 0]
    asking = patch_requests(source, block_tile, slabs, spectrum.shape[3])
    order = jnp.arange(source.shape[0])
    again = jnp.any((source[:, None] == source[None, :]) & (order[:, None] > order[None, :]), axis=1)
    home = jnp.concatenate([source, again.astype(jnp.int32)])
    plane, asked = synthesize(asking, spectrum, groups, slabs)
    fraction, offsets = jnp.transpose(marker_fraction, (1, 0, 2)), jnp.transpose(marker_offsets, (1, 0, 2))
    answer = sample(plane, asked, home, fraction, offsets, groups, slabs)
    return jnp.transpose(answer, (1, 0, 2))


def solution(mesh):
    groups, slabs = mesh.shape["grp"], mesh.shape["gz"]
    both = ("grp", "gz")
    return jax.shard_map(
        functools.partial(local, groups, slabs),
        mesh=mesh,
        in_specs=(
            P(None, None, both, None, None),
            P(both, None, None),
            P(both, None, None),
            P(both, None),
            P(both, None),
        ),
        out_specs=P(both, None, None),
        check_vma=False,
    )
```

```python
import functools
import math

import jax
import jax.numpy as jnp
import ml_dtypes
import numpy as np
from jax import lax
from jax.experimental import pallas as pl
from jax.experimental.pallas import tpu as pltpu
from jax.sharding import PartitionSpec as P

MESH = pl.DeviceIdType.MESH
REACH = 2
PLANES = 2 * REACH + 1
CELLS = 12
LANES = 128
ROWS_OUT = 40


def bit_reversed(count):
    bits = count.bit_length() - 1
    return np.array([int(format(i, f"0{bits}b")[::-1], 2) if bits else 0 for i in range(count)])


def split_table(values):
    high = values.astype(ml_dtypes.bfloat16)
    low = (values - high.astype(np.float64)).astype(ml_dtypes.bfloat16)
    return jnp.asarray(high), jnp.asarray(low)


def split(x):
    high = x.astype(jnp.bfloat16)
    return high, (x - high.astype(jnp.float32)).astype(jnp.bfloat16)


def dot(a, b):
    return jnp.dot(a, b, preferred_element_type=jnp.float32)


def dot3(a, b):
    return dot(a[0], b[0]) + (dot(a[1], b[0]) + dot(a[0], b[1]))


def turn(re, im, angle_num, angle_den):
    eighth = 8 * angle_num % (8 * angle_den) / angle_den
    if eighth == 0:
        return re, im
    if eighth == 2:
        return -im, re
    cosine, sine = math.cos(math.pi * eighth / 4), math.sin(math.pi * eighth / 4)
    if eighth == 1:
        return (re - im) * cosine, (re + im) * cosine
    if eighth == 3:
        return (re + im) * cosine, (re - im) * sine
    return cosine * re - sine * im, sine * re + cosine * im


def butterflies(items, first_half, position_of, real_at_end=False):
    count = len(items)
    half = 1
    while half < count:
        last = real_at_end and 2 * half == count
        for low in range(count):
            if low // half % 2:
                continue
            high = low + half
            span = half * first_half
            re, im = turn(*items[high], position_of(low) % span, 2 * span)
            first = items[low]
            if last:
                items[low], items[high] = (first[0] + re, None), (first[0] - re, None)
            else:
                items[low] = (first[0] + re, first[1] + im)
                items[high] = (first[0] - re, first[1] - im)
        half *= 2
    return items


def wait_for(ref, semaphore):
    pltpu.make_async_copy(ref, ref, semaphore).wait()


def nearby(me, i, count):
    return lax.rem(me + (2 * lax.rem(i, 2) - 1) * lax.div(i + 1, 2) + count, count)


def transform_kernel(
    groups,
    slabs,
    asking_ref,
    spec_hbm,
    table_hbm,
    twiddle_ref,
    inbox,
    spec_ref,
    table,
    asked_ref,
    asked_smem,
    padded,
    message,
    plane_t,
    rows_in,
    rows_z,
    ring_in,
    real_z,
    velocity,
    send_a,
    recv_a,
    send_b,
    recv_b,
    send_c,
    recv_c,
    send_q,
    recv_q,
    load_sem,
    table_sem,
    send_m,
    edge_m,
    recv_m,
):
    g = lax.axis_index("grp")
    s = lax.axis_index("gz")
    side = spec_ref.shape[2]
    loads = [pltpu.make_async_copy(table_hbm, table, table_sem)]
    loads += [pltpu.make_async_copy(spec_hbm.at[:, c], spec_ref.at[:, c], load_sem.at[c]) for c in range(spec_ref.shape[1])]
    for load in loads:
        load.start()
    rows = side // slabs
    share = slabs // groups
    components = spec_ref.shape[1]

    below, above = lax.rem(g + groups - 1, groups), lax.rem(g + 1, groups)
    at_start, at_end = s < REACH, s >= slabs - REACH
    at_edge = jnp.logical_or(at_start, at_end)
    edge_group = jnp.where(at_start, below, above)

    barrier = pltpu.get_barrier_semaphore()

    def greet_slab(i, carry):
        pl.semaphore_signal(barrier, inc=1, device_id=(g, lax.rem(s + i, slabs)), device_id_type=MESH)
        return carry

    def greet_edge(i, carry):
        pl.semaphore_signal(barrier, inc=1, device_id=(edge_group, lax.rem(s + i, slabs)), device_id_type=MESH)
        return carry

    def greet_ring(i, carry):
        pl.semaphore_signal(barrier, inc=1, device_id=(lax.rem(g + i, groups), s), device_id_type=MESH)
        return carry

    lax.fori_loop(1, slabs, greet_slab, 0)
    lax.fori_loop(1, groups, greet_ring, 0)

    @pl.when(at_edge)
    def _():
        lax.fori_loop(0, slabs, greet_edge, 0)


    def transform_plane(c):
        pltpu.make_async_copy(spec_hbm.at[:, c], spec_ref.at[:, c], load_sem.at[c]).wait()
        cosine, sine = (table[0], table[1]), (table[2], table[3])
        re, im = split(spec_ref[0, c]), split(spec_ref[1, c])
        row_re = split(dot3(re, cosine) - dot3(im, sine))
        row_im = split(dot3(re, sine) + dot3(im, cosine))
        plane_t[c, 0] = dot3(cosine, row_re) - dot3(sine, row_im)
        plane_t[c, 1] = dot3(sine, row_re) + dot3(cosine, row_im)

    def send_rows(c):
        def one(i, carry):
            r = nearby(s, i, slabs)
            pltpu.make_async_remote_copy(
                src_ref=plane_t.at[c, :, pl.ds(pl.multiple_of(r * rows, rows), rows), :],
                dst_ref=rows_in.at[c, s],
                send_sem=send_a.at[c],
                recv_sem=recv_a.at[c],
                device_id=(g, r),
                device_id_type=MESH,
            ).start()
            return carry

        pltpu.make_async_copy(
            plane_t.at[c, :, pl.ds(pl.multiple_of(s * rows, rows), rows), :],
            rows_in.at[c, s],
            recv_a.at[c],
        ).start()
        lax.fori_loop(1, slabs, one, 0)

    def ask(place, device):
        pltpu.make_async_remote_copy(
            src_ref=asking_ref,
            dst_ref=asked_ref.at[place],
            send_sem=send_q,
            recv_sem=recv_q,
            device_id=device,
            device_id_type=MESH,
        ).start()

    def ask_slab(i, carry):
        ask(s, (g, nearby(s, i, slabs)))
        return carry

    loads[0].wait()
    transform_plane(0)
    pl.semaphore_wait(barrier, slabs - 1 + groups - 1 + 2 * REACH)
    send_rows(0)
    pltpu.make_async_copy(asking_ref, asked_ref.at[s], recv_q).start()
    lax.fori_loop(1, slabs, ask_slab, 0)
    for k in range(REACH):
        ask(slabs + s, (below, slabs - 1 - k))
        ask(slabs + s, (above, k))

    def later_plane(c, carry):
        transform_plane(c)
        send_rows(c)
        return carry

    lax.fori_loop(1, components, later_plane, 0)

    inner = min(8, slabs)
    outer = slabs // inner

    def along_slab(c, carry):
        wait_for(rows_in.at[c], recv_a.at[c])
        for block in range(outer):
            items = {k: (rows_in[c, inner * block + k, 0], rows_in[c, inner * block + k, 1]) for k in range(inner)}
            items = butterflies(items, 1, lambda k: k)
            for k in range(inner):
                rows_in[c, inner * block + k, 0], rows_in[c, inner * block + k, 1] = items[k]
        for k in range(inner):
            items = {m: (rows_in[c, inner * m + k, 0], rows_in[c, inner * m + k, 1]) for m in range(outer)}
            items = butterflies(items, inner, lambda m, k=k: inner * m + k)
            for m in range(outer):
                w = inner * m + k
                cosine, sine = twiddle_ref[g * 2 * slabs + 2 * w], twiddle_ref[g * 2 * slabs + 2 * w + 1]
                re, im = items[m]
                rows_z[c, w, 0] = cosine * re - sine * im
                rows_z[c, w, 1] = sine * re + cosine * im

        def one(i, inner_carry):
            to = nearby(g, i, groups)
            pltpu.make_async_remote_copy(
                src_ref=rows_z.at[c, pl.ds(to * share, share)],
                dst_ref=ring_in.at[c, g],
                send_sem=send_b.at[c],
                recv_sem=recv_b.at[c],
                device_id=(to, s),
                device_id_type=MESH,
            ).start()
            return inner_carry

        pltpu.make_async_copy(rows_z.at[c, pl.ds(g * share, share)], ring_in.at[c, g], recv_b.at[c]).start()
        lax.fori_loop(1, groups, one, 0)
        return carry

    lax.fori_loop(0, components, along_slab, 0)

    def along_ring(c, carry):
        wait_for(ring_in.at[c], recv_b.at[c])
        for k in range(share):
            items = {q: (ring_in[c, q, k, 0], ring_in[c, q, k, 1]) for q in range(groups)}
            items = butterflies(items, 1, lambda q: q, real_at_end=True)
            for u in range(groups):
                real_z[c, u, k] = items[u][0]

        def one(i, inner_carry):
            to = nearby(g, lax.div(i, share), groups)
            k = lax.rem(i, share)
            w = g * share + k
            mine = jnp.logical_and(to == g, w == s)
            place = velocity.at[c, pl.ds(pl.multiple_of(s * rows, rows), rows), :]

            @pl.when(mine)
            def _():
                pltpu.make_async_copy(real_z.at[c, to, k], place, recv_c.at[c]).start()

            @pl.when(jnp.logical_not(mine))
            def _():
                pltpu.make_async_remote_copy(
                    src_ref=real_z.at[c, to, k],
                    dst_ref=place,
                    send_sem=send_c.at[c],
                    recv_sem=recv_c.at[c],
                    device_id=(to, w),
                    device_id_type=MESH,
                ).start()

            return inner_carry

        lax.fori_loop(0, slabs, one, 0)
        return carry


    edge_place = jnp.where(at_start, slabs + REACH + s, s - (slabs - REACH))
    low_half = lax.broadcasted_iota(jnp.int32, (8, LANES), 0) < 4
    lane = lax.broadcasted_iota(jnp.int32, (16, LANES), 1)

    def place_plane(c):
        wait_for(velocity.at[c], recv_c.at[c])
        for half in range(2):
            columns = slice(half * LANES, (half + 1) * LANES)
            whole = [velocity[c, side - REACH : side, columns], velocity[c, :, columns], velocity[c, 0 : 8 - REACH, columns]]
            padded[c, half] = jnp.concatenate(whole, axis=0).reshape(side // 8 + 1, 8, LANES)

    def cut_for(c, home):
        cut = jnp.zeros((16, LANES), jnp.float32)
        for slot in range(2 * PLANES):
            centre = s + slot // 2 - REACH
            inside = jnp.logical_and(centre >= 0, centre < slabs)
            row = jnp.where(inside, home, home + slabs)
            column = 4 * lax.rem(centre + slabs, slabs) + 2 * (slot % 2)
            tile = asked_smem[row, 0, column]
            first = asked_smem[row, 0, column + 1]
            half = first >> 7
            first = first & (LANES - 1)
            near = jnp.concatenate([padded[c, half, tile], padded[c, half, tile + 1]], axis=0)
            far = jnp.concatenate([padded[c, 1 - half, tile], padded[c, 1 - half, tile + 1]], axis=0)
            cells = jnp.where(lane >= first, near, far)
            moved = pltpu.roll(cells, (CELLS * slot + LANES - first) & (LANES - 1), 1)
            taken = jnp.logical_and(lane >= CELLS * slot, lane < CELLS * (slot + 1))
            cut = jnp.where(taken, moved, cut)
        return cut

    def deliver(home, i, tiles):
        part = pl.ds(8 * tiles[0], 8 * len(tiles))

        @pl.when(at_edge)
        def _():
            pltpu.make_async_remote_copy(
                src_ref=message.at[home, part],
                dst_ref=inbox.at[edge_place, part],
                send_sem=edge_m,
                recv_sem=recv_m,
                device_id=(edge_group, home),
                device_id_type=MESH,
            ).start()

        @pl.when(i == 0)
        def _():
            pltpu.make_async_copy(message.at[home, part], inbox.at[REACH + s, part], recv_m).start()

        @pl.when(i > 0)
        def _():
            pltpu.make_async_remote_copy(
                src_ref=message.at[home, part],
                dst_ref=inbox.at[REACH + s, part],
                send_sem=send_m,
                recv_sem=recv_m,
                device_id=(g, home),
                device_id_type=MESH,
            ).start()

    def serve_first(i, carry):
        home = nearby(s, i, slabs)
        cut = cut_for(0, home)
        message[home, 0:8, :] = cut[0:8]
        message[home, 16:24, :] = cut[8:16]
        return carry

    def serve_second(i, carry):
        home = nearby(s, i, slabs)
        cut = cut_for(1, home)
        message[home, 8:16, :] = cut[0:8]
        message[home, 16:24, :] = jnp.where(low_half, message[home, 16:24, :], pltpu.roll(cut[8:16], 4, 0))
        deliver(home, i, (0, 1, 2))
        return carry

    def serve_third(i, carry):
        home = nearby(s, i, slabs)
        message[home, 24:40, :] = cut_for(2, home)
        deliver(home, i, (3, 4))
        return carry

    along_ring(0, 0)

    @pl.when(at_edge)
    def _():
        wait_for(asked_ref, recv_q)
        pltpu.sync_copy(asked_ref, asked_smem)

    @pl.when(jnp.logical_not(at_edge))
    def _():
        wait_for(asked_ref.at[pl.ds(0, slabs)], recv_q)
        pltpu.sync_copy(asked_ref.at[pl.ds(0, slabs)], asked_smem.at[pl.ds(0, slabs)])

    along_ring(1, 0)
    place_plane(0)
    lax.fori_loop(0, slabs, serve_first, 0)
    along_ring(2, 0)
    place_plane(1)
    lax.fori_loop(0, slabs, serve_second, 0)
    place_plane(2)
    lax.fori_loop(0, slabs, serve_third, 0)
    wait_for(inbox, recv_m)

    wait_for(inbox.at[pl.ds(0, slabs - 1)], send_m)

    @pl.when(at_edge)
    def _():
        wait_for(inbox.at[pl.ds(0, slabs)], edge_m)

    wait_for(asked_ref.at[pl.ds(0, slabs - 1 + 2 * REACH)], send_q)

    holds_own = lax.div(s, share) == g

    def drain(c, carry):
        wait_for(rows_in.at[c, pl.ds(0, slabs - 1)], send_a.at[c])
        wait_for(ring_in.at[c, pl.ds(0, groups - 1)], send_b.at[c])

        @pl.when(holds_own)
        def _():
            wait_for(velocity.at[c, pl.ds(0, side - rows)], send_c.at[c])

        @pl.when(jnp.logical_not(holds_own))
        def _():
            wait_for(velocity.at[c], send_c.at[c])

        return carry

    lax.fori_loop(0, components, drain, 0)


def synthesize(asking, spectrum, groups, slabs):
    components, side = spectrum.shape[1], spectrum.shape[3]
    rows, share = side // slabs, slabs // groups
    ids = np.arange(side)
    angle = 2.0 * np.pi / side * (ids[:, None] * ids[None, :] % side)
    tables = jnp.stack(split_table(np.cos(angle)) + split_table(np.sin(angle)))
    count = groups * slabs
    twist = 2.0 * np.pi / count * (bit_reversed(groups)[:, None] * np.arange(slabs)[None, :])
    scale = 1.0 / math.sqrt(side * side * count)
    twiddle = np.stack([np.cos(twist), np.sin(twist)], axis=-1) * scale
    twiddle = jnp.asarray(twiddle.reshape(-1).astype(np.float32))
    vmem, hbm = pl.BlockSpec(memory_space=pltpu.VMEM), pl.BlockSpec(memory_space=pltpu.HBM)
    f32 = jnp.float32
    return pl.pallas_call(
        functools.partial(transform_kernel, groups, slabs),
        out_shape=jax.ShapeDtypeStruct((slabs + 2 * REACH, ROWS_OUT, LANES), f32),
        in_specs=[vmem, hbm, hbm, pl.BlockSpec(memory_space=pltpu.SMEM)],
        out_specs=vmem,
        scratch_shapes=[
            pltpu.VMEM((2, components, side, side), f32),
            pltpu.VMEM((4, side, side), jnp.bfloat16),
            pltpu.VMEM((2 * slabs, 1, LANES), jnp.int32),
            pltpu.SMEM((2 * slabs, 1, LANES), jnp.int32),
            pltpu.VMEM((components, 2, side // 8 + 1, 8, LANES), f32),
            pltpu.VMEM((slabs, ROWS_OUT, LANES), f32),
            pltpu.VMEM((components, 2, side, side), f32),
            pltpu.VMEM((components, slabs, 2, rows, side), f32),
            pltpu.VMEM((components, slabs, 2, rows, side), f32),
            pltpu.VMEM((components, groups, share, 2, rows, side), f32),
            pltpu.VMEM((components, groups, share, rows, side), f32),
            pltpu.VMEM((components, side, side), f32),
        ]
        + [pltpu.SemaphoreType.DMA((components,))] * 6
        + [pltpu.SemaphoreType.DMA] * 2
        + [pltpu.SemaphoreType.DMA((components,))]
        + [pltpu.SemaphoreType.DMA] * 4,
        compiler_params=pltpu.CompilerParams(
            collective_id=0, has_side_effects=True, vmem_limit_bytes=62 * 2**20
        ),
        cost_estimate=pl.CostEstimate(flops=2_500_000_000, bytes_accessed=100_000_000, transcendentals=0),
    )(asking, spectrum[:, :, 0], tables, twiddle)


def interpolate_kernel(inbox, home_ref, fraction_ref, offset_ref, out_ref, weights):
    blocks, markers = fraction_ref.shape[1], fraction_ref.shape[2]
    weights[...] = jnp.zeros_like(weights)
    group = weights.shape[0]
    first_lanes = lax.broadcasted_iota(jnp.int32, (ROWS_OUT * PLANES, LANES), 1) < 16
    row_y = lax.broadcasted_iota(jnp.int32, (16, markers), 0)
    row_x = jnp.where(row_y < 12, row_y, row_y - 4)
    in_low = lax.broadcasted_iota(jnp.int32, (8, markers), 0) < 4

    def one_block(i, weights):
        f = jnp.concatenate([fraction_ref[d, pl.ds(i, 1), :] for d in range(3)], axis=0)
        o = [offset_ref[d, pl.ds(i, 1), :] for d in range(3)]
        root = jnp.sqrt(1.0 + 4.0 * f - 4.0 * f * f)
        low, high = 3.0 - 2.0 * f, 1.0 + 2.0 * f
        taps = ((low - root) * 0.125, (low + root) * 0.125, (high + root) * 0.125, (high - root) * 0.125)
        weight_x = jnp.zeros((16, markers), jnp.float32)
        weight_y = jnp.zeros((16, markers), jnp.float32)
        for e in range(4):
            weight_x = jnp.where(row_x == o[1] + e, taps[e][1:2], weight_x)
            weight_y = jnp.where(row_y == o[2] + e, taps[e][2:3], weight_y)
        y_high, y_low = split(weight_y)
        weights[0:16, :] = y_high
        weights[16:32, :] = y_low
        weights[LANES : LANES + 16, :] = y_high
        near = o[0] == 0
        none = jnp.zeros((1, markers), jnp.float32)
        tap_z = [none] + [tap[0:1] for tap in taps] + [none]
        weight_z = [jnp.where(near, tap_z[j + 1], tap_z[j]) for j in range(PLANES)]
        source = home_ref[i]
        slot = home_ref[blocks + i]
        cells = []
        for j in range(PLANES):
            place = CELLS * (2 * (PLANES - 1 - j) + slot)
            cells.append(pltpu.roll(inbox[source + j], (2 * LANES - place) & (LANES - 1), 1))
        cells = jnp.concatenate(cells, axis=0)
        cells = jnp.where(first_lanes, cells, pltpu.roll(cells, 16, 1))
        values = dot(jnp.concatenate(split(cells), axis=1), weights[...])
        sums = []
        for t in range(ROWS_OUT // 8):
            total = weight_z[0] * values[8 * t : 8 * t + 8]
            for j in range(1, PLANES):
                total = total + weight_z[j] * values[ROWS_OUT * j + 8 * t : ROWS_OUT * j + 8 * t + 8]
            sums.append(total)
        x_first, x_last = weight_x[0:8], weight_x[8:16]
        mixed, last = sums[2] * x_last, sums[4] * x_last
        tails = (jnp.where(in_low, mixed, 0.0), jnp.where(in_low, 0.0, mixed), jnp.where(in_low, last, 0.0))
        for c in range(3):
            out_ref[c, pl.ds(i, 1), :] = jnp.sum(sums[(0, 1, 3)[c]] * x_first + tails[c], axis=0, keepdims=True)

    def several(i, carry):
        for k in range(group):
            one_block(group * i + k, weights.at[k])
        return carry

    lax.fori_loop(0, blocks // group, several, 0)


def sample(inbox, home, fraction, offsets):
    vmem, smem = pl.BlockSpec(memory_space=pltpu.VMEM), pl.BlockSpec(memory_space=pltpu.SMEM)
    markers = fraction.shape[2]
    return pl.pallas_call(
        interpolate_kernel,
        out_shape=jax.ShapeDtypeStruct(fraction.shape, jnp.float32),
        in_specs=[vmem, smem, vmem, vmem],
        out_specs=vmem,
        scratch_shapes=[pltpu.VMEM((4, 2 * LANES, markers), jnp.bfloat16)],
        cost_estimate=pl.CostEstimate(flops=200_000_000, bytes_accessed=1_500_000, transcendentals=25_000),
    )(inbox, home, fraction, offsets)


def patch_requests(source, block_tile, slabs, side):
    blocks = source.shape[0]
    order = jnp.arange(blocks, dtype=jnp.int32)
    code = (order * side + block_tile[:, 0]) * side + block_tile[:, 1]
    named = source[None, :] == jnp.arange(slabs, dtype=jnp.int32)[:, None]
    first = jnp.min(jnp.where(named, code[None, :], side * side * blocks), axis=1)
    second = jnp.max(jnp.where(named, code[None, :], 0), axis=1)
    chosen = jnp.stack([first, second], axis=1)
    starts = jnp.stack([chosen // side % side, (8 * (chosen % side) - 2 + side) % side], axis=2)
    return jnp.pad(starts.reshape(1, -1), ((0, 0), (0, LANES - 4 * slabs)))


def local(groups, slabs, spectrum, marker_fraction, marker_offsets, block_source, block_tile):
    source = block_source[:, 0]
    asking = patch_requests(source, block_tile, slabs, spectrum.shape[3])
    order = jnp.arange(source.shape[0])
    again = jnp.any((source[:, None] == source[None, :]) & (order[:, None] > order[None, :]), axis=1)
    home = jnp.concatenate([source, again.astype(jnp.int32)])
    asking, home = lax.optimization_barrier((asking, home))
    inbox = synthesize(asking, spectrum, groups, slabs)
    fraction, offsets = jnp.transpose(marker_fraction, (1, 0, 2)), jnp.transpose(marker_offsets, (1, 0, 2))
    answer = sample(inbox, home, fraction, offsets)
    return jnp.transpose(answer, (1, 0, 2))


def solution(mesh):
    groups, slabs = mesh.shape["grp"], mesh.shape["gz"]
    both = ("grp", "gz")
    return jax.shard_map(
        functools.partial(local, groups, slabs),
        mesh=mesh,
        in_specs=(
            P(None, None, both, None, None),
            P(both, None, None),
            P(both, None, None),
            P(both, None),
            P(both, None),
        ),
        out_specs=P(both, None, None),
        check_vma=False,
    )
```

```python
import functools
import math

import jax
import jax.numpy as jnp
import ml_dtypes
import numpy as np
from jax import lax
from jax.experimental import pallas as pl
from jax.experimental.pallas import tpu as pltpu
from jax.sharding import PartitionSpec as P

MESH = pl.DeviceIdType.MESH
REACH = 2
PLANES = 2 * REACH + 1
CELLS = 12
LANES = 128
ROWS_OUT = 40


def bit_reversed(count):
    bits = count.bit_length() - 1
    return np.array([int(format(i, f"0{bits}b")[::-1], 2) if bits else 0 for i in range(count)])


def split_table(values):
    high = values.astype(ml_dtypes.bfloat16)
    low = (values - high.astype(np.float64)).astype(ml_dtypes.bfloat16)
    return jnp.asarray(high), jnp.asarray(low)


def split(x):
    high = x.astype(jnp.bfloat16)
    return high, (x - high.astype(jnp.float32)).astype(jnp.bfloat16)


def dot(a, b):
    return jnp.dot(a, b, preferred_element_type=jnp.float32)


def dot3(a, b):
    return dot(a[0], b[0]) + (dot(a[1], b[0]) + dot(a[0], b[1]))


def turn(re, im, angle_num, angle_den):
    eighth = 8 * angle_num % (8 * angle_den) / angle_den
    if eighth == 0:
        return re, im
    if eighth == 2:
        return -im, re
    cosine, sine = math.cos(math.pi * eighth / 4), math.sin(math.pi * eighth / 4)
    if eighth == 1:
        return (re - im) * cosine, (re + im) * cosine
    if eighth == 3:
        return (re + im) * cosine, (re - im) * sine
    return cosine * re - sine * im, sine * re + cosine * im


def butterflies(items, first_half, position_of, real_at_end=False):
    count = len(items)
    half = 1
    while half < count:
        last = real_at_end and 2 * half == count
        for low in range(count):
            if low // half % 2:
                continue
            high = low + half
            span = half * first_half
            re, im = turn(*items[high], position_of(low) % span, 2 * span)
            first = items[low]
            if last:
                items[low], items[high] = (first[0] + re, None), (first[0] - re, None)
            else:
                items[low] = (first[0] + re, first[1] + im)
                items[high] = (first[0] - re, first[1] - im)
        half *= 2
    return items


def wait_for(ref, semaphore):
    pltpu.make_async_copy(ref, ref, semaphore).wait()


def nearby(me, i, count):
    return lax.rem(me + (2 * lax.rem(i, 2) - 1) * lax.div(i + 1, 2) + count, count)


def transform_kernel(
    groups,
    slabs,
    source_ref,
    tile_ref,
    spec_hbm,
    table_hbm,
    twiddle_ref,
    inbox,
    asking_ref,
    spec_ref,
    table,
    asked_ref,
    asked_smem,
    padded,
    message,
    plane_t,
    rows_in,
    rows_z,
    ring_in,
    real_z,
    velocity,
    send_a,
    recv_a,
    send_b,
    recv_b,
    send_c,
    recv_c,
    send_q,
    recv_q,
    load_sem,
    table_sem,
    send_m,
    edge_m,
    recv_m,
):
    g = lax.axis_index("grp")
    s = lax.axis_index("gz")
    side = spec_ref.shape[2]
    loads = [pltpu.make_async_copy(table_hbm, table, table_sem)]
    loads += [pltpu.make_async_copy(spec_hbm.at[:, c], spec_ref.at[:, c], load_sem.at[c]) for c in range(spec_ref.shape[1])]
    for load in loads:
        load.start()
    rows = side // slabs
    share = slabs // groups
    components = spec_ref.shape[1]

    below, above = lax.rem(g + groups - 1, groups), lax.rem(g + 1, groups)
    at_start, at_end = s < REACH, s >= slabs - REACH
    at_edge = jnp.logical_or(at_start, at_end)
    edge_group = jnp.where(at_start, below, above)

    barrier = pltpu.get_barrier_semaphore()

    def greet_slab(i, carry):
        pl.semaphore_signal(barrier, inc=1, device_id=(g, lax.rem(s + i, slabs)), device_id_type=MESH)
        return carry

    def greet_edge(i, carry):
        pl.semaphore_signal(barrier, inc=1, device_id=(edge_group, lax.rem(s + i, slabs)), device_id_type=MESH)
        return carry

    def greet_ring(i, carry):
        pl.semaphore_signal(barrier, inc=1, device_id=(lax.rem(g + i, groups), s), device_id_type=MESH)
        return carry

    lax.fori_loop(1, slabs, greet_slab, 0)
    lax.fori_loop(1, groups, greet_ring, 0)

    @pl.when(at_edge)
    def _():
        lax.fori_loop(0, slabs, greet_edge, 0)


    def transform_plane(c):
        pltpu.make_async_copy(spec_hbm.at[:, c], spec_ref.at[:, c], load_sem.at[c]).wait()
        cosine, sine = (table[0], table[1]), (table[2], table[3])
        re, im = split(spec_ref[0, c]), split(spec_ref[1, c])
        row_re = split(dot3(re, cosine) - dot3(im, sine))
        row_im = split(dot3(re, sine) + dot3(im, cosine))
        plane_t[c, 0] = dot3(cosine, row_re) - dot3(sine, row_im)
        plane_t[c, 1] = dot3(sine, row_re) + dot3(cosine, row_im)

    def send_rows(c):
        def one(i, carry):
            r = nearby(s, i, slabs)
            pltpu.make_async_remote_copy(
                src_ref=plane_t.at[c, :, pl.ds(pl.multiple_of(r * rows, rows), rows), :],
                dst_ref=rows_in.at[c, s],
                send_sem=send_a.at[c],
                recv_sem=recv_a.at[c],
                device_id=(g, r),
                device_id_type=MESH,
            ).start()
            return carry

        pltpu.make_async_copy(
            plane_t.at[c, :, pl.ds(pl.multiple_of(s * rows, rows), rows), :],
            rows_in.at[c, s],
            recv_a.at[c],
        ).start()
        lax.fori_loop(1, slabs, one, 0)

    def make_requests():
        blocks = source_ref.shape[1]
        down = lax.broadcasted_iota(jnp.int32, (blocks, blocks), 0)
        along = lax.broadcasted_iota(jnp.int32, (blocks, blocks), 1)
        tiles = side // 8
        code = (along[0:1] * tiles + tile_ref[0:1, :]) * tiles + tile_ref[1:2, :]

        def upright(row):
            return jnp.sum(jnp.where(down == along, row.astype(jnp.float32), 0.0), axis=1, keepdims=True)

        spot = lax.broadcasted_iota(jnp.int32, (blocks, LANES), 1)
        named = upright(source_ref[...]) == (spot >> 2).astype(jnp.float32)
        codes = upright(code)
        first = jnp.min(jnp.where(named, codes, float(tiles * tiles * blocks)), axis=0, keepdims=True)
        second = jnp.max(jnp.where(named, codes, 0.0), axis=0, keepdims=True)
        chosen = jnp.where((spot[0:1] & 2) == 0, first, second).astype(jnp.int32)
        across = (chosen & (tiles - 1)) * 8 + side - REACH
        asking_ref[...] = jnp.where((spot[0:1] & 1) == 0, (chosen // tiles) & (tiles - 1), across & (side - 1))

    def ask(place, device):
        pltpu.make_async_remote_copy(
            src_ref=asking_ref,
            dst_ref=asked_ref.at[place],
            send_sem=send_q,
            recv_sem=recv_q,
            device_id=device,
            device_id_type=MESH,
        ).start()

    def ask_slab(i, carry):
        ask(s, (g, nearby(s, i, slabs)))
        return carry

    loads[0].wait()
    transform_plane(0)
    pl.semaphore_wait(barrier, slabs - 1 + groups - 1 + 2 * REACH)
    send_rows(0)
    make_requests()
    pltpu.make_async_copy(asking_ref, asked_ref.at[s], recv_q).start()
    lax.fori_loop(1, slabs, ask_slab, 0)
    for k in range(REACH):
        ask(slabs + s, (below, slabs - 1 - k))
        ask(slabs + s, (above, k))

    def later_plane(c, carry):
        transform_plane(c)
        return carry

    lax.fori_loop(1, components, later_plane, 0)

    inner = min(8, slabs)
    outer = slabs // inner

    def along_slab(c):
        for block in range(outer):
            items = {k: (rows_in[c, inner * block + k, 0], rows_in[c, inner * block + k, 1]) for k in range(inner)}
            items = butterflies(items, 1, lambda k: k)
            for k in range(inner):
                rows_in[c, inner * block + k, 0], rows_in[c, inner * block + k, 1] = items[k]
        for k in range(inner):
            items = {m: (rows_in[c, inner * m + k, 0], rows_in[c, inner * m + k, 1]) for m in range(outer)}
            items = butterflies(items, inner, lambda m, k=k: inner * m + k)
            for m in range(outer):
                w = inner * m + k
                cosine, sine = twiddle_ref[g * 2 * slabs + 2 * w], twiddle_ref[g * 2 * slabs + 2 * w + 1]
                re, im = items[m]
                rows_z[c, w, 0] = cosine * re - sine * im
                rows_z[c, w, 1] = sine * re + cosine * im

    def send_ring(c):
        def one(i, inner_carry):
            to = nearby(g, i, groups)
            pltpu.make_async_remote_copy(
                src_ref=rows_z.at[c, pl.ds(to * share, share)],
                dst_ref=ring_in.at[c, g],
                send_sem=send_b.at[c],
                recv_sem=recv_b.at[c],
                device_id=(to, s),
                device_id_type=MESH,
            ).start()
            return inner_carry

        pltpu.make_async_copy(rows_z.at[c, pl.ds(g * share, share)], ring_in.at[c, g], recv_b.at[c]).start()
        lax.fori_loop(1, groups, one, 0)

    def along_ring(c):
        for k in range(share):
            items = {q: (ring_in[c, q, k, 0], ring_in[c, q, k, 1]) for q in range(groups)}
            items = butterflies(items, 1, lambda q: q, real_at_end=True)
            for u in range(groups):
                real_z[c, u, k] = items[u][0]

        def one(i, inner_carry):
            to = nearby(g, lax.div(i, share), groups)
            k = lax.rem(i, share)
            w = g * share + k
            mine = jnp.logical_and(to == g, w == s)
            place = velocity.at[c, pl.ds(pl.multiple_of(s * rows, rows), rows), :]

            @pl.when(mine)
            def _():
                pltpu.make_async_copy(real_z.at[c, to, k], place, recv_c.at[c]).start()

            @pl.when(jnp.logical_not(mine))
            def _():
                pltpu.make_async_remote_copy(
                    src_ref=real_z.at[c, to, k],
                    dst_ref=place,
                    send_sem=send_c.at[c],
                    recv_sem=recv_c.at[c],
                    device_id=(to, w),
                    device_id_type=MESH,
                ).start()

            return inner_carry

        lax.fori_loop(0, slabs, one, 0)


    edge_place = jnp.where(at_start, slabs + REACH + s, s - (slabs - REACH))
    low_half = lax.broadcasted_iota(jnp.int32, (8, LANES), 0) < 4
    lane = lax.broadcasted_iota(jnp.int32, (16, LANES), 1)

    def place_plane(c):
        wait_for(velocity.at[c], recv_c.at[c])
        for half in range(2):
            columns = slice(half * LANES, (half + 1) * LANES)
            whole = [velocity[c, side - REACH : side, columns], velocity[c, :, columns], velocity[c, 0 : 8 - REACH, columns]]
            padded[c, half] = jnp.concatenate(whole, axis=0).reshape(side // 8 + 1, 8, LANES)

    spots = []
    for slot in range(2 * PLANES):
        centre = s + slot // 2 - REACH
        inside = jnp.logical_and(centre >= 0, centre < slabs)
        column = 4 * lax.rem(centre + slabs, slabs) + 2 * (slot % 2)
        spots.append((jnp.where(inside, 0, slabs), column))

    def cut_for(c, home):
        cut = jnp.zeros((16, LANES), jnp.float32)
        for slot in range(2 * PLANES):
            row, column = home + spots[slot][0], spots[slot][1]
            tile = asked_smem[row, 0, column]
            first = asked_smem[row, 0, column + 1]
            half = first >> 7
            first = first & (LANES - 1)
            near = jnp.concatenate([padded[c, half, tile], padded[c, half, tile + 1]], axis=0)
            far = jnp.concatenate([padded[c, 1 - half, tile], padded[c, 1 - half, tile + 1]], axis=0)
            cells = jnp.where(lane >= first, near, far)
            moved = pltpu.roll(cells, (CELLS * slot + LANES - first) & (LANES - 1), 1)
            taken = jnp.logical_and(lane >= CELLS * slot, lane < CELLS * (slot + 1))
            cut = jnp.where(taken, moved, cut)
        return cut

    def deliver(home, i, tiles):
        part = pl.ds(8 * tiles[0], 8 * len(tiles))

        @pl.when(at_edge)
        def _():
            pltpu.make_async_remote_copy(
                src_ref=message.at[home, part],
                dst_ref=inbox.at[edge_place, part],
                send_sem=edge_m,
                recv_sem=recv_m,
                device_id=(edge_group, home),
                device_id_type=MESH,
            ).start()

        @pl.when(i == 0)
        def _():
            pltpu.make_async_copy(message.at[home, part], inbox.at[REACH + s, part], recv_m).start()

        @pl.when(i > 0)
        def _():
            pltpu.make_async_remote_copy(
                src_ref=message.at[home, part],
                dst_ref=inbox.at[REACH + s, part],
                send_sem=send_m,
                recv_sem=recv_m,
                device_id=(g, home),
                device_id_type=MESH,
            ).start()

    def serve_first(i, carry):
        home = nearby(s, i, slabs)
        cut = cut_for(0, home)
        message[home, 0:8, :] = cut[0:8]
        message[home, 16:24, :] = cut[8:16]
        return carry

    def serve_second(i, carry):
        home = nearby(s, i, slabs)
        cut = cut_for(1, home)
        message[home, 8:16, :] = cut[0:8]
        message[home, 16:24, :] = jnp.where(low_half, message[home, 16:24, :], pltpu.roll(cut[8:16], 4, 0))
        deliver(home, i, (0, 1, 2))
        return carry

    def serve_third(i, carry):
        home = nearby(s, i, slabs)
        message[home, 24:40, :] = cut_for(2, home)
        deliver(home, i, (3, 4))
        return carry

    wait_for(rows_in.at[0], recv_a.at[0])
    send_rows(1)
    along_slab(0)
    send_ring(0)
    wait_for(rows_in.at[1], recv_a.at[1])
    send_rows(2)
    along_slab(1)
    send_ring(1)

    @pl.when(at_edge)
    def _():
        wait_for(asked_ref, recv_q)
        pltpu.sync_copy(asked_ref, asked_smem)

    @pl.when(jnp.logical_not(at_edge))
    def _():
        wait_for(asked_ref.at[pl.ds(0, slabs)], recv_q)
        pltpu.sync_copy(asked_ref.at[pl.ds(0, slabs)], asked_smem.at[pl.ds(0, slabs)])

    wait_for(ring_in.at[0], recv_b.at[0])
    along_ring(0)
    wait_for(rows_in.at[2], recv_a.at[2])
    along_slab(2)
    wait_for(ring_in.at[1], recv_b.at[1])
    send_ring(2)
    along_ring(1)
    place_plane(0)
    lax.fori_loop(0, slabs, serve_first, 0)
    wait_for(ring_in.at[2], recv_b.at[2])
    along_ring(2)
    place_plane(1)
    lax.fori_loop(0, slabs, serve_second, 0)
    place_plane(2)
    lax.fori_loop(0, slabs, serve_third, 0)
    wait_for(inbox, recv_m)

    wait_for(inbox.at[pl.ds(0, slabs - 1)], send_m)

    @pl.when(at_edge)
    def _():
        wait_for(inbox.at[pl.ds(0, slabs)], edge_m)

    wait_for(asked_ref.at[pl.ds(0, slabs - 1 + 2 * REACH)], send_q)

    holds_own = lax.div(s, share) == g

    def drain(c, carry):
        wait_for(rows_in.at[c, pl.ds(0, slabs - 1)], send_a.at[c])
        wait_for(ring_in.at[c, pl.ds(0, groups - 1)], send_b.at[c])

        @pl.when(holds_own)
        def _():
            wait_for(velocity.at[c, pl.ds(0, side - rows)], send_c.at[c])

        @pl.when(jnp.logical_not(holds_own))
        def _():
            wait_for(velocity.at[c], send_c.at[c])

        return carry

    lax.fori_loop(0, components, drain, 0)


def synthesize(source, tiles, spectrum, groups, slabs):
    components, side = spectrum.shape[1], spectrum.shape[3]
    rows, share = side // slabs, slabs // groups
    ids = np.arange(side)
    angle = 2.0 * np.pi / side * (ids[:, None] * ids[None, :] % side)
    tables = jnp.stack(split_table(np.cos(angle)) + split_table(np.sin(angle)))
    count = groups * slabs
    twist = 2.0 * np.pi / count * (bit_reversed(groups)[:, None] * np.arange(slabs)[None, :])
    scale = 1.0 / math.sqrt(side * side * count)
    twiddle = np.stack([np.cos(twist), np.sin(twist)], axis=-1) * scale
    twiddle = jnp.asarray(twiddle.reshape(-1).astype(np.float32))
    vmem, hbm = pl.BlockSpec(memory_space=pltpu.VMEM), pl.BlockSpec(memory_space=pltpu.HBM)
    f32 = jnp.float32
    return pl.pallas_call(
        functools.partial(transform_kernel, groups, slabs),
        out_shape=jax.ShapeDtypeStruct((slabs + 2 * REACH, ROWS_OUT, LANES), f32),
        in_specs=[vmem, vmem, hbm, hbm, pl.BlockSpec(memory_space=pltpu.SMEM)],
        out_specs=vmem,
        scratch_shapes=[
            pltpu.VMEM((1, LANES), jnp.int32),
            pltpu.VMEM((2, components, side, side), f32),
            pltpu.VMEM((4, side, side), jnp.bfloat16),
            pltpu.VMEM((2 * slabs, 1, LANES), jnp.int32),
            pltpu.SMEM((2 * slabs, 1, LANES), jnp.int32),
            pltpu.VMEM((components, 2, side // 8 + 1, 8, LANES), f32),
            pltpu.VMEM((slabs, ROWS_OUT, LANES), f32),
            pltpu.VMEM((components, 2, side, side), f32),
            pltpu.VMEM((components, slabs, 2, rows, side), f32),
            pltpu.VMEM((components, slabs, 2, rows, side), f32),
            pltpu.VMEM((components, groups, share, 2, rows, side), f32),
            pltpu.VMEM((components, groups, share, rows, side), f32),
            pltpu.VMEM((components, side, side), f32),
        ]
        + [pltpu.SemaphoreType.DMA((components,))] * 6
        + [pltpu.SemaphoreType.DMA] * 2
        + [pltpu.SemaphoreType.DMA((components,))]
        + [pltpu.SemaphoreType.DMA] * 4,
        compiler_params=pltpu.CompilerParams(
            collective_id=0, has_side_effects=True, vmem_limit_bytes=62 * 2**20
        ),
        cost_estimate=pl.CostEstimate(flops=2_500_000_000, bytes_accessed=100_000_000, transcendentals=0),
    )(source, tiles, spectrum[:, :, 0], tables, twiddle)


def interpolate_kernel(inbox, source_ref, fraction_ref, offset_ref, out_ref, weights, named):
    blocks, markers = fraction_ref.shape[1], fraction_ref.shape[2]
    weights[...] = jnp.zeros_like(weights)
    group = weights.shape[0]
    first_lanes = lax.broadcasted_iota(jnp.int32, (ROWS_OUT * PLANES, LANES), 1) < 16
    row_y = lax.broadcasted_iota(jnp.int32, (16, markers), 0)
    row_x = jnp.where(row_y < 12, row_y, row_y - 4)
    in_low = lax.broadcasted_iota(jnp.int32, (8, markers), 0) < 4

    for k in range(named.shape[0]):
        named[k] = 0

    def one_block(i, weights):
        f = jnp.concatenate([fraction_ref[d, pl.ds(i, 1), :] for d in range(3)], axis=0)
        o = [offset_ref[d, pl.ds(i, 1), :] for d in range(3)]
        root = jnp.sqrt(1.0 + 4.0 * f - 4.0 * f * f)
        low, high = 3.0 - 2.0 * f, 1.0 + 2.0 * f
        taps = ((low - root) * 0.125, (low + root) * 0.125, (high + root) * 0.125, (high - root) * 0.125)
        weight_x = jnp.zeros((16, markers), jnp.float32)
        weight_y = jnp.zeros((16, markers), jnp.float32)
        for e in range(4):
            weight_x = jnp.where(row_x == o[1] + e, taps[e][1:2], weight_x)
            weight_y = jnp.where(row_y == o[2] + e, taps[e][2:3], weight_y)
        y_high, y_low = split(weight_y)
        weights[0:16, :] = y_high
        weights[16:32, :] = y_low
        weights[LANES : LANES + 16, :] = y_high
        near = o[0] == 0
        none = jnp.zeros((1, markers), jnp.float32)
        tap_z = [none] + [tap[0:1] for tap in taps] + [none]
        weight_z = [jnp.where(near, tap_z[j + 1], tap_z[j]) for j in range(PLANES)]
        source = source_ref[0, i]
        slot = named[source]
        named[source] = 1
        cells = []
        for j in range(PLANES):
            place = CELLS * (2 * (PLANES - 1 - j) + slot)
            cells.append(pltpu.roll(inbox[source + j], (2 * LANES - place) & (LANES - 1), 1))
        cells = jnp.concatenate(cells, axis=0)
        cells = jnp.where(first_lanes, cells, pltpu.roll(cells, 16, 1))
        values = dot(jnp.concatenate(split(cells), axis=1), weights[...])
        sums = []
        for t in range(ROWS_OUT // 8):
            total = weight_z[0] * values[8 * t : 8 * t + 8]
            for j in range(1, PLANES):
                total = total + weight_z[j] * values[ROWS_OUT * j + 8 * t : ROWS_OUT * j + 8 * t + 8]
            sums.append(total)
        x_first, x_last = weight_x[0:8], weight_x[8:16]
        mixed, last = sums[2] * x_last, sums[4] * x_last
        tails = (jnp.where(in_low, mixed, 0.0), jnp.where(in_low, 0.0, mixed), jnp.where(in_low, last, 0.0))
        for c in range(3):
            out_ref[c, pl.ds(i, 1), :] = jnp.sum(sums[(0, 1, 3)[c]] * x_first + tails[c], axis=0, keepdims=True)

    def several(i, carry):
        for k in range(group):
            one_block(group * i + k, weights.at[k])
        return carry

    lax.fori_loop(0, blocks // group, several, 0)


def sample(inbox, source, fraction, offsets, slabs):
    vmem, smem = pl.BlockSpec(memory_space=pltpu.VMEM), pl.BlockSpec(memory_space=pltpu.SMEM)
    markers = fraction.shape[2]
    return pl.pallas_call(
        interpolate_kernel,
        out_shape=jax.ShapeDtypeStruct(fraction.shape, jnp.float32),
        in_specs=[vmem, smem, vmem, vmem],
        out_specs=vmem,
        scratch_shapes=[pltpu.VMEM((4, 2 * LANES, markers), jnp.bfloat16), pltpu.SMEM((slabs,), jnp.int32)],
        cost_estimate=pl.CostEstimate(flops=200_000_000, bytes_accessed=1_500_000, transcendentals=25_000),
    )(inbox, source, fraction, offsets)


def local(groups, slabs, spectrum, marker_fraction, marker_offsets, block_source, block_tile):
    source = jnp.transpose(block_source)
    inbox = synthesize(source, jnp.transpose(block_tile), spectrum, groups, slabs)
    fraction, offsets = jnp.transpose(marker_fraction, (1, 0, 2)), jnp.transpose(marker_offsets, (1, 0, 2))
    answer = sample(inbox, source, fraction, offsets, slabs)
    return jnp.transpose(answer, (1, 0, 2))


def solution(mesh):
    groups, slabs = mesh.shape["grp"], mesh.shape["gz"]
    both = ("grp", "gz")
    return jax.shard_map(
        functools.partial(local, groups, slabs),
        mesh=mesh,
        in_specs=(
            P(None, None, both, None, None),
            P(both, None, None),
            P(both, None, None),
            P(both, None),
            P(both, None),
        ),
        out_specs=P(both, None, None),
        check_vma=False,
    )
```

```python
import functools
import math

import jax
import jax.numpy as jnp
import ml_dtypes
import numpy as np
from jax import lax
from jax.experimental import pallas as pl
from jax.experimental.pallas import tpu as pltpu
from jax.sharding import PartitionSpec as P

MESH = pl.DeviceIdType.MESH
REACH = 2
PLANES = 2 * REACH + 1
CELLS = 12
LANES = 128
ROWS_OUT = 40


def bit_reversed(count):
    bits = count.bit_length() - 1
    return np.array([int(format(i, f"0{bits}b")[::-1], 2) if bits else 0 for i in range(count)])


def split_table(values):
    high = values.astype(ml_dtypes.bfloat16)
    low = (values - high.astype(np.float64)).astype(ml_dtypes.bfloat16)
    return jnp.asarray(high), jnp.asarray(low)


def split(x):
    high = x.astype(jnp.bfloat16)
    return high, (x - high.astype(jnp.float32)).astype(jnp.bfloat16)


def dot(a, b):
    return jnp.dot(a, b, preferred_element_type=jnp.float32)


def dot3(a, b):
    return dot(a[0], b[0]) + (dot(a[1], b[0]) + dot(a[0], b[1]))


def turn(re, im, angle_num, angle_den):
    eighth = 8 * angle_num % (8 * angle_den) / angle_den
    if eighth == 0:
        return re, im
    if eighth == 2:
        return -im, re
    cosine, sine = math.cos(math.pi * eighth / 4), math.sin(math.pi * eighth / 4)
    if eighth == 1:
        return (re - im) * cosine, (re + im) * cosine
    if eighth == 3:
        return (re + im) * cosine, (re - im) * sine
    return cosine * re - sine * im, sine * re + cosine * im


def butterflies(items, first_half, position_of, real_at_end=False):
    count = len(items)
    half = 1
    while half < count:
        last = real_at_end and 2 * half == count
        for low in range(count):
            if low // half % 2:
                continue
            high = low + half
            span = half * first_half
            re, im = turn(*items[high], position_of(low) % span, 2 * span)
            first = items[low]
            if last:
                items[low], items[high] = (first[0] + re, None), (first[0] - re, None)
            else:
                items[low] = (first[0] + re, first[1] + im)
                items[high] = (first[0] - re, first[1] - im)
        half *= 2
    return items


def wait_for(ref, semaphore):
    pltpu.make_async_copy(ref, ref, semaphore).wait()


def nearby(me, i, count):
    return lax.rem(me + (2 * lax.rem(i, 2) - 1) * lax.div(i + 1, 2) + count, count)


def transform_kernel(
    groups,
    slabs,
    source_ref,
    tile_ref,
    spec_hbm,
    table_hbm,
    twiddle_ref,
    inbox,
    asking_ref,
    spec_ref,
    table,
    asked_ref,
    asked_smem,
    padded,
    message,
    plane_t,
    rows_in,
    rows_z,
    ring_in,
    real_z,
    velocity,
    send_a,
    recv_a,
    send_b,
    recv_b,
    send_c,
    recv_c,
    send_q,
    recv_q,
    load_sem,
    table_sem,
    send_m,
    edge_m,
    recv_m,
):
    g = lax.axis_index("grp")
    s = lax.axis_index("gz")
    side = spec_ref.shape[2]
    loads = [pltpu.make_async_copy(table_hbm, table, table_sem)]
    loads += [pltpu.make_async_copy(spec_hbm.at[:, c], spec_ref.at[:, c], load_sem.at[c]) for c in range(spec_ref.shape[1])]
    for load in loads:
        load.start()
    rows = side // slabs
    share = slabs // groups
    components = spec_ref.shape[1]

    below, above = lax.rem(g + groups - 1, groups), lax.rem(g + 1, groups)
    at_start, at_end = s < REACH, s >= slabs - REACH
    at_edge = jnp.logical_or(at_start, at_end)
    edge_group = jnp.where(at_start, below, above)

    barrier = pltpu.get_barrier_semaphore()

    def greet_slab(i, carry):
        pl.semaphore_signal(barrier, inc=1, device_id=(g, lax.rem(s + i, slabs)), device_id_type=MESH)
        return carry

    def greet_edge(i, carry):
        pl.semaphore_signal(barrier, inc=1, device_id=(edge_group, lax.rem(s + i, slabs)), device_id_type=MESH)
        return carry

    def greet_ring(i, carry):
        pl.semaphore_signal(barrier, inc=1, device_id=(lax.rem(g + i, groups), s), device_id_type=MESH)
        return carry

    lax.fori_loop(1, slabs, greet_slab, 0)
    lax.fori_loop(1, groups, greet_ring, 0)

    @pl.when(at_edge)
    def _():
        lax.fori_loop(0, slabs, greet_edge, 0)


    def transform_plane(c):
        pltpu.make_async_copy(spec_hbm.at[:, c], spec_ref.at[:, c], load_sem.at[c]).wait()
        cosine, sine = (table[0], table[1]), (table[2], table[3])
        re, im = split(spec_ref[0, c]), split(spec_ref[1, c])
        row_re = split(dot3(re, cosine) - dot3(im, sine))
        row_im = split(dot3(re, sine) + dot3(im, cosine))
        for part, whole in (
            (0, dot3(cosine, row_re) - dot3(sine, row_im)),
            (1, dot3(sine, row_re) + dot3(cosine, row_im)),
        ):
            for half in range(2):
                plane_t[2 * c + half, part] = whole[:, half * LANES : (half + 1) * LANES]

    def send_rows(c):
        def one(i, carry):
            r = nearby(s, i, slabs)
            pltpu.make_async_remote_copy(
                src_ref=plane_t.at[c, :, pl.ds(pl.multiple_of(r * rows, rows), rows), :],
                dst_ref=rows_in.at[c, s],
                send_sem=send_a.at[c],
                recv_sem=recv_a.at[c],
                device_id=(g, r),
                device_id_type=MESH,
            ).start()
            return carry

        pltpu.make_async_copy(
            plane_t.at[c, :, pl.ds(pl.multiple_of(s * rows, rows), rows), :],
            rows_in.at[c, s],
            recv_a.at[c],
        ).start()
        lax.fori_loop(1, slabs, one, 0)

    def make_requests():
        blocks = source_ref.shape[1]
        down = lax.broadcasted_iota(jnp.int32, (blocks, blocks), 0)
        along = lax.broadcasted_iota(jnp.int32, (blocks, blocks), 1)
        tiles = side // 8
        code = (along[0:1] * tiles + tile_ref[0:1, :]) * tiles + tile_ref[1:2, :]

        def upright(row):
            return jnp.sum(jnp.where(down == along, row.astype(jnp.float32), 0.0), axis=1, keepdims=True)

        spot = lax.broadcasted_iota(jnp.int32, (blocks, LANES), 1)
        named = upright(source_ref[...]) == (spot >> 2).astype(jnp.float32)
        codes = upright(code)
        first = jnp.min(jnp.where(named, codes, float(tiles * tiles * blocks)), axis=0, keepdims=True)
        second = jnp.max(jnp.where(named, codes, 0.0), axis=0, keepdims=True)
        chosen = jnp.where((spot[0:1] & 2) == 0, first, second).astype(jnp.int32)
        across = (chosen & (tiles - 1)) * 8 + side - REACH
        asking_ref[...] = jnp.where((spot[0:1] & 1) == 0, (chosen // tiles) & (tiles - 1), across & (side - 1))

    def ask(place, device):
        pltpu.make_async_remote_copy(
            src_ref=asking_ref,
            dst_ref=asked_ref.at[place],
            send_sem=send_q,
            recv_sem=recv_q,
            device_id=device,
            device_id_type=MESH,
        ).start()

    def ask_slab(i, carry):
        ask(s, (g, nearby(s, i, slabs)))
        return carry

    loads[0].wait()
    transform_plane(0)
    pl.semaphore_wait(barrier, slabs - 1 + groups - 1 + 2 * REACH)
    send_rows(0)
    make_requests()
    pltpu.make_async_copy(asking_ref, asked_ref.at[s], recv_q).start()
    lax.fori_loop(1, slabs, ask_slab, 0)
    for k in range(REACH):
        ask(slabs + s, (below, slabs - 1 - k))
        ask(slabs + s, (above, k))

    transform_plane(1)
    send_rows(1)
    transform_plane(2)

    inner = min(8, slabs)
    outer = slabs // inner

    def along_slab(c):
        for block in range(outer):
            items = {k: (rows_in[c, inner * block + k, 0], rows_in[c, inner * block + k, 1]) for k in range(inner)}
            items = butterflies(items, 1, lambda k: k)
            for k in range(inner):
                rows_in[c, inner * block + k, 0], rows_in[c, inner * block + k, 1] = items[k]
        for k in range(inner):
            items = {m: (rows_in[c, inner * m + k, 0], rows_in[c, inner * m + k, 1]) for m in range(outer)}
            items = butterflies(items, inner, lambda m, k=k: inner * m + k)
            for m in range(outer):
                w = inner * m + k
                cosine, sine = twiddle_ref[g * 2 * slabs + 2 * w], twiddle_ref[g * 2 * slabs + 2 * w + 1]
                re, im = items[m]
                rows_z[c, w, 0] = cosine * re - sine * im
                rows_z[c, w, 1] = sine * re + cosine * im

    def send_ring(c):
        def one(i, inner_carry):
            to = nearby(g, i, groups)
            pltpu.make_async_remote_copy(
                src_ref=rows_z.at[c, pl.ds(to * share, share)],
                dst_ref=ring_in.at[c, g],
                send_sem=send_b.at[c],
                recv_sem=recv_b.at[c],
                device_id=(to, s),
                device_id_type=MESH,
            ).start()
            return inner_carry

        pltpu.make_async_copy(rows_z.at[c, pl.ds(g * share, share)], ring_in.at[c, g], recv_b.at[c]).start()
        lax.fori_loop(1, groups, one, 0)

    def along_ring(c):
        for k in range(share):
            items = {q: (ring_in[c, q, k, 0], ring_in[c, q, k, 1]) for q in range(groups)}
            items = butterflies(items, 1, lambda q: q, real_at_end=True)
            for u in range(groups):
                real_z[c, u, k] = items[u][0]

        def one(i, inner_carry):
            to = nearby(g, lax.div(i, share), groups)
            k = lax.rem(i, share)
            w = g * share + k
            mine = jnp.logical_and(to == g, w == s)
            place = velocity.at[c, pl.ds(pl.multiple_of(s * rows, rows), rows), :]

            @pl.when(mine)
            def _():
                pltpu.make_async_copy(real_z.at[c, to, k], place, recv_c.at[c]).start()

            @pl.when(jnp.logical_not(mine))
            def _():
                pltpu.make_async_remote_copy(
                    src_ref=real_z.at[c, to, k],
                    dst_ref=place,
                    send_sem=send_c.at[c],
                    recv_sem=recv_c.at[c],
                    device_id=(to, w),
                    device_id_type=MESH,
                ).start()

            return inner_carry

        lax.fori_loop(0, slabs, one, 0)


    edge_place = jnp.where(at_start, slabs + REACH + s, s - (slabs - REACH))
    low_half = lax.broadcasted_iota(jnp.int32, (8, LANES), 0) < 4
    lane = lax.broadcasted_iota(jnp.int32, (16, LANES), 1)

    def place_plane(c):
        for half in range(2):
            got = velocity.at[2 * c + half]
            wait_for(got, recv_c.at[2 * c + half])
            whole = [got[side - REACH : side, :], got[...], got[0 : 8 - REACH, :]]
            padded[c, half] = jnp.concatenate(whole, axis=0).reshape(side // 8 + 1, 8, LANES)

    spots = []
    for slot in range(2 * PLANES):
        centre = s + slot // 2 - REACH
        inside = jnp.logical_and(centre >= 0, centre < slabs)
        column = 4 * lax.rem(centre + slabs, slabs) + 2 * (slot % 2)
        spots.append((jnp.where(inside, 0, slabs), column))

    def cut_for(c, home):
        cut = jnp.zeros((16, LANES), jnp.float32)
        for slot in range(2 * PLANES):
            row, column = home + spots[slot][0], spots[slot][1]
            tile = asked_smem[row, 0, column]
            first = asked_smem[row, 0, column + 1]
            half = first >> 7
            first = first & (LANES - 1)
            near = jnp.concatenate([padded[c, half, tile], padded[c, half, tile + 1]], axis=0)
            far = jnp.concatenate([padded[c, 1 - half, tile], padded[c, 1 - half, tile + 1]], axis=0)
            cells = jnp.where(lane >= first, near, far)
            moved = pltpu.roll(cells, (CELLS * slot + LANES - first) & (LANES - 1), 1)
            taken = jnp.logical_and(lane >= CELLS * slot, lane < CELLS * (slot + 1))
            cut = jnp.where(taken, moved, cut)
        return cut

    def deliver(home, i, tiles):
        part = pl.ds(8 * tiles[0], 8 * len(tiles))

        @pl.when(at_edge)
        def _():
            pltpu.make_async_remote_copy(
                src_ref=message.at[home, part],
                dst_ref=inbox.at[edge_place, part],
                send_sem=edge_m,
                recv_sem=recv_m,
                device_id=(edge_group, home),
                device_id_type=MESH,
            ).start()

        @pl.when(i == 0)
        def _():
            pltpu.make_async_copy(message.at[home, part], inbox.at[REACH + s, part], recv_m).start()

        @pl.when(i > 0)
        def _():
            pltpu.make_async_remote_copy(
                src_ref=message.at[home, part],
                dst_ref=inbox.at[REACH + s, part],
                send_sem=send_m,
                recv_sem=recv_m,
                device_id=(g, home),
                device_id_type=MESH,
            ).start()

    def serve_first(i, carry):
        home = nearby(s, i, slabs)
        cut = cut_for(0, home)
        message[home, 0:8, :] = cut[0:8]
        message[home, 16:24, :] = cut[8:16]
        return carry

    def serve_second(i, carry):
        home = nearby(s, i, slabs)
        cut = cut_for(1, home)
        message[home, 8:16, :] = cut[0:8]
        message[home, 16:24, :] = jnp.where(low_half, message[home, 16:24, :], pltpu.roll(cut[8:16], 4, 0))
        deliver(home, i, (0, 1, 2))
        return carry

    def serve_third(i, carry):
        home = nearby(s, i, slabs)
        message[home, 24:40, :] = cut_for(2, home)
        deliver(home, i, (3, 4))
        return carry

    parts = 2 * components

    def spread(k):
        wait_for(rows_in.at[k], recv_a.at[k])
        if k + 2 < parts:
            send_rows(k + 2)
        along_slab(k)

    def gather(k):
        wait_for(ring_in.at[k], recv_b.at[k])
        if k + 2 < parts:
            send_ring(k + 2)
        along_ring(k)

    spread(0)
    send_ring(0)
    spread(1)
    send_ring(1)

    @pl.when(at_edge)
    def _():
        wait_for(asked_ref, recv_q)
        pltpu.sync_copy(asked_ref, asked_smem)

    @pl.when(jnp.logical_not(at_edge))
    def _():
        wait_for(asked_ref.at[pl.ds(0, slabs)], recv_q)
        pltpu.sync_copy(asked_ref.at[pl.ds(0, slabs)], asked_smem.at[pl.ds(0, slabs)])

    for k in range(2, parts):
        spread(k)
        gather(k - 2)
    place_plane(0)
    lax.fori_loop(0, slabs, serve_first, 0)
    gather(parts - 2)
    gather(parts - 1)
    place_plane(1)
    lax.fori_loop(0, slabs, serve_second, 0)
    place_plane(2)
    lax.fori_loop(0, slabs, serve_third, 0)
    wait_for(inbox, recv_m)

    wait_for(inbox.at[pl.ds(0, slabs - 1)], send_m)

    @pl.when(at_edge)
    def _():
        wait_for(inbox.at[pl.ds(0, slabs)], edge_m)

    wait_for(asked_ref.at[pl.ds(0, slabs - 1 + 2 * REACH)], send_q)

    holds_own = lax.div(s, share) == g

    def drain(c, carry):
        wait_for(rows_in.at[c, pl.ds(0, slabs - 1)], send_a.at[c])
        wait_for(ring_in.at[c, pl.ds(0, groups - 1)], send_b.at[c])

        @pl.when(holds_own)
        def _():
            wait_for(velocity.at[c, pl.ds(0, side - rows)], send_c.at[c])

        @pl.when(jnp.logical_not(holds_own))
        def _():
            wait_for(velocity.at[c], send_c.at[c])

        return carry

    lax.fori_loop(0, 2 * components, drain, 0)


def synthesize(source, tiles, spectrum, groups, slabs):
    components, side = spectrum.shape[1], spectrum.shape[3]
    rows, share, parts = side // slabs, slabs // groups, components * side // LANES
    ids = np.arange(side)
    angle = 2.0 * np.pi / side * (ids[:, None] * ids[None, :] % side)
    tables = jnp.stack(split_table(np.cos(angle)) + split_table(np.sin(angle)))
    count = groups * slabs
    twist = 2.0 * np.pi / count * (bit_reversed(groups)[:, None] * np.arange(slabs)[None, :])
    scale = 1.0 / math.sqrt(side * side * count)
    twiddle = np.stack([np.cos(twist), np.sin(twist)], axis=-1) * scale
    twiddle = jnp.asarray(twiddle.reshape(-1).astype(np.float32))
    vmem, hbm = pl.BlockSpec(memory_space=pltpu.VMEM), pl.BlockSpec(memory_space=pltpu.HBM)
    f32 = jnp.float32
    return pl.pallas_call(
        functools.partial(transform_kernel, groups, slabs),
        out_shape=jax.ShapeDtypeStruct((slabs + 2 * REACH, ROWS_OUT, LANES), f32),
        in_specs=[vmem, vmem, hbm, hbm, pl.BlockSpec(memory_space=pltpu.SMEM)],
        out_specs=vmem,
        scratch_shapes=[
            pltpu.VMEM((1, LANES), jnp.int32),
            pltpu.VMEM((2, components, side, side), f32),
            pltpu.VMEM((4, side, side), jnp.bfloat16),
            pltpu.VMEM((2 * slabs, 1, LANES), jnp.int32),
            pltpu.SMEM((2 * slabs, 1, LANES), jnp.int32),
            pltpu.VMEM((components, 2, side // 8 + 1, 8, LANES), f32),
            pltpu.VMEM((slabs, ROWS_OUT, LANES), f32),
            pltpu.VMEM((parts, 2, side, LANES), f32),
            pltpu.VMEM((parts, slabs, 2, rows, LANES), f32),
            pltpu.VMEM((parts, slabs, 2, rows, LANES), f32),
            pltpu.VMEM((parts, groups, share, 2, rows, LANES), f32),
            pltpu.VMEM((parts, groups, share, rows, LANES), f32),
            pltpu.VMEM((parts, side, LANES), f32),
        ]
        + [pltpu.SemaphoreType.DMA((parts,))] * 6
        + [pltpu.SemaphoreType.DMA] * 2
        + [pltpu.SemaphoreType.DMA((components,))]
        + [pltpu.SemaphoreType.DMA] * 4,
        compiler_params=pltpu.CompilerParams(
            collective_id=0, has_side_effects=True, vmem_limit_bytes=62 * 2**20
        ),
        cost_estimate=pl.CostEstimate(flops=2_500_000_000, bytes_accessed=100_000_000, transcendentals=0),
    )(source, tiles, spectrum[:, :, 0], tables, twiddle)


def interpolate_kernel(inbox, source_ref, fraction_ref, offset_ref, out_ref, weights, named):
    blocks, markers = fraction_ref.shape[1], fraction_ref.shape[2]
    weights[...] = jnp.zeros_like(weights)
    group = weights.shape[0]
    first_lanes = lax.broadcasted_iota(jnp.int32, (ROWS_OUT * PLANES, LANES), 1) < 16
    row_y = lax.broadcasted_iota(jnp.int32, (16, markers), 0)
    row_x = jnp.where(row_y < 12, row_y, row_y - 4)
    in_low = lax.broadcasted_iota(jnp.int32, (8, markers), 0) < 4

    for k in range(named.shape[0]):
        named[k] = 0

    def one_block(i, weights):
        f = jnp.concatenate([fraction_ref[d, pl.ds(i, 1), :] for d in range(3)], axis=0)
        o = [offset_ref[d, pl.ds(i, 1), :] for d in range(3)]
        root = jnp.sqrt(1.0 + 4.0 * f - 4.0 * f * f)
        low, high = 3.0 - 2.0 * f, 1.0 + 2.0 * f
        taps = ((low - root) * 0.125, (low + root) * 0.125, (high + root) * 0.125, (high - root) * 0.125)
        weight_x = jnp.zeros((16, markers), jnp.float32)
        weight_y = jnp.zeros((16, markers), jnp.float32)
        for e in range(4):
            weight_x = jnp.where(row_x == o[1] + e, taps[e][1:2], weight_x)
            weight_y = jnp.where(row_y == o[2] + e, taps[e][2:3], weight_y)
        y_high, y_low = split(weight_y)
        weights[0:16, :] = y_high
        weights[16:32, :] = y_low
        weights[LANES : LANES + 16, :] = y_high
        near = o[0] == 0
        none = jnp.zeros((1, markers), jnp.float32)
        tap_z = [none] + [tap[0:1] for tap in taps] + [none]
        weight_z = [jnp.where(near, tap_z[j + 1], tap_z[j]) for j in range(PLANES)]
        source = source_ref[0, i]
        slot = named[source]
        named[source] = 1
        cells = []
        for j in range(PLANES):
            place = CELLS * (2 * (PLANES - 1 - j) + slot)
            cells.append(pltpu.roll(inbox[source + j], (2 * LANES - place) & (LANES - 1), 1))
        cells = jnp.concatenate(cells, axis=0)
        cells = jnp.where(first_lanes, cells, pltpu.roll(cells, 16, 1))
        values = dot(jnp.concatenate(split(cells), axis=1), weights[...])
        sums = []
        for t in range(ROWS_OUT // 8):
            total = weight_z[0] * values[8 * t : 8 * t + 8]
            for j in range(1, PLANES):
                total = total + weight_z[j] * values[ROWS_OUT * j + 8 * t : ROWS_OUT * j + 8 * t + 8]
            sums.append(total)
        x_first, x_last = weight_x[0:8], weight_x[8:16]
        mixed, last = sums[2] * x_last, sums[4] * x_last
        tails = (jnp.where(in_low, mixed, 0.0), jnp.where(in_low, 0.0, mixed), jnp.where(in_low, last, 0.0))
        for c in range(3):
            out_ref[c, pl.ds(i, 1), :] = jnp.sum(sums[(0, 1, 3)[c]] * x_first + tails[c], axis=0, keepdims=True)

    def several(i, carry):
        for k in range(group):
            one_block(group * i + k, weights.at[k])
        return carry

    lax.fori_loop(0, blocks // group, several, 0)


def sample(inbox, source, fraction, offsets, slabs):
    vmem, smem = pl.BlockSpec(memory_space=pltpu.VMEM), pl.BlockSpec(memory_space=pltpu.SMEM)
    markers = fraction.shape[2]
    return pl.pallas_call(
        interpolate_kernel,
        out_shape=jax.ShapeDtypeStruct(fraction.shape, jnp.float32),
        in_specs=[vmem, smem, vmem, vmem],
        out_specs=vmem,
        scratch_shapes=[pltpu.VMEM((4, 2 * LANES, markers), jnp.bfloat16), pltpu.SMEM((slabs,), jnp.int32)],
        cost_estimate=pl.CostEstimate(flops=200_000_000, bytes_accessed=1_500_000, transcendentals=25_000),
    )(inbox, source, fraction, offsets)


def local(groups, slabs, spectrum, marker_fraction, marker_offsets, block_source, block_tile):
    source = jnp.transpose(block_source)
    inbox = synthesize(source, jnp.transpose(block_tile), spectrum, groups, slabs)
    fraction, offsets = jnp.transpose(marker_fraction, (1, 0, 2)), jnp.transpose(marker_offsets, (1, 0, 2))
    answer = sample(inbox, source, fraction, offsets, slabs)
    return jnp.transpose(answer, (1, 0, 2))


def solution(mesh):
    groups, slabs = mesh.shape["grp"], mesh.shape["gz"]
    both = ("grp", "gz")
    return jax.shard_map(
        functools.partial(local, groups, slabs),
        mesh=mesh,
        in_specs=(
            P(None, None, both, None, None),
            P(both, None, None),
            P(both, None, None),
            P(both, None),
            P(both, None),
        ),
        out_specs=P(both, None, None),
        check_vma=False,
    )
```

```python
import functools
import math

import jax
import jax.numpy as jnp
import ml_dtypes
import numpy as np
from jax import lax
from jax.experimental import pallas as pl
from jax.experimental.pallas import tpu as pltpu
from jax.sharding import PartitionSpec as P

MESH = pl.DeviceIdType.MESH
REACH = 2
PLANES = 2 * REACH + 1
CELLS = 12
LANES = 128
ROWS_OUT = 40


def bit_reversed(count):
    bits = count.bit_length() - 1
    return np.array([int(format(i, f"0{bits}b")[::-1], 2) if bits else 0 for i in range(count)])


def split_table(values):
    high = values.astype(ml_dtypes.bfloat16)
    low = (values - high.astype(np.float64)).astype(ml_dtypes.bfloat16)
    return jnp.asarray(high), jnp.asarray(low)


def split(x):
    high = x.astype(jnp.bfloat16)
    return high, (x - high.astype(jnp.float32)).astype(jnp.bfloat16)


def dot(a, b):
    return jnp.dot(a, b, preferred_element_type=jnp.float32)


def dot3(a, b):
    return dot(a[0], b[0]) + (dot(a[1], b[0]) + dot(a[0], b[1]))


def turn(re, im, angle_num, angle_den):
    eighth = 8 * angle_num % (8 * angle_den) / angle_den
    if eighth == 0:
        return re, im
    if eighth == 2:
        return -im, re
    cosine, sine = math.cos(math.pi * eighth / 4), math.sin(math.pi * eighth / 4)
    if eighth == 1:
        return (re - im) * cosine, (re + im) * cosine
    if eighth == 3:
        return (re + im) * cosine, (re - im) * sine
    return cosine * re - sine * im, sine * re + cosine * im


def butterflies(items, first_half, position_of, real_at_end=False):
    count = len(items)
    half = 1
    while half < count:
        last = real_at_end and 2 * half == count
        for low in range(count):
            if low // half % 2:
                continue
            high = low + half
            span = half * first_half
            re, im = turn(*items[high], position_of(low) % span, 2 * span)
            first = items[low]
            if last:
                items[low], items[high] = (first[0] + re, None), (first[0] - re, None)
            else:
                items[low] = (first[0] + re, first[1] + im)
                items[high] = (first[0] - re, first[1] - im)
        half *= 2
    return items


def wait_for(ref, semaphore):
    pltpu.make_async_copy(ref, ref, semaphore).wait()


def nearby(me, i, count):
    return lax.rem(me + (2 * lax.rem(i, 2) - 1) * lax.div(i + 1, 2) + count, count)


def transform_kernel(
    groups,
    slabs,
    source_ref,
    tile_ref,
    spec_hbm,
    table_hbm,
    twiddle_ref,
    inbox,
    asking_ref,
    spec_ref,
    table,
    asked_ref,
    asked_smem,
    padded,
    message,
    plane_t,
    rows_in,
    rows_z,
    ring_in,
    real_z,
    velocity,
    send_a,
    recv_a,
    send_b,
    recv_b,
    send_c,
    recv_c,
    send_q,
    recv_q,
    load_sem,
    table_sem,
    send_m,
    edge_m,
    recv_m,
):
    g = lax.axis_index("grp")
    s = lax.axis_index("gz")
    side = spec_ref.shape[2]
    loads = [pltpu.make_async_copy(table_hbm, table, table_sem)]
    loads += [pltpu.make_async_copy(spec_hbm.at[:, c], spec_ref.at[:, c], load_sem.at[c]) for c in range(spec_ref.shape[1])]
    for load in loads:
        load.start()
    rows = side // slabs
    share = slabs // groups
    components = spec_ref.shape[1]

    below, above = lax.rem(g + groups - 1, groups), lax.rem(g + 1, groups)
    at_start, at_end = s < REACH, s >= slabs - REACH
    at_edge = jnp.logical_or(at_start, at_end)
    edge_group = jnp.where(at_start, below, above)

    barrier = pltpu.get_barrier_semaphore()

    def greet_slab(i, carry):
        pl.semaphore_signal(barrier, inc=1, device_id=(g, lax.rem(s + i, slabs)), device_id_type=MESH)
        return carry

    def greet_edge(i, carry):
        pl.semaphore_signal(barrier, inc=1, device_id=(edge_group, lax.rem(s + i, slabs)), device_id_type=MESH)
        return carry

    def greet_ring(i, carry):
        pl.semaphore_signal(barrier, inc=1, device_id=(lax.rem(g + i, groups), s), device_id_type=MESH)
        return carry

    lax.fori_loop(1, slabs, greet_slab, 0)
    lax.fori_loop(1, groups, greet_ring, 0)

    @pl.when(at_edge)
    def _():
        lax.fori_loop(0, slabs, greet_edge, 0)


    def transform_plane(c):
        pltpu.make_async_copy(spec_hbm.at[:, c], spec_ref.at[:, c], load_sem.at[c]).wait()
        cosine, sine = (table[0], table[1]), (table[2], table[3])
        re, im = split(spec_ref[0, c]), split(spec_ref[1, c])
        row_re = split(dot3(re, cosine) - dot3(im, sine))
        row_im = split(dot3(re, sine) + dot3(im, cosine))
        for part, whole in (
            (0, dot3(cosine, row_re) - dot3(sine, row_im)),
            (1, dot3(sine, row_re) + dot3(cosine, row_im)),
        ):
            for half in range(2):
                plane_t[2 * c + half, part] = whole[:, half * LANES : (half + 1) * LANES]

    def send_rows(c):
        def one(i, carry):
            r = nearby(s, i, slabs)
            pltpu.make_async_remote_copy(
                src_ref=plane_t.at[c, :, pl.ds(pl.multiple_of(r * rows, rows), rows), :],
                dst_ref=rows_in.at[c, s],
                send_sem=send_a.at[c],
                recv_sem=recv_a.at[c],
                device_id=(g, r),
                device_id_type=MESH,
            ).start()
            return carry

        pltpu.make_async_copy(
            plane_t.at[c, :, pl.ds(pl.multiple_of(s * rows, rows), rows), :],
            rows_in.at[c, s],
            recv_a.at[c],
        ).start()
        lax.fori_loop(1, slabs, one, 0)

    def make_requests():
        blocks = source_ref.shape[1]
        down = lax.broadcasted_iota(jnp.int32, (blocks, blocks), 0)
        along = lax.broadcasted_iota(jnp.int32, (blocks, blocks), 1)
        tiles = side // 8
        code = (along[0:1] * tiles + tile_ref[0:1, :]) * tiles + tile_ref[1:2, :]

        def upright(row):
            return jnp.sum(jnp.where(down == along, row.astype(jnp.float32), 0.0), axis=1, keepdims=True)

        spot = lax.broadcasted_iota(jnp.int32, (blocks, LANES), 1)
        named = upright(source_ref[...]) == (spot >> 2).astype(jnp.float32)
        codes = upright(code)
        first = jnp.min(jnp.where(named, codes, float(tiles * tiles * blocks)), axis=0, keepdims=True)
        second = jnp.max(jnp.where(named, codes, 0.0), axis=0, keepdims=True)
        chosen = jnp.where((spot[0:1] & 2) == 0, first, second).astype(jnp.int32)
        across = (chosen & (tiles - 1)) * 8 + side - REACH
        asking_ref[...] = jnp.where((spot[0:1] & 1) == 0, (chosen // tiles) & (tiles - 1), across & (side - 1))

    def ask(place, device):
        pltpu.make_async_remote_copy(
            src_ref=asking_ref,
            dst_ref=asked_ref.at[place],
            send_sem=send_q,
            recv_sem=recv_q,
            device_id=device,
            device_id_type=MESH,
        ).start()

    def ask_slab(i, carry):
        ask(s, (g, nearby(s, i, slabs)))
        return carry

    loads[0].wait()
    transform_plane(0)
    pl.semaphore_wait(barrier, slabs - 1 + groups - 1 + 2 * REACH)
    send_rows(0)
    transform_plane(1)
    send_rows(1)

    inner = min(8, slabs)
    outer = slabs // inner

    def along_slab(c):
        for block in range(outer):
            items = {k: (rows_in[c, inner * block + k, 0], rows_in[c, inner * block + k, 1]) for k in range(inner)}
            items = butterflies(items, 1, lambda k: k)
            for k in range(inner):
                rows_in[c, inner * block + k, 0], rows_in[c, inner * block + k, 1] = items[k]
        for k in range(inner):
            items = {m: (rows_in[c, inner * m + k, 0], rows_in[c, inner * m + k, 1]) for m in range(outer)}
            items = butterflies(items, inner, lambda m, k=k: inner * m + k)
            for m in range(outer):
                w = inner * m + k
                cosine, sine = twiddle_ref[g * 2 * slabs + 2 * w], twiddle_ref[g * 2 * slabs + 2 * w + 1]
                re, im = items[m]
                rows_z[c, w, 0] = cosine * re - sine * im
                rows_z[c, w, 1] = sine * re + cosine * im

    def send_ring(c):
        def one(i, inner_carry):
            to = nearby(g, i, groups)
            pltpu.make_async_remote_copy(
                src_ref=rows_z.at[c, pl.ds(to * share, share)],
                dst_ref=ring_in.at[c, g],
                send_sem=send_b.at[c],
                recv_sem=recv_b.at[c],
                device_id=(to, s),
                device_id_type=MESH,
            ).start()
            return inner_carry

        pltpu.make_async_copy(rows_z.at[c, pl.ds(g * share, share)], ring_in.at[c, g], recv_b.at[c]).start()
        lax.fori_loop(1, groups, one, 0)

    def along_ring(c):
        for k in range(share):
            items = {q: (ring_in[c, q, k, 0], ring_in[c, q, k, 1]) for q in range(groups)}
            items = butterflies(items, 1, lambda q: q, real_at_end=True)
            for u in range(groups):
                real_z[c, u, k] = items[u][0]

        def one(i, inner_carry):
            to = nearby(g, lax.div(i, share), groups)
            k = lax.rem(i, share)
            w = g * share + k
            mine = jnp.logical_and(to == g, w == s)
            place = velocity.at[c, pl.ds(pl.multiple_of(s * rows, rows), rows), :]

            @pl.when(mine)
            def _():
                pltpu.make_async_copy(real_z.at[c, to, k], place, recv_c.at[c]).start()

            @pl.when(jnp.logical_not(mine))
            def _():
                pltpu.make_async_remote_copy(
                    src_ref=real_z.at[c, to, k],
                    dst_ref=place,
                    send_sem=send_c.at[c],
                    recv_sem=recv_c.at[c],
                    device_id=(to, w),
                    device_id_type=MESH,
                ).start()

            return inner_carry

        lax.fori_loop(0, slabs, one, 0)


    edge_place = jnp.where(at_start, slabs + REACH + s, s - (slabs - REACH))
    low_half = lax.broadcasted_iota(jnp.int32, (8, LANES), 0) < 4
    lane = lax.broadcasted_iota(jnp.int32, (16, LANES), 1)

    def place_plane(c):
        for half in range(2):
            got = velocity.at[2 * c + half]
            wait_for(got, recv_c.at[2 * c + half])
            whole = [got[side - REACH : side, :], got[...], got[0 : 8 - REACH, :]]
            padded[c, half] = jnp.concatenate(whole, axis=0).reshape(side // 8 + 1, 8, LANES)

    spots = []
    for slot in range(2 * PLANES):
        centre = s + slot // 2 - REACH
        inside = jnp.logical_and(centre >= 0, centre < slabs)
        column = 4 * lax.rem(centre + slabs, slabs) + 2 * (slot % 2)
        spots.append((jnp.where(inside, 0, slabs), column))

    def cut_for(c, home):
        cut = jnp.zeros((16, LANES), jnp.float32)
        for slot in range(2 * PLANES):
            row, column = home + spots[slot][0], spots[slot][1]
            tile = asked_smem[row, 0, column]
            first = asked_smem[row, 0, column + 1]
            half = first >> 7
            first = first & (LANES - 1)
            near = jnp.concatenate([padded[c, half, tile], padded[c, half, tile + 1]], axis=0)
            far = jnp.concatenate([padded[c, 1 - half, tile], padded[c, 1 - half, tile + 1]], axis=0)
            cells = jnp.where(lane >= first, near, far)
            moved = pltpu.roll(cells, (CELLS * slot + LANES - first) & (LANES - 1), 1)
            taken = jnp.logical_and(lane >= CELLS * slot, lane < CELLS * (slot + 1))
            cut = jnp.where(taken, moved, cut)
        return cut

    def deliver(home, own, tiles):
        part = pl.ds(8 * tiles[0], 8 * len(tiles))

        @pl.when(at_edge)
        def _():
            pltpu.make_async_remote_copy(
                src_ref=message.at[home, part],
                dst_ref=inbox.at[edge_place, part],
                send_sem=edge_m,
                recv_sem=recv_m,
                device_id=(edge_group, home),
                device_id_type=MESH,
            ).start()

        def keep():
            pltpu.make_async_copy(message.at[home, part], inbox.at[REACH + s, part], recv_m).start()

        def give():
            pltpu.make_async_remote_copy(
                src_ref=message.at[home, part],
                dst_ref=inbox.at[REACH + s, part],
                send_sem=send_m,
                recv_sem=recv_m,
                device_id=(g, home),
                device_id_type=MESH,
            ).start()

        if own is None:
            give()
        else:
            pl.when(own)(keep)
            pl.when(jnp.logical_not(own))(give)

    at_once = 4

    def homes_of(i):
        return [nearby(s, at_once * i + k, slabs) for k in range(at_once)]

    def serve_first(i, carry):
        homes = homes_of(i)
        for home, cut in zip(homes, [cut_for(0, home) for home in homes]):
            message[home, 0:8, :] = cut[0:8]
            message[home, 16:24, :] = cut[8:16]
        return carry

    def serve_second(i, carry):
        homes = homes_of(i)
        for home, cut in zip(homes, [cut_for(1, home) for home in homes]):
            message[home, 8:16, :] = cut[0:8]
            message[home, 16:24, :] = jnp.where(low_half, message[home, 16:24, :], pltpu.roll(cut[8:16], 4, 0))
        for k, home in enumerate(homes):
            deliver(home, None if k else i == 0, (0, 1, 2))
        return carry

    def serve_third(i, carry):
        homes = homes_of(i)
        for home, cut in zip(homes, [cut_for(2, home) for home in homes]):
            message[home, 24:40, :] = cut
        for k, home in enumerate(homes):
            deliver(home, None if k else i == 0, (3, 4))
        return carry

    parts = 2 * components

    def spread(k):
        wait_for(rows_in.at[k], recv_a.at[k])
        if k + 2 < parts:
            send_rows(k + 2)
        along_slab(k)

    def gather(k):
        wait_for(ring_in.at[k], recv_b.at[k])
        if k + 2 < parts:
            send_ring(k + 2)
        along_ring(k)

    spread(0)
    send_ring(0)
    make_requests()
    pltpu.make_async_copy(asking_ref, asked_ref.at[s], recv_q).start()
    lax.fori_loop(1, slabs, ask_slab, 0)
    for k in range(REACH):
        ask(slabs + s, (below, slabs - 1 - k))
        ask(slabs + s, (above, k))
    transform_plane(2)
    spread(1)
    send_ring(1)

    for k in range(2, parts):
        spread(k)
        gather(k - 2)
    @pl.when(at_edge)
    def _():
        wait_for(asked_ref, recv_q)
        pltpu.sync_copy(asked_ref, asked_smem)

    @pl.when(jnp.logical_not(at_edge))
    def _():
        wait_for(asked_ref.at[pl.ds(0, slabs)], recv_q)
        pltpu.sync_copy(asked_ref.at[pl.ds(0, slabs)], asked_smem.at[pl.ds(0, slabs)])

    place_plane(0)
    lax.fori_loop(0, slabs // at_once, serve_first, 0)
    gather(parts - 2)
    gather(parts - 1)
    place_plane(1)
    lax.fori_loop(0, slabs // at_once, serve_second, 0)
    place_plane(2)
    lax.fori_loop(0, slabs // at_once, serve_third, 0)
    wait_for(inbox, recv_m)

    wait_for(inbox.at[pl.ds(0, slabs - 1)], send_m)

    @pl.when(at_edge)
    def _():
        wait_for(inbox.at[pl.ds(0, slabs)], edge_m)

    wait_for(asked_ref.at[pl.ds(0, slabs - 1 + 2 * REACH)], send_q)

    holds_own = lax.div(s, share) == g

    def drain(c, carry):
        wait_for(rows_in.at[c, pl.ds(0, slabs - 1)], send_a.at[c])
        wait_for(ring_in.at[c, pl.ds(0, groups - 1)], send_b.at[c])

        @pl.when(holds_own)
        def _():
            wait_for(velocity.at[c, pl.ds(0, side - rows)], send_c.at[c])

        @pl.when(jnp.logical_not(holds_own))
        def _():
            wait_for(velocity.at[c], send_c.at[c])

        return carry

    lax.fori_loop(0, 2 * components, drain, 0)


def synthesize(source, tiles, spectrum, groups, slabs):
    components, side = spectrum.shape[1], spectrum.shape[3]
    rows, share, parts = side // slabs, slabs // groups, components * side // LANES
    ids = np.arange(side)
    angle = 2.0 * np.pi / side * (ids[:, None] * ids[None, :] % side)
    tables = jnp.stack(split_table(np.cos(angle)) + split_table(np.sin(angle)))
    count = groups * slabs
    twist = 2.0 * np.pi / count * (bit_reversed(groups)[:, None] * np.arange(slabs)[None, :])
    scale = 1.0 / math.sqrt(side * side * count)
    twiddle = np.stack([np.cos(twist), np.sin(twist)], axis=-1) * scale
    twiddle = jnp.asarray(twiddle.reshape(-1).astype(np.float32))
    vmem, hbm = pl.BlockSpec(memory_space=pltpu.VMEM), pl.BlockSpec(memory_space=pltpu.HBM)
    f32 = jnp.float32
    return pl.pallas_call(
        functools.partial(transform_kernel, groups, slabs),
        out_shape=jax.ShapeDtypeStruct((slabs + 2 * REACH, ROWS_OUT, LANES), f32),
        in_specs=[vmem, vmem, hbm, hbm, pl.BlockSpec(memory_space=pltpu.SMEM)],
        out_specs=vmem,
        scratch_shapes=[
            pltpu.VMEM((1, LANES), jnp.int32),
            pltpu.VMEM((2, components, side, side), f32),
            pltpu.VMEM((4, side, side), jnp.bfloat16),
            pltpu.VMEM((2 * slabs, 1, LANES), jnp.int32),
            pltpu.SMEM((2 * slabs, 1, LANES), jnp.int32),
            pltpu.VMEM((components, 2, side // 8 + 1, 8, LANES), f32),
            pltpu.VMEM((slabs, ROWS_OUT, LANES), f32),
            pltpu.VMEM((parts, 2, side, LANES), f32),
            pltpu.VMEM((parts, slabs, 2, rows, LANES), f32),
            pltpu.VMEM((parts, slabs, 2, rows, LANES), f32),
            pltpu.VMEM((parts, groups, share, 2, rows, LANES), f32),
            pltpu.VMEM((parts, groups, share, rows, LANES), f32),
            pltpu.VMEM((parts, side, LANES), f32),
        ]
        + [pltpu.SemaphoreType.DMA((parts,))] * 6
        + [pltpu.SemaphoreType.DMA] * 2
        + [pltpu.SemaphoreType.DMA((components,))]
        + [pltpu.SemaphoreType.DMA] * 4,
        compiler_params=pltpu.CompilerParams(
            collective_id=0, has_side_effects=True, vmem_limit_bytes=62 * 2**20
        ),
        cost_estimate=pl.CostEstimate(flops=2_500_000_000, bytes_accessed=100_000_000, transcendentals=0),
    )(source, tiles, spectrum[:, :, 0], tables, twiddle)


def interpolate_kernel(inbox, source_ref, fraction_ref, offset_ref, out_ref, weights, named):
    blocks, markers = fraction_ref.shape[1], fraction_ref.shape[2]
    weights[...] = jnp.zeros_like(weights)
    group = weights.shape[0]
    first_lanes = lax.broadcasted_iota(jnp.int32, (ROWS_OUT * PLANES, LANES), 1) < 16
    row_y = lax.broadcasted_iota(jnp.int32, (16, markers), 0)
    row_x = jnp.where(row_y < 12, row_y, row_y - 4)
    in_low = lax.broadcasted_iota(jnp.int32, (8, markers), 0) < 4

    for k in range(named.shape[0]):
        named[k] = 0

    def one_block(i, weights):
        f = jnp.concatenate([fraction_ref[d, pl.ds(i, 1), :] for d in range(3)], axis=0)
        o = [offset_ref[d, pl.ds(i, 1), :] for d in range(3)]
        root = jnp.sqrt(1.0 + 4.0 * f - 4.0 * f * f)
        low, high = 3.0 - 2.0 * f, 1.0 + 2.0 * f
        taps = ((low - root) * 0.125, (low + root) * 0.125, (high + root) * 0.125, (high - root) * 0.125)
        weight_x = jnp.zeros((16, markers), jnp.float32)
        weight_y = jnp.zeros((16, markers), jnp.float32)
        for e in range(4):
            weight_x = jnp.where(row_x == o[1] + e, taps[e][1:2], weight_x)
            weight_y = jnp.where(row_y == o[2] + e, taps[e][2:3], weight_y)
        y_high, y_low = split(weight_y)
        weights[0:16, :] = y_high
        weights[16:32, :] = y_low
        weights[LANES : LANES + 16, :] = y_high
        near = o[0] == 0
        none = jnp.zeros((1, markers), jnp.float32)
        tap_z = [none] + [tap[0:1] for tap in taps] + [none]
        weight_z = [jnp.where(near, tap_z[j + 1], tap_z[j]) for j in range(PLANES)]
        source = source_ref[0, i]
        slot = named[source]
        named[source] = 1
        cells = []
        for j in range(PLANES):
            place = CELLS * (2 * (PLANES - 1 - j) + slot)
            cells.append(pltpu.roll(inbox[source + j], (2 * LANES - place) & (LANES - 1), 1))
        cells = jnp.concatenate(cells, axis=0)
        cells = jnp.where(first_lanes, cells, pltpu.roll(cells, 16, 1))
        values = dot(jnp.concatenate(split(cells), axis=1), weights[...])
        sums = []
        for t in range(ROWS_OUT // 8):
            total = weight_z[0] * values[8 * t : 8 * t + 8]
            for j in range(1, PLANES):
                total = total + weight_z[j] * values[ROWS_OUT * j + 8 * t : ROWS_OUT * j + 8 * t + 8]
            sums.append(total)
        x_first, x_last = weight_x[0:8], weight_x[8:16]
        mixed, last = sums[2] * x_last, sums[4] * x_last
        tails = (jnp.where(in_low, mixed, 0.0), jnp.where(in_low, 0.0, mixed), jnp.where(in_low, last, 0.0))
        for c in range(3):
            out_ref[c, pl.ds(i, 1), :] = jnp.sum(sums[(0, 1, 3)[c]] * x_first + tails[c], axis=0, keepdims=True)

    def several(i, carry):
        for k in range(group):
            one_block(group * i + k, weights.at[k])
        return carry

    lax.fori_loop(0, blocks // group, several, 0)


def sample(inbox, source, fraction, offsets, slabs):
    vmem, smem = pl.BlockSpec(memory_space=pltpu.VMEM), pl.BlockSpec(memory_space=pltpu.SMEM)
    markers = fraction.shape[2]
    return pl.pallas_call(
        interpolate_kernel,
        out_shape=jax.ShapeDtypeStruct(fraction.shape, jnp.float32),
        in_specs=[vmem, smem, vmem, vmem],
        out_specs=vmem,
        scratch_shapes=[pltpu.VMEM((8, 2 * LANES, markers), jnp.bfloat16), pltpu.SMEM((slabs,), jnp.int32)],
        cost_estimate=pl.CostEstimate(flops=200_000_000, bytes_accessed=1_500_000, transcendentals=25_000),
    )(inbox, source, fraction, offsets)


def local(groups, slabs, spectrum, marker_fraction, marker_offsets, block_source, block_tile):
    source = jnp.transpose(block_source)
    inbox = synthesize(source, jnp.transpose(block_tile), spectrum, groups, slabs)
    fraction, offsets = jnp.transpose(marker_fraction, (1, 0, 2)), jnp.transpose(marker_offsets, (1, 0, 2))
    answer = sample(inbox, source, fraction, offsets, slabs)
    return jnp.transpose(answer, (1, 0, 2))


def solution(mesh):
    groups, slabs = mesh.shape["grp"], mesh.shape["gz"]
    both = ("grp", "gz")
    return jax.shard_map(
        functools.partial(local, groups, slabs),
        mesh=mesh,
        in_specs=(
            P(None, None, both, None, None),
            P(both, None, None),
            P(both, None, None),
            P(both, None),
            P(both, None),
        ),
        out_specs=P(both, None, None),
        check_vma=False,
    )
```

```python
import functools
import math

import jax
import jax.numpy as jnp
import ml_dtypes
import numpy as np
from jax import lax
from jax.experimental import pallas as pl
from jax.experimental.pallas import tpu as pltpu
from jax.sharding import PartitionSpec as P

MESH = pl.DeviceIdType.MESH
REACH = 2
PLANES = 2 * REACH + 1
CELLS = 12
LANES = 128
ROWS_OUT = 40


def bit_reversed(count):
    bits = count.bit_length() - 1
    return np.array([int(format(i, f"0{bits}b")[::-1], 2) if bits else 0 for i in range(count)])


def split_table(values):
    high = values.astype(ml_dtypes.bfloat16)
    low = (values - high.astype(np.float64)).astype(ml_dtypes.bfloat16)
    return jnp.asarray(high), jnp.asarray(low)


def split(x):
    high = x.astype(jnp.bfloat16)
    return high, (x - high.astype(jnp.float32)).astype(jnp.bfloat16)


def dot(a, b):
    return jnp.dot(a, b, preferred_element_type=jnp.float32)


def dot3(a, b):
    return dot(a[0], b[0]) + (dot(a[1], b[0]) + dot(a[0], b[1]))


def turn(re, im, angle_num, angle_den):
    eighth = 8 * angle_num % (8 * angle_den) / angle_den
    if eighth == 0:
        return re, im
    if eighth == 2:
        return -im, re
    cosine, sine = math.cos(math.pi * eighth / 4), math.sin(math.pi * eighth / 4)
    if eighth == 1:
        return (re - im) * cosine, (re + im) * cosine
    if eighth == 3:
        return (re + im) * cosine, (re - im) * sine
    return cosine * re - sine * im, sine * re + cosine * im


def butterflies(items, first_half, position_of, real_at_end=False):
    count = len(items)
    half = 1
    while half < count:
        last = real_at_end and 2 * half == count
        for low in range(count):
            if low // half % 2:
                continue
            high = low + half
            span = half * first_half
            re, im = turn(*items[high], position_of(low) % span, 2 * span)
            first = items[low]
            if last:
                items[low], items[high] = (first[0] + re, None), (first[0] - re, None)
            else:
                items[low] = (first[0] + re, first[1] + im)
                items[high] = (first[0] - re, first[1] - im)
        half *= 2
    return items


def wait_for(ref, semaphore):
    pltpu.make_async_copy(ref, ref, semaphore).wait()


def nearby(me, i, count):
    return lax.rem(me + (2 * lax.rem(i, 2) - 1) * lax.div(i + 1, 2) + count, count)


def transform_kernel(
    groups,
    slabs,
    source_ref,
    tile_ref,
    spec_hbm,
    table_hbm,
    twiddle_ref,
    inbox,
    asking_ref,
    spec_ref,
    table,
    asked_ref,
    asked_smem,
    padded,
    message,
    plane_t,
    rows_in,
    rows_z,
    ring_in,
    real_z,
    velocity,
    send_a,
    recv_a,
    send_b,
    recv_b,
    send_c,
    recv_c,
    send_q,
    recv_q,
    load_sem,
    table_sem,
    send_m,
    edge_m,
    recv_m,
):
    g = lax.axis_index("grp")
    s = lax.axis_index("gz")
    side = spec_ref.shape[2]
    loads = [pltpu.make_async_copy(table_hbm, table, table_sem)]
    loads += [pltpu.make_async_copy(spec_hbm.at[:, c], spec_ref.at[:, c], load_sem.at[c]) for c in range(spec_ref.shape[1])]
    for load in loads:
        load.start()
    rows = side // slabs
    share = slabs // groups
    components = spec_ref.shape[1]

    below, above = lax.rem(g + groups - 1, groups), lax.rem(g + 1, groups)
    at_start, at_end = s < REACH, s >= slabs - REACH
    at_edge = jnp.logical_or(at_start, at_end)
    edge_group = jnp.where(at_start, below, above)

    barrier = pltpu.get_barrier_semaphore()

    def greet_slab(i, carry):
        pl.semaphore_signal(barrier, inc=1, device_id=(g, lax.rem(s + i, slabs)), device_id_type=MESH)
        return carry

    def greet_edge(i, carry):
        pl.semaphore_signal(barrier, inc=1, device_id=(edge_group, lax.rem(s + i, slabs)), device_id_type=MESH)
        return carry

    def greet_ring(i, carry):
        pl.semaphore_signal(barrier, inc=1, device_id=(lax.rem(g + i, groups), s), device_id_type=MESH)
        return carry

    lax.fori_loop(1, slabs, greet_slab, 0)
    lax.fori_loop(1, groups, greet_ring, 0)

    @pl.when(at_edge)
    def _():
        lax.fori_loop(0, slabs, greet_edge, 0)


    def transform_plane(c):
        pltpu.make_async_copy(spec_hbm.at[:, c], spec_ref.at[:, c], load_sem.at[c]).wait()
        cosine, sine = (table[0], table[1]), (table[2], table[3])
        re, im = split(spec_ref[0, c]), split(spec_ref[1, c])
        row_re = split(dot3(re, cosine) - dot3(im, sine))
        row_im = split(dot3(re, sine) + dot3(im, cosine))
        for part, whole in (
            (0, dot3(cosine, row_re) - dot3(sine, row_im)),
            (1, dot3(sine, row_re) + dot3(cosine, row_im)),
        ):
            for half in range(2):
                plane_t[2 * c + half, part] = whole[:, half * LANES : (half + 1) * LANES]

    def send_rows(c):
        def one(i, carry):
            r = nearby(s, i, slabs)
            pltpu.make_async_remote_copy(
                src_ref=plane_t.at[c, :, pl.ds(pl.multiple_of(r * rows, rows), rows), :],
                dst_ref=rows_in.at[c, s],
                send_sem=send_a.at[c],
                recv_sem=recv_a.at[c],
                device_id=(g, r),
                device_id_type=MESH,
            ).start()
            return carry

        pltpu.make_async_copy(
            plane_t.at[c, :, pl.ds(pl.multiple_of(s * rows, rows), rows), :],
            rows_in.at[c, s],
            recv_a.at[c],
        ).start()
        lax.fori_loop(1, slabs, one, 0)

    def make_requests():
        blocks = source_ref.shape[1]
        down = lax.broadcasted_iota(jnp.int32, (blocks, blocks), 0)
        along = lax.broadcasted_iota(jnp.int32, (blocks, blocks), 1)
        tiles = side // 8
        code = (along[0:1] * tiles + tile_ref[0:1, :]) * tiles + tile_ref[1:2, :]

        def upright(row):
            return jnp.sum(jnp.where(down == along, row.astype(jnp.float32), 0.0), axis=1, keepdims=True)

        spot = lax.broadcasted_iota(jnp.int32, (blocks, LANES), 1)
        named = upright(source_ref[...]) == (spot >> 2).astype(jnp.float32)
        codes = upright(code)
        first = jnp.min(jnp.where(named, codes, float(tiles * tiles * blocks)), axis=0, keepdims=True)
        second = jnp.max(jnp.where(named, codes, 0.0), axis=0, keepdims=True)
        chosen = jnp.where((spot[0:1] & 2) == 0, first, second).astype(jnp.int32)
        across = (chosen & (tiles - 1)) * 8 + side - REACH
        asking_ref[...] = jnp.where((spot[0:1] & 1) == 0, (chosen // tiles) & (tiles - 1), across & (side - 1))

    def ask(place, device):
        pltpu.make_async_remote_copy(
            src_ref=asking_ref,
            dst_ref=asked_ref.at[place],
            send_sem=send_q,
            recv_sem=recv_q,
            device_id=device,
            device_id_type=MESH,
        ).start()

    def ask_slab(i, carry):
        ask(s, (g, nearby(s, i, slabs)))
        return carry

    loads[0].wait()
    transform_plane(0)
    pl.semaphore_wait(barrier, slabs - 1 + groups - 1 + 2 * REACH)
    send_rows(0)
    transform_plane(1)
    send_rows(1)

    inner = min(8, slabs)
    outer = slabs // inner

    def along_slab(c):
        for block in range(outer):
            items = {k: (rows_in[c, inner * block + k, 0], rows_in[c, inner * block + k, 1]) for k in range(inner)}
            items = butterflies(items, 1, lambda k: k)
            for k in range(inner):
                rows_in[c, inner * block + k, 0], rows_in[c, inner * block + k, 1] = items[k]
        for k in range(inner):
            items = {m: (rows_in[c, inner * m + k, 0], rows_in[c, inner * m + k, 1]) for m in range(outer)}
            items = butterflies(items, inner, lambda m, k=k: inner * m + k)
            for m in range(outer):
                w = inner * m + k
                cosine, sine = twiddle_ref[g * 2 * slabs + 2 * w], twiddle_ref[g * 2 * slabs + 2 * w + 1]
                re, im = items[m]
                rows_z[c, w, 0] = cosine * re - sine * im
                rows_z[c, w, 1] = sine * re + cosine * im

    def send_ring(c):
        def one(i, inner_carry):
            to = nearby(g, i, groups)
            pltpu.make_async_remote_copy(
                src_ref=rows_z.at[c, pl.ds(to * share, share)],
                dst_ref=ring_in.at[c, g],
                send_sem=send_b.at[c],
                recv_sem=recv_b.at[c],
                device_id=(to, s),
                device_id_type=MESH,
            ).start()
            return inner_carry

        pltpu.make_async_copy(rows_z.at[c, pl.ds(g * share, share)], ring_in.at[c, g], recv_b.at[c]).start()
        lax.fori_loop(1, groups, one, 0)

    def along_ring(c):
        for k in range(share):
            items = {q: (ring_in[c, q, k, 0], ring_in[c, q, k, 1]) for q in range(groups)}
            items = butterflies(items, 1, lambda q: q, real_at_end=True)
            for u in range(groups):
                real_z[c, u, k] = items[u][0]

        def one(i, inner_carry):
            to = nearby(g, lax.div(i, share), groups)
            k = lax.rem(i, share)
            w = g * share + k
            mine = jnp.logical_and(to == g, w == s)
            place = velocity.at[c, pl.ds(pl.multiple_of(s * rows, rows), rows), :]

            @pl.when(mine)
            def _():
                pltpu.make_async_copy(real_z.at[c, to, k], place, recv_c.at[c]).start()

            @pl.when(jnp.logical_not(mine))
            def _():
                pltpu.make_async_remote_copy(
                    src_ref=real_z.at[c, to, k],
                    dst_ref=place,
                    send_sem=send_c.at[c],
                    recv_sem=recv_c.at[c],
                    device_id=(to, w),
                    device_id_type=MESH,
                ).start()

            return inner_carry

        lax.fori_loop(0, slabs, one, 0)


    edge_place = jnp.where(at_start, slabs + REACH + s, s - (slabs - REACH))
    low_half = lax.broadcasted_iota(jnp.int32, (8, LANES), 0) < 4
    lane = lax.broadcasted_iota(jnp.int32, (16, LANES), 1)

    def place_plane(c):
        for half in range(2):
            got = velocity.at[2 * c + half]
            wait_for(got, recv_c.at[2 * c + half])
            whole = [got[side - REACH : side, :], got[...], got[0 : 8 - REACH, :]]
            padded[c, half] = jnp.concatenate(whole, axis=0).reshape(side // 8 + 1, 8, LANES)

    spots = []
    for slot in range(2 * PLANES):
        centre = s + slot // 2 - REACH
        inside = jnp.logical_and(centre >= 0, centre < slabs)
        column = 4 * lax.rem(centre + slabs, slabs) + 2 * (slot % 2)
        spots.append((jnp.where(inside, 0, slabs), column))

    def cut_for(c, home):
        cut = jnp.zeros((16, LANES), jnp.float32)
        for slot in range(2 * PLANES):
            row, column = home + spots[slot][0], spots[slot][1]
            tile = asked_smem[row, 0, column]
            first = asked_smem[row, 0, column + 1]
            half = first >> 7
            first = first & (LANES - 1)
            near = jnp.concatenate([padded[c, half, tile], padded[c, half, tile + 1]], axis=0)
            far = jnp.concatenate([padded[c, 1 - half, tile], padded[c, 1 - half, tile + 1]], axis=0)
            cells = jnp.where(lane >= first, near, far)
            moved = pltpu.roll(cells, (CELLS * slot + LANES - first) & (LANES - 1), 1)
            taken = jnp.logical_and(lane >= CELLS * slot, lane < CELLS * (slot + 1))
            cut = jnp.where(taken, moved, cut)
        return cut

    def deliver(home, own, tiles):
        part = pl.ds(8 * tiles[0], 8 * len(tiles))

        @pl.when(at_edge)
        def _():
            pltpu.make_async_remote_copy(
                src_ref=message.at[home, part],
                dst_ref=inbox.at[edge_place, part],
                send_sem=edge_m,
                recv_sem=recv_m,
                device_id=(edge_group, home),
                device_id_type=MESH,
            ).start()

        def keep():
            pltpu.make_async_copy(message.at[home, part], inbox.at[REACH + s, part], recv_m).start()

        def give():
            pltpu.make_async_remote_copy(
                src_ref=message.at[home, part],
                dst_ref=inbox.at[REACH + s, part],
                send_sem=send_m,
                recv_sem=recv_m,
                device_id=(g, home),
                device_id_type=MESH,
            ).start()

        if own is None:
            give()
        else:
            pl.when(own)(keep)
            pl.when(jnp.logical_not(own))(give)

    at_once = 4

    def homes_of(i):
        return [nearby(s, at_once * i + k, slabs) for k in range(at_once)]

    def serve_first(i, carry):
        homes = homes_of(i)
        for home, cut in zip(homes, [cut_for(0, home) for home in homes]):
            message[home, 0:8, :] = cut[0:8]
            message[home, 16:24, :] = cut[8:16]
        return carry

    def serve_second(i, carry):
        homes = homes_of(i)
        for home, cut in zip(homes, [cut_for(1, home) for home in homes]):
            message[home, 8:16, :] = cut[0:8]
            message[home, 16:24, :] = jnp.where(low_half, message[home, 16:24, :], pltpu.roll(cut[8:16], 4, 0))
        for k, home in enumerate(homes):
            deliver(home, None if k else i == 0, (0, 1, 2))
        return carry

    def serve_third(i, carry):
        homes = homes_of(i)
        for home, cut in zip(homes, [cut_for(2, home) for home in homes]):
            message[home, 24:40, :] = cut
        for k, home in enumerate(homes):
            deliver(home, None if k else i == 0, (3, 4))
        return carry

    parts = 2 * components

    def spread(k):
        wait_for(rows_in.at[k], recv_a.at[k])
        if k + 2 < parts:
            send_rows(k + 2)
        along_slab(k)
        send_ring(k)

    def gather(k):
        wait_for(ring_in.at[k], recv_b.at[k])
        along_ring(k)

    spread(0)
    spread(1)
    transform_plane(2)
    make_requests()
    pltpu.make_async_copy(asking_ref, asked_ref.at[s], recv_q).start()
    lax.fori_loop(1, slabs, ask_slab, 0)
    for k in range(REACH):
        ask(slabs + s, (below, slabs - 1 - k))
        ask(slabs + s, (above, k))

    for k in range(2, parts):
        spread(k)
        gather(k - 2)
    @pl.when(at_edge)
    def _():
        wait_for(asked_ref, recv_q)
        pltpu.sync_copy(asked_ref, asked_smem)

    @pl.when(jnp.logical_not(at_edge))
    def _():
        wait_for(asked_ref.at[pl.ds(0, slabs)], recv_q)
        pltpu.sync_copy(asked_ref.at[pl.ds(0, slabs)], asked_smem.at[pl.ds(0, slabs)])

    place_plane(0)
    lax.fori_loop(0, slabs // at_once, serve_first, 0)
    gather(parts - 2)
    gather(parts - 1)
    place_plane(1)
    lax.fori_loop(0, slabs // at_once, serve_second, 0)
    place_plane(2)
    lax.fori_loop(0, slabs // at_once, serve_third, 0)
    wait_for(inbox, recv_m)

    wait_for(inbox.at[pl.ds(0, slabs - 1)], send_m)

    @pl.when(at_edge)
    def _():
        wait_for(inbox.at[pl.ds(0, slabs)], edge_m)

    wait_for(asked_ref.at[pl.ds(0, slabs - 1 + 2 * REACH)], send_q)

    holds_own = lax.div(s, share) == g

    def drain(c, carry):
        wait_for(rows_in.at[c, pl.ds(0, slabs - 1)], send_a.at[c])
        wait_for(ring_in.at[c, pl.ds(0, groups - 1)], send_b.at[c])

        @pl.when(holds_own)
        def _():
            wait_for(velocity.at[c, pl.ds(0, side - rows)], send_c.at[c])

        @pl.when(jnp.logical_not(holds_own))
        def _():
            wait_for(velocity.at[c], send_c.at[c])

        return carry

    lax.fori_loop(0, 2 * components, drain, 0)


def synthesize(source, tiles, spectrum, groups, slabs):
    components, side = spectrum.shape[1], spectrum.shape[3]
    rows, share, parts = side // slabs, slabs // groups, components * side // LANES
    ids = np.arange(side)
    angle = 2.0 * np.pi / side * (ids[:, None] * ids[None, :] % side)
    tables = jnp.stack(split_table(np.cos(angle)) + split_table(np.sin(angle)))
    count = groups * slabs
    twist = 2.0 * np.pi / count * (bit_reversed(groups)[:, None] * np.arange(slabs)[None, :])
    scale = 1.0 / math.sqrt(side * side * count)
    twiddle = np.stack([np.cos(twist), np.sin(twist)], axis=-1) * scale
    twiddle = jnp.asarray(twiddle.reshape(-1).astype(np.float32))
    vmem, hbm = pl.BlockSpec(memory_space=pltpu.VMEM), pl.BlockSpec(memory_space=pltpu.HBM)
    f32 = jnp.float32
    return pl.pallas_call(
        functools.partial(transform_kernel, groups, slabs),
        out_shape=jax.ShapeDtypeStruct((slabs + 2 * REACH, ROWS_OUT, LANES), f32),
        in_specs=[vmem, vmem, hbm, hbm, pl.BlockSpec(memory_space=pltpu.SMEM)],
        out_specs=vmem,
        scratch_shapes=[
            pltpu.VMEM((1, LANES), jnp.int32),
            pltpu.VMEM((2, components, side, side), f32),
            pltpu.VMEM((4, side, side), jnp.bfloat16),
            pltpu.VMEM((2 * slabs, 1, LANES), jnp.int32),
            pltpu.SMEM((2 * slabs, 1, LANES), jnp.int32),
            pltpu.VMEM((components, 2, side // 8 + 1, 8, LANES), f32),
            pltpu.VMEM((slabs, ROWS_OUT, LANES), f32),
            pltpu.VMEM((parts, 2, side, LANES), f32),
            pltpu.VMEM((parts, slabs, 2, rows, LANES), f32),
            pltpu.VMEM((parts, slabs, 2, rows, LANES), f32),
            pltpu.VMEM((parts, groups, share, 2, rows, LANES), f32),
            pltpu.VMEM((parts, groups, share, rows, LANES), f32),
            pltpu.VMEM((parts, side, LANES), f32),
        ]
        + [pltpu.SemaphoreType.DMA((parts,))] * 6
        + [pltpu.SemaphoreType.DMA] * 2
        + [pltpu.SemaphoreType.DMA((components,))]
        + [pltpu.SemaphoreType.DMA] * 4,
        compiler_params=pltpu.CompilerParams(
            collective_id=0, has_side_effects=True, vmem_limit_bytes=62 * 2**20
        ),
        cost_estimate=pl.CostEstimate(flops=2_500_000_000, bytes_accessed=100_000_000, transcendentals=0),
    )(source, tiles, spectrum[:, :, 0], tables, twiddle)


def interpolate_kernel(inbox, source_ref, fraction_ref, offset_ref, out_ref, weights, named):
    blocks, markers = fraction_ref.shape[1], fraction_ref.shape[2]
    weights[...] = jnp.zeros_like(weights)
    group = weights.shape[0]
    first_lanes = lax.broadcasted_iota(jnp.int32, (ROWS_OUT * PLANES, LANES), 1) < 16
    row_y = lax.broadcasted_iota(jnp.int32, (16, markers), 0)
    row_x = jnp.where(row_y < 12, row_y, row_y - 4)
    in_low = lax.broadcasted_iota(jnp.int32, (8, markers), 0) < 4

    for k in range(named.shape[0]):
        named[k] = 0

    def one_block(i, weights):
        f = jnp.concatenate([fraction_ref[d, pl.ds(i, 1), :] for d in range(3)], axis=0)
        o = [offset_ref[d, pl.ds(i, 1), :] for d in range(3)]
        root = jnp.sqrt(1.0 + 4.0 * f - 4.0 * f * f)
        low, high = 3.0 - 2.0 * f, 1.0 + 2.0 * f
        taps = ((low - root) * 0.125, (low + root) * 0.125, (high + root) * 0.125, (high - root) * 0.125)
        weight_x = jnp.zeros((16, markers), jnp.float32)
        weight_y = jnp.zeros((16, markers), jnp.float32)
        for e in range(4):
            weight_x = jnp.where(row_x == o[1] + e, taps[e][1:2], weight_x)
            weight_y = jnp.where(row_y == o[2] + e, taps[e][2:3], weight_y)
        y_high, y_low = split(weight_y)
        weights[0:16, :] = y_high
        weights[16:32, :] = y_low
        weights[LANES : LANES + 16, :] = y_high
        near = o[0] == 0
        none = jnp.zeros((1, markers), jnp.float32)
        tap_z = [none] + [tap[0:1] for tap in taps] + [none]
        weight_z = [jnp.where(near, tap_z[j + 1], tap_z[j]) for j in range(PLANES)]
        source = source_ref[0, i]
        slot = named[source]
        named[source] = 1
        cells = []
        for j in range(PLANES):
            place = CELLS * (2 * (PLANES - 1 - j) + slot)
            cells.append(pltpu.roll(inbox[source + j], (2 * LANES - place) & (LANES - 1), 1))
        cells = jnp.concatenate(cells, axis=0)
        cells = jnp.where(first_lanes, cells, pltpu.roll(cells, 16, 1))
        values = dot(jnp.concatenate(split(cells), axis=1), weights[...])
        sums = []
        for t in range(ROWS_OUT // 8):
            total = weight_z[0] * values[8 * t : 8 * t + 8]
            for j in range(1, PLANES):
                total = total + weight_z[j] * values[ROWS_OUT * j + 8 * t : ROWS_OUT * j + 8 * t + 8]
            sums.append(total)
        x_first, x_last = weight_x[0:8], weight_x[8:16]
        mixed, last = sums[2] * x_last, sums[4] * x_last
        tails = (jnp.where(in_low, mixed, 0.0), jnp.where(in_low, 0.0, mixed), jnp.where(in_low, last, 0.0))
        for c in range(3):
            out_ref[c, pl.ds(i, 1), :] = jnp.sum(sums[(0, 1, 3)[c]] * x_first + tails[c], axis=0, keepdims=True)

    def several(i, carry):
        for k in range(group):
            one_block(group * i + k, weights.at[k])
        return carry

    lax.fori_loop(0, blocks // group, several, 0)


def sample(inbox, source, fraction, offsets, slabs):
    vmem, smem = pl.BlockSpec(memory_space=pltpu.VMEM), pl.BlockSpec(memory_space=pltpu.SMEM)
    markers = fraction.shape[2]
    return pl.pallas_call(
        interpolate_kernel,
        out_shape=jax.ShapeDtypeStruct(fraction.shape, jnp.float32),
        in_specs=[vmem, smem, vmem, vmem],
        out_specs=vmem,
        scratch_shapes=[pltpu.VMEM((8, 2 * LANES, markers), jnp.bfloat16), pltpu.SMEM((slabs,), jnp.int32)],
        cost_estimate=pl.CostEstimate(flops=200_000_000, bytes_accessed=1_500_000, transcendentals=25_000),
    )(inbox, source, fraction, offsets)


def local(groups, slabs, spectrum, marker_fraction, marker_offsets, block_source, block_tile):
    source = jnp.transpose(block_source)
    inbox = synthesize(source, jnp.transpose(block_tile), spectrum, groups, slabs)
    fraction, offsets = jnp.transpose(marker_fraction, (1, 0, 2)), jnp.transpose(marker_offsets, (1, 0, 2))
    answer = sample(inbox, source, fraction, offsets, slabs)
    return jnp.transpose(answer, (1, 0, 2))


def solution(mesh):
    groups, slabs = mesh.shape["grp"], mesh.shape["gz"]
    both = ("grp", "gz")
    return jax.shard_map(
        functools.partial(local, groups, slabs),
        mesh=mesh,
        in_specs=(
            P(None, None, both, None, None),
            P(both, None, None),
            P(both, None, None),
            P(both, None),
            P(both, None),
        ),
        out_specs=P(both, None, None),
        check_vma=False,
    )
```

```python
import functools
import math

import jax
import jax.numpy as jnp
import ml_dtypes
import numpy as np
from jax import lax
from jax.experimental import pallas as pl
from jax.experimental.pallas import tpu as pltpu
from jax.sharding import PartitionSpec as P

MESH = pl.DeviceIdType.MESH
REACH = 2
PLANES = 2 * REACH + 1
CELLS = 12
LANES = 128
ROWS_OUT = 40


def bit_reversed(count):
    bits = count.bit_length() - 1
    return np.array([int(format(i, f"0{bits}b")[::-1], 2) if bits else 0 for i in range(count)])


def split_table(values):
    high = values.astype(ml_dtypes.bfloat16)
    low = (values - high.astype(np.float64)).astype(ml_dtypes.bfloat16)
    return jnp.asarray(high), jnp.asarray(low)


def split(x):
    high = x.astype(jnp.bfloat16)
    return high, (x - high.astype(jnp.float32)).astype(jnp.bfloat16)


def dot(a, b):
    return jnp.dot(a, b, preferred_element_type=jnp.float32)


def dot3(a, b):
    return dot(a[0], b[0]) + (dot(a[1], b[0]) + dot(a[0], b[1]))


def turn(re, im, angle_num, angle_den):
    eighth = 8 * angle_num % (8 * angle_den) / angle_den
    if eighth == 0:
        return re, im
    if eighth == 2:
        return -im, re
    cosine, sine = math.cos(math.pi * eighth / 4), math.sin(math.pi * eighth / 4)
    if eighth == 1:
        return (re - im) * cosine, (re + im) * cosine
    if eighth == 3:
        return (re + im) * cosine, (re - im) * sine
    return cosine * re - sine * im, sine * re + cosine * im


def butterflies(items, first_half, position_of, real_at_end=False):
    count = len(items)
    half = 1
    while half < count:
        last = real_at_end and 2 * half == count
        for low in range(count):
            if low // half % 2:
                continue
            high = low + half
            span = half * first_half
            re, im = turn(*items[high], position_of(low) % span, 2 * span)
            first = items[low]
            if last:
                items[low], items[high] = (first[0] + re, None), (first[0] - re, None)
            else:
                items[low] = (first[0] + re, first[1] + im)
                items[high] = (first[0] - re, first[1] - im)
        half *= 2
    return items


def wait_for(ref, semaphore):
    pltpu.make_async_copy(ref, ref, semaphore).wait()


def nearby(me, i, count):
    return lax.rem(me + (2 * lax.rem(i, 2) - 1) * lax.div(i + 1, 2) + count, count)


def transform_kernel(
    groups,
    slabs,
    source_ref,
    tile_ref,
    spec_hbm,
    table_hbm,
    twiddle_ref,
    inbox,
    asking_ref,
    spec_ref,
    table,
    asked_ref,
    asked_smem,
    padded,
    message,
    plane_t,
    rows_in,
    rows_z,
    ring_in,
    real_z,
    velocity,
    send_a,
    recv_a,
    send_b,
    recv_b,
    send_c,
    recv_c,
    send_q,
    recv_q,
    load_sem,
    table_sem,
    send_m,
    edge_m,
    recv_m,
    send_e,
    recv_e,
):
    g = lax.axis_index("grp")
    s = lax.axis_index("gz")
    side = spec_ref.shape[2]
    loads = [pltpu.make_async_copy(table_hbm, table, table_sem)]
    loads += [pltpu.make_async_copy(spec_hbm.at[:, c], spec_ref.at[:, c], load_sem.at[c]) for c in range(spec_ref.shape[1])]
    for load in loads:
        load.start()
    rows = side // slabs
    share = slabs // groups
    components = spec_ref.shape[1]

    below, above = lax.rem(g + groups - 1, groups), lax.rem(g + 1, groups)
    at_start, at_end = s < REACH, s >= slabs - REACH
    at_edge = jnp.logical_or(at_start, at_end)
    edge_group = jnp.where(at_start, below, above)

    barrier = pltpu.get_barrier_semaphore()

    def greet_slab(i, carry):
        pl.semaphore_signal(barrier, inc=1, device_id=(g, lax.rem(s + i, slabs)), device_id_type=MESH)
        return carry

    def greet_ring(i, carry):
        pl.semaphore_signal(barrier, inc=1, device_id=(lax.rem(g + i, groups), s), device_id_type=MESH)
        return carry

    lax.fori_loop(1, slabs, greet_slab, 0)
    lax.fori_loop(1, groups, greet_ring, 0)

    def transform_plane(c):
        pltpu.make_async_copy(spec_hbm.at[:, c], spec_ref.at[:, c], load_sem.at[c]).wait()
        cosine, sine = (table[0], table[1]), (table[2], table[3])
        re, im = split(spec_ref[0, c]), split(spec_ref[1, c])
        row_re = split(dot3(re, cosine) - dot3(im, sine))
        row_im = split(dot3(re, sine) + dot3(im, cosine))
        for part, whole in (
            (0, dot3(cosine, row_re) - dot3(sine, row_im)),
            (1, dot3(sine, row_re) + dot3(cosine, row_im)),
        ):
            for half in range(2):
                plane_t[2 * c + half, part] = whole[:, half * LANES : (half + 1) * LANES]

    def send_rows(c):
        def one(i, carry):
            r = nearby(s, i, slabs)
            pltpu.make_async_remote_copy(
                src_ref=plane_t.at[c, :, pl.ds(pl.multiple_of(r * rows, rows), rows), :],
                dst_ref=rows_in.at[c, s],
                send_sem=send_a.at[c],
                recv_sem=recv_a.at[c],
                device_id=(g, r),
                device_id_type=MESH,
            ).start()
            return carry

        pltpu.make_async_copy(
            plane_t.at[c, :, pl.ds(pl.multiple_of(s * rows, rows), rows), :],
            rows_in.at[c, s],
            recv_a.at[c],
        ).start()
        lax.fori_loop(1, slabs, one, 0)

    def make_requests():
        blocks = source_ref.shape[1]
        down = lax.broadcasted_iota(jnp.int32, (blocks, blocks), 0)
        along = lax.broadcasted_iota(jnp.int32, (blocks, blocks), 1)
        tiles = side // 8
        code = (along[0:1] * tiles + tile_ref[0:1, :]) * tiles + tile_ref[1:2, :]

        def upright(row):
            return jnp.sum(jnp.where(down == along, row.astype(jnp.float32), 0.0), axis=1, keepdims=True)

        spot = lax.broadcasted_iota(jnp.int32, (blocks, LANES), 1)
        named = upright(source_ref[...]) == (spot >> 2).astype(jnp.float32)
        codes = upright(code)
        first = jnp.min(jnp.where(named, codes, float(tiles * tiles * blocks)), axis=0, keepdims=True)
        second = jnp.max(jnp.where(named, codes, 0.0), axis=0, keepdims=True)
        chosen = jnp.where((spot[0:1] & 2) == 0, first, second).astype(jnp.int32)
        across = (chosen & (tiles - 1)) * 8 + side - REACH
        asking_ref[...] = jnp.where((spot[0:1] & 1) == 0, (chosen // tiles) & (tiles - 1), across & (side - 1))

    def ask(place, device):
        pltpu.make_async_remote_copy(
            src_ref=asking_ref,
            dst_ref=asked_ref.at[place],
            send_sem=send_q,
            recv_sem=recv_q,
            device_id=device,
            device_id_type=MESH,
        ).start()

    def ask_slab(i, carry):
        ask(s, (g, nearby(s, i, slabs)))
        return carry

    loads[0].wait()
    transform_plane(0)
    pl.semaphore_wait(barrier, slabs - 1 + groups - 1)
    send_rows(0)
    transform_plane(1)
    send_rows(1)

    inner = min(8, slabs)
    outer = slabs // inner

    def along_slab(c):
        for block in range(outer):
            items = {k: (rows_in[c, inner * block + k, 0], rows_in[c, inner * block + k, 1]) for k in range(inner)}
            items = butterflies(items, 1, lambda k: k)
            for k in range(inner):
                rows_in[c, inner * block + k, 0], rows_in[c, inner * block + k, 1] = items[k]
        for k in range(inner):
            items = {m: (rows_in[c, inner * m + k, 0], rows_in[c, inner * m + k, 1]) for m in range(outer)}
            items = butterflies(items, inner, lambda m, k=k: inner * m + k)
            for m in range(outer):
                w = inner * m + k
                cosine, sine = twiddle_ref[g * 2 * slabs + 2 * w], twiddle_ref[g * 2 * slabs + 2 * w + 1]
                re, im = items[m]
                rows_z[c, w, 0] = cosine * re - sine * im
                rows_z[c, w, 1] = sine * re + cosine * im

    def send_ring(c):
        def one(i, inner_carry):
            to = nearby(g, i, groups)
            pltpu.make_async_remote_copy(
                src_ref=rows_z.at[c, pl.ds(to * share, share)],
                dst_ref=ring_in.at[c, g],
                send_sem=send_b.at[c],
                recv_sem=recv_b.at[c],
                device_id=(to, s),
                device_id_type=MESH,
            ).start()
            return inner_carry

        pltpu.make_async_copy(rows_z.at[c, pl.ds(g * share, share)], ring_in.at[c, g], recv_b.at[c]).start()
        lax.fori_loop(1, groups, one, 0)

    def along_ring(c):
        for k in range(share):
            items = {q: (ring_in[c, q, k, 0], ring_in[c, q, k, 1]) for q in range(groups)}
            items = butterflies(items, 1, lambda q: q, real_at_end=True)
            for u in range(groups):
                real_z[c, u, k] = items[u][0]

        def one(i, inner_carry):
            to = nearby(g, lax.div(i, share), groups)
            k = lax.rem(i, share)
            w = g * share + k
            mine = jnp.logical_and(to == g, w == s)
            place = velocity.at[c, pl.ds(pl.multiple_of(s * rows, rows), rows), :]

            @pl.when(mine)
            def _():
                pltpu.make_async_copy(real_z.at[c, to, k], place, recv_c.at[c]).start()

            @pl.when(jnp.logical_not(mine))
            def _():
                pltpu.make_async_remote_copy(
                    src_ref=real_z.at[c, to, k],
                    dst_ref=place,
                    send_sem=send_c.at[c],
                    recv_sem=recv_c.at[c],
                    device_id=(to, w),
                    device_id_type=MESH,
                ).start()

            return inner_carry

        lax.fori_loop(0, slabs, one, 0)


    edge_place = jnp.where(at_start, slabs + REACH + s, s - (slabs - REACH))
    low_half = lax.broadcasted_iota(jnp.int32, (8, LANES), 0) < 4
    lane = lax.broadcasted_iota(jnp.int32, (16, LANES), 1)

    def place_plane(c):
        for half in range(2):
            got = velocity.at[2 * c + half]
            wait_for(got, recv_c.at[2 * c + half])
            whole = [got[side - REACH : side, :], got[...], got[0 : 8 - REACH, :]]
            padded[c, half] = jnp.concatenate(whole, axis=0).reshape(side // 8 + 1, 8, LANES)

    spots = []
    for slot in range(2 * PLANES):
        centre = s + slot // 2 - REACH
        inside = jnp.logical_and(centre >= 0, centre < slabs)
        column = 4 * lax.rem(centre + slabs, slabs) + 2 * (slot % 2)
        spots.append((jnp.where(inside, 0, slabs), column))

    def cut_for(c, home):
        cut = jnp.zeros((16, LANES), jnp.float32)
        for slot in range(2 * PLANES):
            row, column = home + spots[slot][0], spots[slot][1]
            tile = asked_smem[row, 0, column]
            first = asked_smem[row, 0, column + 1]
            half = first >> 7
            first = first & (LANES - 1)
            near = jnp.concatenate([padded[c, half, tile], padded[c, half, tile + 1]], axis=0)
            far = jnp.concatenate([padded[c, 1 - half, tile], padded[c, 1 - half, tile + 1]], axis=0)
            cells = jnp.where(lane >= first, near, far)
            moved = pltpu.roll(cells, (CELLS * slot + LANES - first) & (LANES - 1), 1)
            taken = jnp.logical_and(lane >= CELLS * slot, lane < CELLS * (slot + 1))
            cut = jnp.where(taken, moved, cut)
        return cut

    def deliver(home, own, tiles):
        part = pl.ds(8 * tiles[0], 8 * len(tiles))

        @pl.when(at_edge)
        def _():
            pltpu.make_async_remote_copy(
                src_ref=message.at[home, part],
                dst_ref=inbox.at[edge_place, part],
                send_sem=edge_m,
                recv_sem=recv_m,
                device_id=(edge_group, home),
                device_id_type=MESH,
            ).start()

        def keep():
            pltpu.make_async_copy(message.at[home, part], inbox.at[REACH + s, part], recv_m).start()

        def give():
            pltpu.make_async_remote_copy(
                src_ref=message.at[home, part],
                dst_ref=inbox.at[REACH + s, part],
                send_sem=send_m,
                recv_sem=recv_m,
                device_id=(g, home),
                device_id_type=MESH,
            ).start()

        if own is None:
            give()
        else:
            pl.when(own)(keep)
            pl.when(jnp.logical_not(own))(give)

    at_once = 4

    def homes_of(i):
        return [nearby(s, at_once * i + k, slabs) for k in range(at_once)]

    def serve_first(i, carry):
        homes = homes_of(i)
        for home, cut in zip(homes, [cut_for(0, home) for home in homes]):
            message[home, 0:8, :] = cut[0:8]
            message[home, 16:24, :] = cut[8:16]
        return carry

    def serve_second(i, carry):
        homes = homes_of(i)
        for home, cut in zip(homes, [cut_for(1, home) for home in homes]):
            message[home, 8:16, :] = cut[0:8]
            message[home, 16:24, :] = jnp.where(low_half, message[home, 16:24, :], pltpu.roll(cut[8:16], 4, 0))
        for k, home in enumerate(homes):
            deliver(home, None if k else i == 0, (0, 1, 2))
        return carry

    def serve_third(i, carry):
        homes = homes_of(i)
        for home, cut in zip(homes, [cut_for(2, home) for home in homes]):
            message[home, 24:40, :] = cut
        for k, home in enumerate(homes):
            deliver(home, None if k else i == 0, (3, 4))
        return carry

    parts = 2 * components

    def spread(k):
        wait_for(rows_in.at[k], recv_a.at[k])
        if k + 2 < parts:
            send_rows(k + 2)
        along_slab(k)
        send_ring(k)

    def gather(k):
        wait_for(ring_in.at[k], recv_b.at[k])
        along_ring(k)

    spread(0)
    spread(1)
    transform_plane(2)
    make_requests()
    pltpu.make_async_copy(asking_ref, asked_ref.at[s], recv_q).start()
    lax.fori_loop(1, slabs, ask_slab, 0)
    for k in range(2, parts):
        spread(k)
        gather(k - 2)
    wait_for(asked_ref.at[pl.ds(0, slabs)], recv_q)
    pltpu.sync_copy(asked_ref.at[pl.ds(0, slabs)], asked_smem.at[pl.ds(0, slabs)])

    @pl.when(at_edge)
    def _():
        passed = pltpu.make_async_remote_copy(
            src_ref=asked_ref.at[pl.ds(0, slabs)],
            dst_ref=asked_ref.at[pl.ds(slabs, slabs)],
            send_sem=send_e,
            recv_sem=recv_e,
            device_id=(jnp.where(at_start, above, below), s),
            device_id_type=MESH,
        )
        passed.start()
        passed.wait()
        pltpu.sync_copy(asked_ref.at[pl.ds(slabs, slabs)], asked_smem.at[pl.ds(slabs, slabs)])

    place_plane(0)
    lax.fori_loop(0, slabs // at_once, serve_first, 0)
    gather(parts - 2)
    gather(parts - 1)
    place_plane(1)
    lax.fori_loop(0, slabs // at_once, serve_second, 0)
    place_plane(2)
    lax.fori_loop(0, slabs // at_once, serve_third, 0)
    wait_for(inbox, recv_m)

    wait_for(inbox.at[pl.ds(0, slabs - 1)], send_m)

    @pl.when(at_edge)
    def _():
        wait_for(inbox.at[pl.ds(0, slabs)], edge_m)

    wait_for(asked_ref.at[pl.ds(0, slabs - 1)], send_q)

    holds_own = lax.div(s, share) == g

    def drain(c, carry):
        wait_for(rows_in.at[c, pl.ds(0, slabs - 1)], send_a.at[c])
        wait_for(ring_in.at[c, pl.ds(0, groups - 1)], send_b.at[c])

        @pl.when(holds_own)
        def _():
            wait_for(velocity.at[c, pl.ds(0, side - rows)], send_c.at[c])

        @pl.when(jnp.logical_not(holds_own))
        def _():
            wait_for(velocity.at[c], send_c.at[c])

        return carry

    lax.fori_loop(0, 2 * components, drain, 0)


def synthesize(source, tiles, spectrum, groups, slabs):
    components, side = spectrum.shape[1], spectrum.shape[3]
    rows, share, parts = side // slabs, slabs // groups, components * side // LANES
    ids = np.arange(side)
    angle = 2.0 * np.pi / side * (ids[:, None] * ids[None, :] % side)
    tables = jnp.stack(split_table(np.cos(angle)) + split_table(np.sin(angle)))
    count = groups * slabs
    twist = 2.0 * np.pi / count * (bit_reversed(groups)[:, None] * np.arange(slabs)[None, :])
    scale = 1.0 / math.sqrt(side * side * count)
    twiddle = np.stack([np.cos(twist), np.sin(twist)], axis=-1) * scale
    twiddle = jnp.asarray(twiddle.reshape(-1).astype(np.float32))
    vmem, hbm = pl.BlockSpec(memory_space=pltpu.VMEM), pl.BlockSpec(memory_space=pltpu.HBM)
    f32 = jnp.float32
    return pl.pallas_call(
        functools.partial(transform_kernel, groups, slabs),
        out_shape=jax.ShapeDtypeStruct((slabs + 2 * REACH, ROWS_OUT, LANES), f32),
        in_specs=[vmem, vmem, hbm, hbm, pl.BlockSpec(memory_space=pltpu.SMEM)],
        out_specs=vmem,
        scratch_shapes=[
            pltpu.VMEM((1, LANES), jnp.int32),
            pltpu.VMEM((2, components, side, side), f32),
            pltpu.VMEM((4, side, side), jnp.bfloat16),
            pltpu.VMEM((2 * slabs, 1, LANES), jnp.int32),
            pltpu.SMEM((2 * slabs, 1, LANES), jnp.int32),
            pltpu.VMEM((components, 2, side // 8 + 1, 8, LANES), f32),
            pltpu.VMEM((slabs, ROWS_OUT, LANES), f32),
            pltpu.VMEM((parts, 2, side, LANES), f32),
            pltpu.VMEM((parts, slabs, 2, rows, LANES), f32),
            pltpu.VMEM((parts, slabs, 2, rows, LANES), f32),
            pltpu.VMEM((parts, groups, share, 2, rows, LANES), f32),
            pltpu.VMEM((parts, groups, share, rows, LANES), f32),
            pltpu.VMEM((parts, side, LANES), f32),
        ]
        + [pltpu.SemaphoreType.DMA((parts,))] * 6
        + [pltpu.SemaphoreType.DMA] * 2
        + [pltpu.SemaphoreType.DMA((components,))]
        + [pltpu.SemaphoreType.DMA] * 6,
        compiler_params=pltpu.CompilerParams(
            collective_id=0, has_side_effects=True, vmem_limit_bytes=62 * 2**20
        ),
        cost_estimate=pl.CostEstimate(flops=2_500_000_000, bytes_accessed=100_000_000, transcendentals=0),
    )(source, tiles, spectrum[:, :, 0], tables, twiddle)


def interpolate_kernel(inbox, source_ref, fraction_ref, offset_ref, out_ref, weights, named):
    blocks, markers = fraction_ref.shape[1], fraction_ref.shape[2]
    weights[...] = jnp.zeros_like(weights)
    group = weights.shape[0]
    first_lanes = lax.broadcasted_iota(jnp.int32, (ROWS_OUT * PLANES, LANES), 1) < 16
    row_y = lax.broadcasted_iota(jnp.int32, (16, markers), 0)
    row_x = jnp.where(row_y < 12, row_y, row_y - 4)
    in_low = lax.broadcasted_iota(jnp.int32, (8, markers), 0) < 4

    for k in range(named.shape[0]):
        named[k] = 0

    def one_block(i, weights):
        f = jnp.concatenate([fraction_ref[d, pl.ds(i, 1), :] for d in range(3)], axis=0)
        o = [offset_ref[d, pl.ds(i, 1), :] for d in range(3)]
        root = jnp.sqrt(1.0 + 4.0 * f - 4.0 * f * f)
        low, high = 3.0 - 2.0 * f, 1.0 + 2.0 * f
        taps = ((low - root) * 0.125, (low + root) * 0.125, (high + root) * 0.125, (high - root) * 0.125)
        weight_x = jnp.zeros((16, markers), jnp.float32)
        weight_y = jnp.zeros((16, markers), jnp.float32)
        for e in range(4):
            weight_x = jnp.where(row_x == o[1] + e, taps[e][1:2], weight_x)
            weight_y = jnp.where(row_y == o[2] + e, taps[e][2:3], weight_y)
        y_high, y_low = split(weight_y)
        weights[0:16, :] = y_high
        weights[16:32, :] = y_low
        weights[LANES : LANES + 16, :] = y_high
        near = o[0] == 0
        none = jnp.zeros((1, markers), jnp.float32)
        tap_z = [none] + [tap[0:1] for tap in taps] + [none]
        weight_z = [jnp.where(near, tap_z[j + 1], tap_z[j]) for j in range(PLANES)]
        source = source_ref[0, i]
        slot = named[source]
        named[source] = 1
        cells = []
        for j in range(PLANES):
            place = CELLS * (2 * (PLANES - 1 - j) + slot)
            cells.append(pltpu.roll(inbox[source + j], (2 * LANES - place) & (LANES - 1), 1))
        cells = jnp.concatenate(cells, axis=0)
        cells = jnp.where(first_lanes, cells, pltpu.roll(cells, 16, 1))
        values = dot(jnp.concatenate(split(cells), axis=1), weights[...])
        sums = []
        for t in range(ROWS_OUT // 8):
            total = weight_z[0] * values[8 * t : 8 * t + 8]
            for j in range(1, PLANES):
                total = total + weight_z[j] * values[ROWS_OUT * j + 8 * t : ROWS_OUT * j + 8 * t + 8]
            sums.append(total)
        x_first, x_last = weight_x[0:8], weight_x[8:16]
        mixed, last = sums[2] * x_last, sums[4] * x_last
        tails = (jnp.where(in_low, mixed, 0.0), jnp.where(in_low, 0.0, mixed), jnp.where(in_low, last, 0.0))
        for c in range(3):
            out_ref[c, pl.ds(i, 1), :] = jnp.sum(sums[(0, 1, 3)[c]] * x_first + tails[c], axis=0, keepdims=True)

    def several(i, carry):
        for k in range(group):
            one_block(group * i + k, weights.at[k])
        return carry

    lax.fori_loop(0, blocks // group, several, 0)


def sample(inbox, source, fraction, offsets, slabs):
    vmem, smem = pl.BlockSpec(memory_space=pltpu.VMEM), pl.BlockSpec(memory_space=pltpu.SMEM)
    markers = fraction.shape[2]
    return pl.pallas_call(
        interpolate_kernel,
        out_shape=jax.ShapeDtypeStruct(fraction.shape, jnp.float32),
        in_specs=[vmem, smem, vmem, vmem],
        out_specs=vmem,
        scratch_shapes=[pltpu.VMEM((8, 2 * LANES, markers), jnp.bfloat16), pltpu.SMEM((slabs,), jnp.int32)],
        cost_estimate=pl.CostEstimate(flops=200_000_000, bytes_accessed=1_500_000, transcendentals=25_000),
    )(inbox, source, fraction, offsets)


def local(groups, slabs, spectrum, marker_fraction, marker_offsets, block_source, block_tile):
    source = jnp.transpose(block_source)
    inbox = synthesize(source, jnp.transpose(block_tile), spectrum, groups, slabs)
    fraction, offsets = jnp.transpose(marker_fraction, (1, 0, 2)), jnp.transpose(marker_offsets, (1, 0, 2))
    answer = sample(inbox, source, fraction, offsets, slabs)
    return jnp.transpose(answer, (1, 0, 2))


def solution(mesh):
    groups, slabs = mesh.shape["grp"], mesh.shape["gz"]
    both = ("grp", "gz")
    return jax.shard_map(
        functools.partial(local, groups, slabs),
        mesh=mesh,
        in_specs=(
            P(None, None, both, None, None),
            P(both, None, None),
            P(both, None, None),
            P(both, None),
            P(both, None),
        ),
        out_specs=P(both, None, None),
        check_vma=False,
    )
```

```python
import functools
import math

import jax
import jax.numpy as jnp
import ml_dtypes
import numpy as np
from jax import lax
from jax.experimental import pallas as pl
from jax.experimental.pallas import tpu as pltpu
from jax.sharding import PartitionSpec as P

MESH = pl.DeviceIdType.MESH
REACH = 2
PLANES = 2 * REACH + 1
CELLS = 12
LANES = 128
ROWS_OUT = 40


def bit_reversed(count):
    bits = count.bit_length() - 1
    return np.array([int(format(i, f"0{bits}b")[::-1], 2) if bits else 0 for i in range(count)])


def split_table(values):
    high = values.astype(ml_dtypes.bfloat16)
    low = (values - high.astype(np.float64)).astype(ml_dtypes.bfloat16)
    return jnp.asarray(high), jnp.asarray(low)


def split(x):
    high = x.astype(jnp.bfloat16)
    return high, (x - high.astype(jnp.float32)).astype(jnp.bfloat16)


def dot(a, b):
    return jnp.dot(a, b, preferred_element_type=jnp.float32)


def dot3(a, b):
    return dot(a[0], b[0]) + (dot(a[1], b[0]) + dot(a[0], b[1]))


def turn(re, im, angle_num, angle_den):
    eighth = 8 * angle_num % (8 * angle_den) / angle_den
    if eighth == 0:
        return re, im
    if eighth == 2:
        return -im, re
    cosine, sine = math.cos(math.pi * eighth / 4), math.sin(math.pi * eighth / 4)
    if eighth == 1:
        return (re - im) * cosine, (re + im) * cosine
    if eighth == 3:
        return (re + im) * cosine, (re - im) * sine
    return cosine * re - sine * im, sine * re + cosine * im


def butterflies(items, first_half, position_of, real_at_end=False):
    count = len(items)
    half = 1
    while half < count:
        last = real_at_end and 2 * half == count
        for low in range(count):
            if low // half % 2:
                continue
            high = low + half
            span = half * first_half
            re, im = turn(*items[high], position_of(low) % span, 2 * span)
            first = items[low]
            if last:
                items[low], items[high] = (first[0] + re, None), (first[0] - re, None)
            else:
                items[low] = (first[0] + re, first[1] + im)
                items[high] = (first[0] - re, first[1] - im)
        half *= 2
    return items


def wait_for(ref, semaphore):
    pltpu.make_async_copy(ref, ref, semaphore).wait()


def nearby(me, i, count):
    return lax.rem(me + (2 * lax.rem(i, 2) - 1) * lax.div(i + 1, 2) + count, count)


def transform_kernel(
    groups,
    slabs,
    source_ref,
    tile_ref,
    spec_hbm,
    table_hbm,
    twiddle_ref,
    inbox,
    asking_ref,
    spec_ref,
    table,
    asked_ref,
    asked_smem,
    padded,
    message,
    plane_t,
    rows_in,
    rows_z,
    ring_in,
    real_z,
    velocity,
    send_a,
    recv_a,
    send_b,
    recv_b,
    send_c,
    recv_c,
    send_q,
    recv_q,
    load_sem,
    table_sem,
    send_m,
    edge_m,
    recv_m,
    send_e,
    recv_e,
):
    g = lax.axis_index("grp")
    s = lax.axis_index("gz")
    side = spec_ref.shape[2]
    loads = [pltpu.make_async_copy(table_hbm, table, table_sem)]
    loads += [pltpu.make_async_copy(spec_hbm.at[:, c], spec_ref.at[:, c], load_sem.at[c]) for c in range(spec_ref.shape[1])]
    for load in loads:
        load.start()
    rows = side // slabs
    share = slabs // groups
    components = spec_ref.shape[1]

    below, above = lax.rem(g + groups - 1, groups), lax.rem(g + 1, groups)
    at_start, at_end = s < REACH, s >= slabs - REACH
    at_edge = jnp.logical_or(at_start, at_end)
    edge_group = jnp.where(at_start, below, above)

    barrier = pltpu.get_barrier_semaphore()

    def greet_slab(i, carry):
        pl.semaphore_signal(barrier, inc=1, device_id=(g, lax.rem(s + i, slabs)), device_id_type=MESH)
        return carry

    def greet_ring(i, carry):
        pl.semaphore_signal(barrier, inc=1, device_id=(lax.rem(g + i, groups), s), device_id_type=MESH)
        return carry

    lax.fori_loop(1, slabs, greet_slab, 0)
    lax.fori_loop(1, groups, greet_ring, 0)

    def transform_plane(c):
        pltpu.make_async_copy(spec_hbm.at[:, c], spec_ref.at[:, c], load_sem.at[c]).wait()
        cosine, sine = (table[0], table[1]), (table[2], table[3])
        re, im = split(spec_ref[0, c]), split(spec_ref[1, c])
        row_re = split(dot3(re, cosine) - dot3(im, sine))
        row_im = split(dot3(re, sine) + dot3(im, cosine))
        for part, whole in (
            (0, dot3(cosine, row_re) - dot3(sine, row_im)),
            (1, dot3(sine, row_re) + dot3(cosine, row_im)),
        ):
            for half in range(2):
                plane_t[2 * c + half, part] = whole[:, half * LANES : (half + 1) * LANES]

    def send_rows(c):
        def one(i, carry):
            r = nearby(s, i, slabs)
            pltpu.make_async_remote_copy(
                src_ref=plane_t.at[c, :, pl.ds(pl.multiple_of(r * rows, rows), rows), :],
                dst_ref=rows_in.at[c, s],
                send_sem=send_a.at[c],
                recv_sem=recv_a.at[c],
                device_id=(g, r),
                device_id_type=MESH,
            ).start()
            return carry

        pltpu.make_async_copy(
            plane_t.at[c, :, pl.ds(pl.multiple_of(s * rows, rows), rows), :],
            rows_in.at[c, s],
            recv_a.at[c],
        ).start()
        lax.fori_loop(1, slabs, one, 0)

    def make_requests():
        blocks = source_ref.shape[1]
        down = lax.broadcasted_iota(jnp.int32, (blocks, blocks), 0)
        along = lax.broadcasted_iota(jnp.int32, (blocks, blocks), 1)
        tiles = side // 8
        code = (along[0:1] * tiles + tile_ref[0:1, :]) * tiles + tile_ref[1:2, :]

        def upright(row):
            return jnp.sum(jnp.where(down == along, row.astype(jnp.float32), 0.0), axis=1, keepdims=True)

        spot = lax.broadcasted_iota(jnp.int32, (blocks, LANES), 1)
        named = upright(source_ref[...]) == (spot >> 2).astype(jnp.float32)
        codes = upright(code)
        first = jnp.min(jnp.where(named, codes, float(tiles * tiles * blocks)), axis=0, keepdims=True)
        second = jnp.max(jnp.where(named, codes, 0.0), axis=0, keepdims=True)
        chosen = jnp.where((spot[0:1] & 2) == 0, first, second).astype(jnp.int32)
        across = (chosen & (tiles - 1)) * 8 + side - REACH
        asking_ref[...] = jnp.where((spot[0:1] & 1) == 0, (chosen // tiles) & (tiles - 1), across & (side - 1))

    def ask(place, device):
        pltpu.make_async_remote_copy(
            src_ref=asking_ref,
            dst_ref=asked_ref.at[place],
            send_sem=send_q,
            recv_sem=recv_q,
            device_id=device,
            device_id_type=MESH,
        ).start()

    def ask_slab(i, carry):
        ask(s, (g, nearby(s, i, slabs)))
        return carry

    loads[0].wait()
    transform_plane(0)
    pl.semaphore_wait(barrier, slabs - 1 + groups - 1)
    send_rows(0)
    transform_plane(1)
    send_rows(1)

    inner = min(8, slabs)
    outer = slabs // inner

    def along_slab(c):
        for block in range(outer):
            items = {k: (rows_in[c, inner * block + k, 0], rows_in[c, inner * block + k, 1]) for k in range(inner)}
            items = butterflies(items, 1, lambda k: k)
            for k in range(inner):
                rows_in[c, inner * block + k, 0], rows_in[c, inner * block + k, 1] = items[k]
        for k in range(inner):
            items = {m: (rows_in[c, inner * m + k, 0], rows_in[c, inner * m + k, 1]) for m in range(outer)}
            items = butterflies(items, inner, lambda m, k=k: inner * m + k)
            for m in range(outer):
                w = inner * m + k
                cosine, sine = twiddle_ref[g * 2 * slabs + 2 * w], twiddle_ref[g * 2 * slabs + 2 * w + 1]
                re, im = items[m]
                rows_z[c, w, 0] = cosine * re - sine * im
                rows_z[c, w, 1] = sine * re + cosine * im

    def send_ring(c):
        def one(i, inner_carry):
            to = nearby(g, i, groups)
            pltpu.make_async_remote_copy(
                src_ref=rows_z.at[c, pl.ds(to * share, share)],
                dst_ref=ring_in.at[c, g],
                send_sem=send_b.at[c],
                recv_sem=recv_b.at[c],
                device_id=(to, s),
                device_id_type=MESH,
            ).start()
            return inner_carry

        pltpu.make_async_copy(rows_z.at[c, pl.ds(g * share, share)], ring_in.at[c, g], recv_b.at[c]).start()
        lax.fori_loop(1, groups, one, 0)

    def along_ring(c):
        for k in range(share):
            items = {q: (ring_in[c, q, k, 0], ring_in[c, q, k, 1]) for q in range(groups)}
            items = butterflies(items, 1, lambda q: q, real_at_end=True)
            for u in range(groups):
                real_z[c, u, k] = items[u][0]

        def one(i, inner_carry):
            to = nearby(g, lax.div(i, share), groups)
            k = lax.rem(i, share)
            w = g * share + k
            mine = jnp.logical_and(to == g, w == s)
            place = velocity.at[c, pl.ds(pl.multiple_of(s * rows, rows), rows), :]

            @pl.when(mine)
            def _():
                pltpu.make_async_copy(real_z.at[c, to, k], place, recv_c.at[c]).start()

            @pl.when(jnp.logical_not(mine))
            def _():
                pltpu.make_async_remote_copy(
                    src_ref=real_z.at[c, to, k],
                    dst_ref=place,
                    send_sem=send_c.at[c],
                    recv_sem=recv_c.at[c],
                    device_id=(to, w),
                    device_id_type=MESH,
                ).start()

            return inner_carry

        lax.fori_loop(0, slabs, one, 0)


    edge_place = jnp.where(at_start, slabs + REACH + s, s - (slabs - REACH))
    low_half = lax.broadcasted_iota(jnp.int32, (8, LANES), 0) < 4
    lane = lax.broadcasted_iota(jnp.int32, (16, LANES), 1)

    def place_plane(c):
        for half in range(2):
            got = velocity.at[2 * c + half]
            wait_for(got, recv_c.at[2 * c + half])
            whole = [got[side - REACH : side, :], got[...], got[0 : 8 - REACH, :]]
            padded[c, half] = jnp.concatenate(whole, axis=0).reshape(side // 8 + 1, 8, LANES)

    spots = []
    for slot in range(2 * PLANES):
        centre = s + slot // 2 - REACH
        inside = jnp.logical_and(centre >= 0, centre < slabs)
        column = 4 * lax.rem(centre + slabs, slabs) + 2 * (slot % 2)
        spots.append((jnp.where(inside, 0, slabs), column))

    def cut_for(c, home):
        cut = jnp.zeros((16, LANES), jnp.float32)
        for slot in range(2 * PLANES):
            row, column = home + spots[slot][0], spots[slot][1]
            tile = asked_smem[row, 0, column]
            first = asked_smem[row, 0, column + 1]
            half = first >> 7
            first = first & (LANES - 1)
            near = jnp.concatenate([padded[c, half, tile], padded[c, half, tile + 1]], axis=0)
            far = jnp.concatenate([padded[c, 1 - half, tile], padded[c, 1 - half, tile + 1]], axis=0)
            cells = jnp.where(lane >= first, near, far)
            moved = pltpu.roll(cells, (CELLS * slot + LANES - first) & (LANES - 1), 1)
            taken = jnp.logical_and(lane >= CELLS * slot, lane < CELLS * (slot + 1))
            cut = jnp.where(taken, moved, cut)
        return cut

    def deliver(home, own, tiles):
        part = pl.ds(8 * tiles[0], 8 * len(tiles))

        @pl.when(at_edge)
        def _():
            pltpu.make_async_remote_copy(
                src_ref=message.at[home, part],
                dst_ref=inbox.at[edge_place, part],
                send_sem=edge_m,
                recv_sem=recv_m,
                device_id=(edge_group, home),
                device_id_type=MESH,
            ).start()

        def keep():
            pltpu.make_async_copy(message.at[home, part], inbox.at[REACH + s, part], recv_m).start()

        def give():
            pltpu.make_async_remote_copy(
                src_ref=message.at[home, part],
                dst_ref=inbox.at[REACH + s, part],
                send_sem=send_m,
                recv_sem=recv_m,
                device_id=(g, home),
                device_id_type=MESH,
            ).start()

        if own is None:
            give()
        else:
            pl.when(own)(keep)
            pl.when(jnp.logical_not(own))(give)

    at_once = 4

    def homes_of(i):
        return [nearby(s, at_once * i + k, slabs) for k in range(at_once)]

    def serve_first(i, carry):
        homes = homes_of(i)
        for home, cut in zip(homes, [cut_for(0, home) for home in homes]):
            message[home, 0:8, :] = cut[0:8]
            message[home, 16:24, :] = cut[8:16]
        return carry

    def serve_second(i, carry):
        homes = homes_of(i)
        for home, cut in zip(homes, [cut_for(1, home) for home in homes]):
            message[home, 8:16, :] = cut[0:8]
            message[home, 16:24, :] = jnp.where(low_half, message[home, 16:24, :], pltpu.roll(cut[8:16], 4, 0))
        for k, home in enumerate(homes):
            deliver(home, None if k else i == 0, (0, 1, 2))
        return carry

    def serve_third(i, carry):
        homes = homes_of(i)
        for home, cut in zip(homes, [cut_for(2, home) for home in homes]):
            message[home, 24:40, :] = cut
        for k, home in enumerate(homes):
            deliver(home, None if k else i == 0, (3, 4))
        return carry

    parts = 2 * components

    def spread(k):
        wait_for(rows_in.at[k], recv_a.at[k])
        if k + 2 < parts:
            send_rows(k + 2)
        along_slab(k)
        send_ring(k)

    def gather(k):
        wait_for(ring_in.at[k], recv_b.at[k])
        along_ring(k)

    spread(0)
    spread(1)
    transform_plane(2)
    make_requests()
    pltpu.make_async_copy(asking_ref, asked_ref.at[s], recv_q).start()
    lax.fori_loop(1, slabs, ask_slab, 0)
    spread(2)
    gather(0)

    own_asked, more_asked = pl.ds(0, slabs), pl.ds(slabs, slabs)
    wait_for(asked_ref.at[own_asked], recv_q)

    @pl.when(at_edge)
    def _():
        pltpu.make_async_remote_copy(
            src_ref=asked_ref.at[own_asked],
            dst_ref=asked_ref.at[more_asked],
            send_sem=send_e,
            recv_sem=recv_e,
            device_id=(jnp.where(at_start, above, below), s),
            device_id_type=MESH,
        ).start()

    pltpu.sync_copy(asked_ref.at[own_asked], asked_smem.at[own_asked])
    for k in range(3, parts):
        spread(k)
        gather(k - 2)

    @pl.when(at_edge)
    def _():
        wait_for(asked_ref.at[more_asked], recv_e)
        wait_for(asked_ref.at[own_asked], send_e)
        pltpu.sync_copy(asked_ref.at[more_asked], asked_smem.at[more_asked])

    place_plane(0)
    lax.fori_loop(0, slabs // at_once, serve_first, 0)
    gather(parts - 2)
    gather(parts - 1)
    place_plane(1)
    lax.fori_loop(0, slabs // at_once, serve_second, 0)
    place_plane(2)
    lax.fori_loop(0, slabs // at_once, serve_third, 0)
    wait_for(inbox, recv_m)

    wait_for(inbox.at[pl.ds(0, slabs - 1)], send_m)

    @pl.when(at_edge)
    def _():
        wait_for(inbox.at[pl.ds(0, slabs)], edge_m)

    wait_for(asked_ref.at[pl.ds(0, slabs - 1)], send_q)

    holds_own = lax.div(s, share) == g

    def drain(c, carry):
        wait_for(rows_in.at[c, pl.ds(0, slabs - 1)], send_a.at[c])
        wait_for(ring_in.at[c, pl.ds(0, groups - 1)], send_b.at[c])

        @pl.when(holds_own)
        def _():
            wait_for(velocity.at[c, pl.ds(0, side - rows)], send_c.at[c])

        @pl.when(jnp.logical_not(holds_own))
        def _():
            wait_for(velocity.at[c], send_c.at[c])

        return carry

    lax.fori_loop(0, 2 * components, drain, 0)


def synthesize(source, tiles, spectrum, groups, slabs):
    components, side = spectrum.shape[1], spectrum.shape[3]
    rows, share, parts = side // slabs, slabs // groups, components * side // LANES
    ids = np.arange(side)
    angle = 2.0 * np.pi / side * (ids[:, None] * ids[None, :] % side)
    tables = jnp.stack(split_table(np.cos(angle)) + split_table(np.sin(angle)))
    count = groups * slabs
    twist = 2.0 * np.pi / count * (bit_reversed(groups)[:, None] * np.arange(slabs)[None, :])
    scale = 1.0 / math.sqrt(side * side * count)
    twiddle = np.stack([np.cos(twist), np.sin(twist)], axis=-1) * scale
    twiddle = jnp.asarray(twiddle.reshape(-1).astype(np.float32))
    vmem, hbm = pl.BlockSpec(memory_space=pltpu.VMEM), pl.BlockSpec(memory_space=pltpu.HBM)
    f32 = jnp.float32
    return pl.pallas_call(
        functools.partial(transform_kernel, groups, slabs),
        out_shape=jax.ShapeDtypeStruct((slabs + 2 * REACH, ROWS_OUT, LANES), f32),
        in_specs=[vmem, vmem, hbm, hbm, pl.BlockSpec(memory_space=pltpu.SMEM)],
        out_specs=vmem,
        scratch_shapes=[
            pltpu.VMEM((1, LANES), jnp.int32),
            pltpu.VMEM((2, components, side, side), f32),
            pltpu.VMEM((4, side, side), jnp.bfloat16),
            pltpu.VMEM((2 * slabs, 1, LANES), jnp.int32),
            pltpu.SMEM((2 * slabs, 1, LANES), jnp.int32),
            pltpu.VMEM((components, 2, side // 8 + 1, 8, LANES), f32),
            pltpu.VMEM((slabs, ROWS_OUT, LANES), f32),
            pltpu.VMEM((parts, 2, side, LANES), f32),
            pltpu.VMEM((parts, slabs, 2, rows, LANES), f32),
            pltpu.VMEM((parts, slabs, 2, rows, LANES), f32),
            pltpu.VMEM((parts, groups, share, 2, rows, LANES), f32),
            pltpu.VMEM((parts, groups, share, rows, LANES), f32),
            pltpu.VMEM((parts, side, LANES), f32),
        ]
        + [pltpu.SemaphoreType.DMA((parts,))] * 6
        + [pltpu.SemaphoreType.DMA] * 2
        + [pltpu.SemaphoreType.DMA((components,))]
        + [pltpu.SemaphoreType.DMA] * 6,
        compiler_params=pltpu.CompilerParams(
            collective_id=0, has_side_effects=True, vmem_limit_bytes=62 * 2**20
        ),
        cost_estimate=pl.CostEstimate(flops=2_500_000_000, bytes_accessed=100_000_000, transcendentals=0),
    )(source, tiles, spectrum[:, :, 0], tables, twiddle)


def interpolate_kernel(inbox, source_ref, fraction_ref, offset_ref, out_ref, weights, named):
    blocks, markers = fraction_ref.shape[1], fraction_ref.shape[2]
    weights[...] = jnp.zeros_like(weights)
    group = weights.shape[0]
    first_lanes = lax.broadcasted_iota(jnp.int32, (ROWS_OUT * PLANES, LANES), 1) < 16
    row_y = lax.broadcasted_iota(jnp.int32, (16, markers), 0)
    row_x = jnp.where(row_y < 12, row_y, row_y - 4)
    in_low = lax.broadcasted_iota(jnp.int32, (8, markers), 0) < 4

    for k in range(named.shape[0]):
        named[k] = 0

    def one_block(i, weights):
        f = jnp.concatenate([fraction_ref[d, pl.ds(i, 1), :] for d in range(3)], axis=0)
        o = [offset_ref[d, pl.ds(i, 1), :] for d in range(3)]
        root = jnp.sqrt(1.0 + 4.0 * f - 4.0 * f * f)
        low, high = 3.0 - 2.0 * f, 1.0 + 2.0 * f
        taps = ((low - root) * 0.125, (low + root) * 0.125, (high + root) * 0.125, (high - root) * 0.125)
        weight_x = jnp.zeros((16, markers), jnp.float32)
        weight_y = jnp.zeros((16, markers), jnp.float32)
        for e in range(4):
            weight_x = jnp.where(row_x == o[1] + e, taps[e][1:2], weight_x)
            weight_y = jnp.where(row_y == o[2] + e, taps[e][2:3], weight_y)
        y_high, y_low = split(weight_y)
        weights[0:16, :] = y_high
        weights[16:32, :] = y_low
        weights[LANES : LANES + 16, :] = y_high
        near = o[0] == 0
        none = jnp.zeros((1, markers), jnp.float32)
        tap_z = [none] + [tap[0:1] for tap in taps] + [none]
        weight_z = [jnp.where(near, tap_z[j + 1], tap_z[j]) for j in range(PLANES)]
        source = source_ref[0, i]
        slot = named[source]
        named[source] = 1
        cells = []
        for j in range(PLANES):
            place = CELLS * (2 * (PLANES - 1 - j) + slot)
            cells.append(pltpu.roll(inbox[source + j], (2 * LANES - place) & (LANES - 1), 1))
        cells = jnp.concatenate(cells, axis=0)
        cells = jnp.where(first_lanes, cells, pltpu.roll(cells, 16, 1))
        values = dot(jnp.concatenate(split(cells), axis=1), weights[...])
        sums = []
        for t in range(ROWS_OUT // 8):
            total = weight_z[0] * values[8 * t : 8 * t + 8]
            for j in range(1, PLANES):
                total = total + weight_z[j] * values[ROWS_OUT * j + 8 * t : ROWS_OUT * j + 8 * t + 8]
            sums.append(total)
        x_first, x_last = weight_x[0:8], weight_x[8:16]
        mixed, last = sums[2] * x_last, sums[4] * x_last
        tails = (jnp.where(in_low, mixed, 0.0), jnp.where(in_low, 0.0, mixed), jnp.where(in_low, last, 0.0))
        for c in range(3):
            out_ref[c, pl.ds(i, 1), :] = jnp.sum(sums[(0, 1, 3)[c]] * x_first + tails[c], axis=0, keepdims=True)

    def several(i, carry):
        for k in range(group):
            one_block(group * i + k, weights.at[k])
        return carry

    lax.fori_loop(0, blocks // group, several, 0)


def sample(inbox, source, fraction, offsets, slabs):
    vmem, smem = pl.BlockSpec(memory_space=pltpu.VMEM), pl.BlockSpec(memory_space=pltpu.SMEM)
    markers = fraction.shape[2]
    return pl.pallas_call(
        interpolate_kernel,
        out_shape=jax.ShapeDtypeStruct(fraction.shape, jnp.float32),
        in_specs=[vmem, smem, vmem, vmem],
        out_specs=vmem,
        scratch_shapes=[pltpu.VMEM((8, 2 * LANES, markers), jnp.bfloat16), pltpu.SMEM((slabs,), jnp.int32)],
        cost_estimate=pl.CostEstimate(flops=200_000_000, bytes_accessed=1_500_000, transcendentals=25_000),
    )(inbox, source, fraction, offsets)


def local(groups, slabs, spectrum, marker_fraction, marker_offsets, block_source, block_tile):
    source = jnp.transpose(block_source)
    inbox = synthesize(source, jnp.transpose(block_tile), spectrum, groups, slabs)
    fraction, offsets = jnp.transpose(marker_fraction, (1, 0, 2)), jnp.transpose(marker_offsets, (1, 0, 2))
    answer = sample(inbox, source, fraction, offsets, slabs)
    return jnp.transpose(answer, (1, 0, 2))


def solution(mesh):
    groups, slabs = mesh.shape["grp"], mesh.shape["gz"]
    both = ("grp", "gz")
    return jax.shard_map(
        functools.partial(local, groups, slabs),
        mesh=mesh,
        in_specs=(
            P(None, None, both, None, None),
            P(both, None, None),
            P(both, None, None),
            P(both, None),
            P(both, None),
        ),
        out_specs=P(both, None, None),
        check_vma=False,
    )
```

```python
import functools
import math

import jax
import jax.numpy as jnp
import ml_dtypes
import numpy as np
from jax import lax
from jax.experimental import pallas as pl
from jax.experimental.pallas import tpu as pltpu
from jax.sharding import PartitionSpec as P

MESH = pl.DeviceIdType.MESH
REACH = 2
PLANES = 2 * REACH + 1
CELLS = 12
LANES = 128
ROWS_OUT = 40


def bit_reversed(count):
    bits = count.bit_length() - 1
    return np.array([int(format(i, f"0{bits}b")[::-1], 2) if bits else 0 for i in range(count)])


def split_table(values):
    high = values.astype(ml_dtypes.bfloat16)
    low = (values - high.astype(np.float64)).astype(ml_dtypes.bfloat16)
    return jnp.asarray(high), jnp.asarray(low)


def split(x):
    high = x.astype(jnp.bfloat16)
    return high, (x - high.astype(jnp.float32)).astype(jnp.bfloat16)


def dot(a, b):
    return jnp.dot(a, b, preferred_element_type=jnp.float32)


def dot3(a, b):
    return dot(a[0], b[0]) + (dot(a[1], b[0]) + dot(a[0], b[1]))


def turn(re, im, angle_num, angle_den):
    eighth = 8 * angle_num % (8 * angle_den) / angle_den
    if eighth == 0:
        return re, im
    if eighth == 2:
        return -im, re
    cosine, sine = math.cos(math.pi * eighth / 4), math.sin(math.pi * eighth / 4)
    if eighth == 1:
        return (re - im) * cosine, (re + im) * cosine
    if eighth == 3:
        return (re + im) * cosine, (re - im) * sine
    return cosine * re - sine * im, sine * re + cosine * im


def butterflies(items, first_half, position_of, real_at_end=False):
    count = len(items)
    half = 1
    while half < count:
        last = real_at_end and 2 * half == count
        for low in range(count):
            if low // half % 2:
                continue
            high = low + half
            span = half * first_half
            re, im = turn(*items[high], position_of(low) % span, 2 * span)
            first = items[low]
            if last:
                items[low], items[high] = (first[0] + re, None), (first[0] - re, None)
            else:
                items[low] = (first[0] + re, first[1] + im)
                items[high] = (first[0] - re, first[1] - im)
        half *= 2
    return items


def wait_for(ref, semaphore):
    pltpu.make_async_copy(ref, ref, semaphore).wait()


def nearby(me, i, count):
    return lax.rem(me + (2 * lax.rem(i, 2) - 1) * lax.div(i + 1, 2) + count, count)


def transform_kernel(
    groups,
    slabs,
    source_ref,
    tile_ref,
    spec_hbm,
    table_hbm,
    twiddle_ref,
    inbox,
    asking_ref,
    spec_ref,
    table,
    asked_ref,
    asked_smem,
    padded,
    message,
    plane_t,
    rows_in,
    rows_z,
    ring_in,
    real_z,
    velocity,
    send_a,
    recv_a,
    send_b,
    recv_b,
    send_c,
    recv_c,
    send_q,
    recv_q,
    load_sem,
    table_sem,
    send_m,
    edge_m,
    recv_m,
    send_e,
    recv_e,
):
    g = lax.axis_index("grp")
    s = lax.axis_index("gz")
    side = spec_ref.shape[2]
    loads = [pltpu.make_async_copy(table_hbm, table, table_sem)]
    loads += [pltpu.make_async_copy(spec_hbm.at[:, c], spec_ref.at[:, c], load_sem.at[c]) for c in range(spec_ref.shape[1])]
    for load in loads:
        load.start()
    rows = side // slabs
    share = slabs // groups
    components = spec_ref.shape[1]

    below, above = lax.rem(g + groups - 1, groups), lax.rem(g + 1, groups)
    at_start, at_end = s < REACH, s >= slabs - REACH
    at_edge = jnp.logical_or(at_start, at_end)
    edge_group = jnp.where(at_start, below, above)

    barrier = pltpu.get_barrier_semaphore()

    def greet_slab(i, carry):
        pl.semaphore_signal(barrier, inc=1, device_id=(g, lax.rem(s + i, slabs)), device_id_type=MESH)
        return carry

    def greet_ring(i, carry):
        pl.semaphore_signal(barrier, inc=1, device_id=(lax.rem(g + i, groups), s), device_id_type=MESH)
        return carry

    lax.fori_loop(1, slabs, greet_slab, 0)
    lax.fori_loop(1, groups, greet_ring, 0)

    def transform_plane(c):
        pltpu.make_async_copy(spec_hbm.at[:, c], spec_ref.at[:, c], load_sem.at[c]).wait()
        cosine, sine = (table[0], table[1]), (table[2], table[3])
        re, im = split(spec_ref[0, c]), split(spec_ref[1, c])
        row_re = split(dot3(re, cosine) - dot3(im, sine))
        row_im = split(dot3(re, sine) + dot3(im, cosine))
        for part, whole in (
            (0, dot3(cosine, row_re) - dot3(sine, row_im)),
            (1, dot3(sine, row_re) + dot3(cosine, row_im)),
        ):
            for half in range(2):
                plane_t[2 * c + half, part] = whole[:, half * LANES : (half + 1) * LANES]

    def send_rows(c):
        def one(i, carry):
            r = nearby(s, i, slabs)
            pltpu.make_async_remote_copy(
                src_ref=plane_t.at[c, :, pl.ds(pl.multiple_of(r * rows, rows), rows), :],
                dst_ref=rows_in.at[c, s],
                send_sem=send_a.at[c],
                recv_sem=recv_a.at[c],
                device_id=(g, r),
                device_id_type=MESH,
            ).start()
            return carry

        pltpu.make_async_copy(
            plane_t.at[c, :, pl.ds(pl.multiple_of(s * rows, rows), rows), :],
            rows_in.at[c, s],
            recv_a.at[c],
        ).start()
        lax.fori_loop(1, slabs, one, 0)

    def make_requests():
        blocks = source_ref.shape[1]
        down = lax.broadcasted_iota(jnp.int32, (blocks, blocks), 0)
        along = lax.broadcasted_iota(jnp.int32, (blocks, blocks), 1)
        tiles = side // 8
        code = (along[0:1] * tiles + tile_ref[0:1, :]) * tiles + tile_ref[1:2, :]

        def upright(row):
            return jnp.sum(jnp.where(down == along, row.astype(jnp.float32), 0.0), axis=1, keepdims=True)

        spot = lax.broadcasted_iota(jnp.int32, (blocks, LANES), 1)
        named = upright(source_ref[...]) == (spot >> 2).astype(jnp.float32)
        codes = upright(code)
        first = jnp.min(jnp.where(named, codes, float(tiles * tiles * blocks)), axis=0, keepdims=True)
        second = jnp.max(jnp.where(named, codes, 0.0), axis=0, keepdims=True)
        chosen = jnp.where((spot[0:1] & 2) == 0, first, second).astype(jnp.int32)
        across = (chosen & (tiles - 1)) * 8 + side - REACH
        asking_ref[...] = jnp.where((spot[0:1] & 1) == 0, (chosen // tiles) & (tiles - 1), across & (side - 1))

    def ask(place, device):
        pltpu.make_async_remote_copy(
            src_ref=asking_ref,
            dst_ref=asked_ref.at[place],
            send_sem=send_q,
            recv_sem=recv_q,
            device_id=device,
            device_id_type=MESH,
        ).start()

    def ask_slab(i, carry):
        ask(s, (g, nearby(s, i, slabs)))
        return carry

    loads[0].wait()
    transform_plane(0)
    pl.semaphore_wait(barrier, slabs - 1 + groups - 1)
    send_rows(0)
    transform_plane(1)
    send_rows(1)

    inner = min(8, slabs)
    outer = slabs // inner

    def along_slab(c):
        for block in range(outer):
            items = {k: (rows_in[c, inner * block + k, 0], rows_in[c, inner * block + k, 1]) for k in range(inner)}
            items = butterflies(items, 1, lambda k: k)
            for k in range(inner):
                rows_in[c, inner * block + k, 0], rows_in[c, inner * block + k, 1] = items[k]
        for k in range(inner):
            items = {m: (rows_in[c, inner * m + k, 0], rows_in[c, inner * m + k, 1]) for m in range(outer)}
            items = butterflies(items, inner, lambda m, k=k: inner * m + k)
            for m in range(outer):
                w = inner * m + k
                cosine, sine = twiddle_ref[g * 2 * slabs + 2 * w], twiddle_ref[g * 2 * slabs + 2 * w + 1]
                re, im = items[m]
                rows_z[c, w, 0] = cosine * re - sine * im
                rows_z[c, w, 1] = sine * re + cosine * im

    real_only = g < 2

    def send_ring_parts(c, count):
        def piece(to):
            return rows_z.at[c, pl.ds(to * share, share), pl.ds(0, count)]

        def one(i, inner_carry):
            to = nearby(g, i, groups)
            pltpu.make_async_remote_copy(
                src_ref=piece(to),
                dst_ref=ring_in.at[c, g, :, pl.ds(0, count)],
                send_sem=send_b.at[c],
                recv_sem=recv_b.at[c],
                device_id=(to, s),
                device_id_type=MESH,
            ).start()
            return inner_carry

        pltpu.make_async_copy(piece(g), ring_in.at[c, g, :, pl.ds(0, count)], recv_b.at[c]).start()
        lax.fori_loop(1, groups, one, 0)

    def send_ring(c):
        @pl.when(real_only)
        def _():
            send_ring_parts(c, 1)

        @pl.when(jnp.logical_not(real_only))
        def _():
            send_ring_parts(c, 2)

    def along_ring(c):
        for k in range(share):
            items = {q: (ring_in[c, q, k, 0], ring_in[c, q, k, 1] if q > 1 else jnp.zeros((rows, LANES), jnp.float32)) for q in range(groups)}
            items = butterflies(items, 1, lambda q: q, real_at_end=True)
            for u in range(groups):
                real_z[c, u, k] = items[u][0]

        def one(i, inner_carry):
            to = nearby(g, lax.div(i, share), groups)
            k = lax.rem(i, share)
            w = g * share + k
            mine = jnp.logical_and(to == g, w == s)
            place = velocity.at[c, pl.ds(pl.multiple_of(s * rows, rows), rows), :]

            @pl.when(mine)
            def _():
                pltpu.make_async_copy(real_z.at[c, to, k], place, recv_c.at[c]).start()

            @pl.when(jnp.logical_not(mine))
            def _():
                pltpu.make_async_remote_copy(
                    src_ref=real_z.at[c, to, k],
                    dst_ref=place,
                    send_sem=send_c.at[c],
                    recv_sem=recv_c.at[c],
                    device_id=(to, w),
                    device_id_type=MESH,
                ).start()

            return inner_carry

        lax.fori_loop(0, slabs, one, 0)


    edge_place = jnp.where(at_start, slabs + REACH + s, s - (slabs - REACH))
    low_half = lax.broadcasted_iota(jnp.int32, (8, LANES), 0) < 4
    lane = lax.broadcasted_iota(jnp.int32, (16, LANES), 1)

    def place_plane(c):
        for half in range(2):
            got = velocity.at[2 * c + half]
            wait_for(got, recv_c.at[2 * c + half])
            whole = [got[side - REACH : side, :], got[...], got[0 : 8 - REACH, :]]
            padded[c, half] = jnp.concatenate(whole, axis=0).reshape(side // 8 + 1, 8, LANES)

    spots = []
    for slot in range(2 * PLANES):
        centre = s + slot // 2 - REACH
        inside = jnp.logical_and(centre >= 0, centre < slabs)
        column = 4 * lax.rem(centre + slabs, slabs) + 2 * (slot % 2)
        spots.append((jnp.where(inside, 0, slabs), column))

    def cut_for(c, home):
        cut = jnp.zeros((16, LANES), jnp.float32)
        for slot in range(2 * PLANES):
            row, column = home + spots[slot][0], spots[slot][1]
            tile = asked_smem[row, 0, column]
            first = asked_smem[row, 0, column + 1]
            half = first >> 7
            first = first & (LANES - 1)
            near = jnp.concatenate([padded[c, half, tile], padded[c, half, tile + 1]], axis=0)
            far = jnp.concatenate([padded[c, 1 - half, tile], padded[c, 1 - half, tile + 1]], axis=0)
            cells = jnp.where(lane >= first, near, far)
            moved = pltpu.roll(cells, (CELLS * slot + LANES - first) & (LANES - 1), 1)
            taken = jnp.logical_and(lane >= CELLS * slot, lane < CELLS * (slot + 1))
            cut = jnp.where(taken, moved, cut)
        return cut

    def deliver(home, own, tiles):
        part = pl.ds(8 * tiles[0], 8 * len(tiles))

        @pl.when(at_edge)
        def _():
            pltpu.make_async_remote_copy(
                src_ref=message.at[home, part],
                dst_ref=inbox.at[edge_place, part],
                send_sem=edge_m,
                recv_sem=recv_m,
                device_id=(edge_group, home),
                device_id_type=MESH,
            ).start()

        def keep():
            pltpu.make_async_copy(message.at[home, part], inbox.at[REACH + s, part], recv_m).start()

        def give():
            pltpu.make_async_remote_copy(
                src_ref=message.at[home, part],
                dst_ref=inbox.at[REACH + s, part],
                send_sem=send_m,
                recv_sem=recv_m,
                device_id=(g, home),
                device_id_type=MESH,
            ).start()

        if own is None:
            give()
        else:
            pl.when(own)(keep)
            pl.when(jnp.logical_not(own))(give)

    at_once = 4

    def homes_of(i):
        return [nearby(s, at_once * i + k, slabs) for k in range(at_once)]

    def serve_first(i, carry):
        homes = homes_of(i)
        for home, cut in zip(homes, [cut_for(0, home) for home in homes]):
            message[home, 0:8, :] = cut[0:8]
            message[home, 16:24, :] = cut[8:16]
        return carry

    def serve_second(i, carry):
        homes = homes_of(i)
        for home, cut in zip(homes, [cut_for(1, home) for home in homes]):
            message[home, 8:16, :] = cut[0:8]
            message[home, 16:24, :] = jnp.where(low_half, message[home, 16:24, :], pltpu.roll(cut[8:16], 4, 0))
        for k, home in enumerate(homes):
            deliver(home, None if k else i == 0, (0, 1, 2))
        return carry

    def serve_third(i, carry):
        homes = homes_of(i)
        for home, cut in zip(homes, [cut_for(2, home) for home in homes]):
            message[home, 24:40, :] = cut
        for k, home in enumerate(homes):
            deliver(home, None if k else i == 0, (3, 4))
        return carry

    parts = 2 * components

    def spread(k):
        wait_for(rows_in.at[k], recv_a.at[k])
        if k + 2 < parts:
            send_rows(k + 2)
        along_slab(k)
        send_ring(k)

    def gather(k):
        wait_for(ring_in.at[k, pl.ds(0, groups - 1)], recv_b.at[k])
        along_ring(k)

    spread(0)
    spread(1)
    transform_plane(2)
    make_requests()
    pltpu.make_async_copy(asking_ref, asked_ref.at[s], recv_q).start()
    lax.fori_loop(1, slabs, ask_slab, 0)
    spread(2)
    gather(0)

    own_asked, more_asked = pl.ds(0, slabs), pl.ds(slabs, slabs)
    wait_for(asked_ref.at[own_asked], recv_q)

    @pl.when(at_edge)
    def _():
        pltpu.make_async_remote_copy(
            src_ref=asked_ref.at[own_asked],
            dst_ref=asked_ref.at[more_asked],
            send_sem=send_e,
            recv_sem=recv_e,
            device_id=(jnp.where(at_start, above, below), s),
            device_id_type=MESH,
        ).start()

    pltpu.sync_copy(asked_ref.at[own_asked], asked_smem.at[own_asked])
    for k in range(3, parts):
        spread(k)
        gather(k - 2)

    @pl.when(at_edge)
    def _():
        wait_for(asked_ref.at[more_asked], recv_e)
        wait_for(asked_ref.at[own_asked], send_e)
        pltpu.sync_copy(asked_ref.at[more_asked], asked_smem.at[more_asked])

    place_plane(0)
    lax.fori_loop(0, slabs // at_once, serve_first, 0)
    gather(parts - 2)
    gather(parts - 1)
    place_plane(1)
    lax.fori_loop(0, slabs // at_once, serve_second, 0)
    place_plane(2)
    lax.fori_loop(0, slabs // at_once, serve_third, 0)
    wait_for(inbox, recv_m)

    wait_for(inbox.at[pl.ds(0, slabs - 1)], send_m)

    @pl.when(at_edge)
    def _():
        wait_for(inbox.at[pl.ds(0, slabs)], edge_m)

    wait_for(asked_ref.at[pl.ds(0, slabs - 1)], send_q)

    holds_own = lax.div(s, share) == g

    def drain(c, carry):
        wait_for(rows_in.at[c, pl.ds(0, slabs - 1)], send_a.at[c])
        @pl.when(real_only)
        def _():
            wait_for(ring_in.at[c, pl.ds(0, groups - 1), :, pl.ds(0, 1)], send_b.at[c])

        @pl.when(jnp.logical_not(real_only))
        def _():
            wait_for(ring_in.at[c, pl.ds(0, groups - 1)], send_b.at[c])

        @pl.when(holds_own)
        def _():
            wait_for(velocity.at[c, pl.ds(0, side - rows)], send_c.at[c])

        @pl.when(jnp.logical_not(holds_own))
        def _():
            wait_for(velocity.at[c], send_c.at[c])

        return carry

    lax.fori_loop(0, 2 * components, drain, 0)


def synthesize(source, tiles, spectrum, groups, slabs):
    components, side = spectrum.shape[1], spectrum.shape[3]
    rows, share, parts = side // slabs, slabs // groups, components * side // LANES
    ids = np.arange(side)
    angle = 2.0 * np.pi / side * (ids[:, None] * ids[None, :] % side)
    tables = jnp.stack(split_table(np.cos(angle)) + split_table(np.sin(angle)))
    count = groups * slabs
    twist = 2.0 * np.pi / count * (bit_reversed(groups)[:, None] * np.arange(slabs)[None, :])
    scale = 1.0 / math.sqrt(side * side * count)
    twiddle = np.stack([np.cos(twist), np.sin(twist)], axis=-1) * scale
    twiddle = jnp.asarray(twiddle.reshape(-1).astype(np.float32))
    vmem, hbm = pl.BlockSpec(memory_space=pltpu.VMEM), pl.BlockSpec(memory_space=pltpu.HBM)
    f32 = jnp.float32
    return pl.pallas_call(
        functools.partial(transform_kernel, groups, slabs),
        out_shape=jax.ShapeDtypeStruct((slabs + 2 * REACH, ROWS_OUT, LANES), f32),
        in_specs=[vmem, vmem, hbm, hbm, pl.BlockSpec(memory_space=pltpu.SMEM)],
        out_specs=vmem,
        scratch_shapes=[
            pltpu.VMEM((1, LANES), jnp.int32),
            pltpu.VMEM((2, components, side, side), f32),
            pltpu.VMEM((4, side, side), jnp.bfloat16),
            pltpu.VMEM((2 * slabs, 1, LANES), jnp.int32),
            pltpu.SMEM((2 * slabs, 1, LANES), jnp.int32),
            pltpu.VMEM((components, 2, side // 8 + 1, 8, LANES), f32),
            pltpu.VMEM((slabs, ROWS_OUT, LANES), f32),
            pltpu.VMEM((parts, 2, side, LANES), f32),
            pltpu.VMEM((parts, slabs, 2, rows, LANES), f32),
            pltpu.VMEM((parts, slabs, 2, rows, LANES), f32),
            pltpu.VMEM((parts, groups, share, 2, rows, LANES), f32),
            pltpu.VMEM((parts, groups, share, rows, LANES), f32),
            pltpu.VMEM((parts, side, LANES), f32),
        ]
        + [pltpu.SemaphoreType.DMA((parts,))] * 6
        + [pltpu.SemaphoreType.DMA] * 2
        + [pltpu.SemaphoreType.DMA((components,))]
        + [pltpu.SemaphoreType.DMA] * 6,
        compiler_params=pltpu.CompilerParams(
            collective_id=0, has_side_effects=True, vmem_limit_bytes=62 * 2**20
        ),
        cost_estimate=pl.CostEstimate(flops=2_500_000_000, bytes_accessed=100_000_000, transcendentals=0),
    )(source, tiles, spectrum[:, :, 0], tables, twiddle)


def interpolate_kernel(inbox, source_ref, fraction_ref, offset_ref, out_ref, weights, named):
    blocks, markers = fraction_ref.shape[1], fraction_ref.shape[2]
    weights[...] = jnp.zeros_like(weights)
    group = weights.shape[0]
    first_lanes = lax.broadcasted_iota(jnp.int32, (ROWS_OUT * PLANES, LANES), 1) < 16
    row_y = lax.broadcasted_iota(jnp.int32, (16, markers), 0)
    row_x = jnp.where(row_y < 12, row_y, row_y - 4)
    in_low = lax.broadcasted_iota(jnp.int32, (8, markers), 0) < 4

    for k in range(named.shape[0]):
        named[k] = 0

    def one_block(i, weights):
        f = jnp.concatenate([fraction_ref[d, pl.ds(i, 1), :] for d in range(3)], axis=0)
        o = [offset_ref[d, pl.ds(i, 1), :] for d in range(3)]
        root = jnp.sqrt(1.0 + 4.0 * f - 4.0 * f * f)
        low, high = 3.0 - 2.0 * f, 1.0 + 2.0 * f
        taps = ((low - root) * 0.125, (low + root) * 0.125, (high + root) * 0.125, (high - root) * 0.125)
        weight_x = jnp.zeros((16, markers), jnp.float32)
        weight_y = jnp.zeros((16, markers), jnp.float32)
        for e in range(4):
            weight_x = jnp.where(row_x == o[1] + e, taps[e][1:2], weight_x)
            weight_y = jnp.where(row_y == o[2] + e, taps[e][2:3], weight_y)
        y_high, y_low = split(weight_y)
        weights[0:16, :] = y_high
        weights[16:32, :] = y_low
        weights[LANES : LANES + 16, :] = y_high
        near = o[0] == 0
        none = jnp.zeros((1, markers), jnp.float32)
        tap_z = [none] + [tap[0:1] for tap in taps] + [none]
        weight_z = [jnp.where(near, tap_z[j + 1], tap_z[j]) for j in range(PLANES)]
        source = source_ref[0, i]
        slot = named[source]
        named[source] = 1
        cells = []
        for j in range(PLANES):
            place = CELLS * (2 * (PLANES - 1 - j) + slot)
            cells.append(pltpu.roll(inbox[source + j], (2 * LANES - place) & (LANES - 1), 1))
        cells = jnp.concatenate(cells, axis=0)
        cells = jnp.where(first_lanes, cells, pltpu.roll(cells, 16, 1))
        values = dot(jnp.concatenate(split(cells), axis=1), weights[...])
        sums = []
        for t in range(ROWS_OUT // 8):
            total = weight_z[0] * values[8 * t : 8 * t + 8]
            for j in range(1, PLANES):
                total = total + weight_z[j] * values[ROWS_OUT * j + 8 * t : ROWS_OUT * j + 8 * t + 8]
            sums.append(total)
        x_first, x_last = weight_x[0:8], weight_x[8:16]
        mixed, last = sums[2] * x_last, sums[4] * x_last
        tails = (jnp.where(in_low, mixed, 0.0), jnp.where(in_low, 0.0, mixed), jnp.where(in_low, last, 0.0))
        for c in range(3):
            out_ref[c, pl.ds(i, 1), :] = jnp.sum(sums[(0, 1, 3)[c]] * x_first + tails[c], axis=0, keepdims=True)

    def several(i, carry):
        for k in range(group):
            one_block(group * i + k, weights.at[k])
        return carry

    lax.fori_loop(0, blocks // group, several, 0)


def sample(inbox, source, fraction, offsets, slabs):
    vmem, smem = pl.BlockSpec(memory_space=pltpu.VMEM), pl.BlockSpec(memory_space=pltpu.SMEM)
    markers = fraction.shape[2]
    return pl.pallas_call(
        interpolate_kernel,
        out_shape=jax.ShapeDtypeStruct(fraction.shape, jnp.float32),
        in_specs=[vmem, smem, vmem, vmem],
        out_specs=vmem,
        scratch_shapes=[pltpu.VMEM((8, 2 * LANES, markers), jnp.bfloat16), pltpu.SMEM((slabs,), jnp.int32)],
        cost_estimate=pl.CostEstimate(flops=200_000_000, bytes_accessed=1_500_000, transcendentals=25_000),
    )(inbox, source, fraction, offsets)


def local(groups, slabs, spectrum, marker_fraction, marker_offsets, block_source, block_tile):
    source = jnp.transpose(block_source)
    inbox = synthesize(source, jnp.transpose(block_tile), spectrum, groups, slabs)
    fraction, offsets = jnp.transpose(marker_fraction, (1, 0, 2)), jnp.transpose(marker_offsets, (1, 0, 2))
    answer = sample(inbox, source, fraction, offsets, slabs)
    return jnp.transpose(answer, (1, 0, 2))


def solution(mesh):
    groups, slabs = mesh.shape["grp"], mesh.shape["gz"]
    both = ("grp", "gz")
    return jax.shard_map(
        functools.partial(local, groups, slabs),
        mesh=mesh,
        in_specs=(
            P(None, None, both, None, None),
            P(both, None, None),
            P(both, None, None),
            P(both, None),
            P(both, None),
        ),
        out_specs=P(both, None, None),
        check_vma=False,
    )
```
